256 devices in a mesh: particle: 32 (over z, x_lo, core), slab: 8 (over x_hi, y).
Axes of the slice: x: 4 (x_hi: 2, x_lo: 2; x = x_hi * 2 + x_lo), y: 4, z: 8, core: 2. Of those that a mesh axis runs over, the one named last changes fastest.
Arguments:
- ref_map: bfloat16 [1024, 256], P('slab'), may hold values from -6 to 6
- images: bfloat16 [512, 2, 2048], P(('particle', 'slab')), may hold values from -6 to 6
- ctf_table: bfloat16 [64, 2048], replicated, may hold values from -1 to 1
- ctf_class: int32 [512], P(('particle', 'slab')), may hold values from 0 to 63
- block_index: int32 [512, 64, 16, 4], P(('particle', 'slab')), may hold values from 0 to 1023
- interp_kind: int32 [512, 64, 16, 4], P(('particle', 'slab')), may hold values from 0 to 7
- interp_bank: bfloat16 [8, 128, 128], replicated, may hold values from -0.25 to 0.25
Outputs:
- data_map: float32 [1024, 256], P(('particle', 'slab'))
- weight_map: float32 [1024, 128], P(('particle', 'slab'))
- posterior: float32 [512, 64], P(('particle', 'slab'))
The draws below stay inside these ranges and needn't reach their ends.
Inputs may be any that keep to these rules, and one draw needn't show every extreme that they name: `block_index`: map blocks of the whole window. `interp_kind`: bank entries. `ctf_class`: rows of ctf_table.
All inputs are finite; a program needn't handle non-finite values.
Results may differ from the reference program's by a relative error of at most 0.0013.
Values may be sent and summed in bfloat16 or wider, within the bound.
A program may use at most 128 MiB of HBM per device.

```python
import jax
import jax.numpy as jnp
from jax import lax

LINE = 256
PLINES = 8
BW = 128
TAPS = 4
KINDS = 8
CAND = 64
SIDE = 32
NCLASS = 64
IMG_DEV = 2
PIX = 2048
PB = 16
NBLK = 1024
IMAGES = 512


def set_ends(entries, own_key, smallest, largest):
    extent = entries.shape
    place = [jax.random.randint(jax.random.fold_in(own_key, axis), (), 0, extent[axis]) for axis in range(len(extent))]
    entries = entries.at[tuple(place)].set(smallest)
    longest = extent.index(max(extent))
    place[longest] = (place[longest] + 1) % extent[longest]
    return entries.at[tuple(place)].set(largest)


def level_of(rng, shape, split, least, top_value):
    def one(position, shards_of):
        heights = jax.random.uniform(jax.random.fold_in(jax.random.fold_in(rng, 6), position), (shards_of,), jnp.float32, least / len(split), top_value / len(split))
        return jnp.repeat(jnp.exp(heights), shape[position] // shards_of).reshape((-1,) + (1,) * (len(shape) - position - 1))

    loudness = one(*split[0])
    for cut in split[1:]:
        loudness = loudness * one(*cut)
    return loudness


def scatter_about(stream_key, extent, spread, limit, split=(), kind=jnp.bfloat16):
    result = spread * jax.random.normal(stream_key, extent, jnp.float32)
    if split:
        result = result * level_of(stream_key, extent, split, -0.22, 0.18)
    return jnp.clip(result, -limit, limit).astype(kind)


def setup_inputs(seed: int = 0) -> dict:
    key_list = jax.random.split(jax.random.key(seed), 8)
    return {
        "ref_map": scatter_about(key_list[0], (NBLK, 2 * BW), 1.0, 6.0, ((0, 8),)),
        "images": scatter_about(key_list[1], (IMAGES, 2, PIX), 1.0, 6.0, ((0, 256),)),
        "ctf_table": jnp.clip(jax.random.uniform(key_list[2], (NCLASS, PIX), jnp.float32, -1.0, 1.0), -1.0, 1.0).astype(jnp.bfloat16),
        "ctf_class": set_ends(jax.random.randint(key_list[3], (IMAGES,), 0, NCLASS), jax.random.fold_in(key_list[3], 1), 0, NCLASS - 1).astype(jnp.int32),
        "block_index": set_ends(jax.random.randint(key_list[4], (IMAGES, CAND, PB, TAPS), 0, NBLK), jax.random.fold_in(key_list[4], 1), 0, NBLK - 1).astype(jnp.int32),
        "interp_kind": set_ends(jax.random.randint(key_list[5], (IMAGES, CAND, PB, TAPS), 0, KINDS), jax.random.fold_in(key_list[5], 1), 0, KINDS - 1).astype(jnp.int32),
        "interp_bank": scatter_about(key_list[6], (KINDS, BW, BW), (BW * TAPS) ** -0.5, 0.25),
    }


def shift_table():
    pixels = jnp.arange(PIX, dtype=jnp.int32)
    freq_x = pixels % LINE - LINE // 2
    freq_y = pixels // LINE - PLINES // 2
    shift_ids = jnp.arange(SIDE * SIDE, dtype=jnp.int32)
    shift_x = shift_ids % SIDE - SIDE // 2
    shift_y = shift_ids // SIDE - SIDE // 2
    phase_num = (freq_x[:, None] * shift_x[None, :] + freq_y[:, None] * shift_y[None, :]) % LINE
    angles = (2.0 * jnp.pi / LINE) * phase_num.astype(jnp.float32)
    return jnp.concatenate([jnp.cos(angles), -jnp.sin(angles)], axis=0).astype(jnp.bfloat16)


def score_group(table_rows, shifts, images, ctf_gain, block_index, interp_kind, block_total):
    image_count, cand_count, block_count, tap_count = block_index.shape
    blk_width = table_rows.shape[1] // 2
    row_ids = interp_kind * block_total + block_index
    picked = jnp.take(table_rows, row_ids.reshape(-1), axis=0)
    picked = picked.reshape(image_count, cand_count, block_count, tap_count, 2, blk_width)
    projection = jnp.sum(picked.astype(jnp.float32), axis=3)
    image_pix = images.astype(jnp.float32).reshape(image_count, 2, block_count, blk_width)
    real_part = image_pix[:, 0][:, None]
    imag_part = image_pix[:, 1][:, None]
    ctf_grid = ctf_gain.reshape(image_count, 1, block_count, blk_width)
    proj_re = projection[:, :, :, 0, :]
    proj_im = projection[:, :, :, 1, :]
    cross_re = ctf_grid * (real_part * proj_re + imag_part * proj_im)
    cross_im = ctf_grid * (imag_part * proj_re - real_part * proj_im)
    stacked = jnp.concatenate([cross_re.reshape(image_count, cand_count, -1), cross_im.reshape(image_count, cand_count, -1)], axis=-1).astype(jnp.bfloat16)
    scores = jnp.dot(stacked.reshape(image_count * cand_count, -1), shifts, preferred_element_type=jnp.float32)
    energy = jnp.mean(scores * scores, axis=-1).reshape(image_count, cand_count)
    posterior = cand_count * energy / (jnp.sum(energy, axis=1, keepdims=True) + 1e-6)
    contrib = jnp.stack([ctf_grid * real_part, ctf_grid * imag_part, ctf_grid * ctf_grid], axis=-2)
    contrib = posterior[:, :, None, None, None] * contrib
    rows_all = jnp.broadcast_to(contrib[:, :, :, None], (image_count, cand_count, block_count, tap_count, 3, blk_width))
    seg_sums = jax.ops.segment_sum(rows_all.reshape(-1, 3 * blk_width), row_ids.reshape(-1), num_segments=table_rows.shape[0])
    return posterior, seg_sums


def reference(ref_map, images, ctf_table, ctf_class, block_index, interp_kind, interp_bank):
    blocks = ref_map.astype(jnp.float32).reshape(NBLK, 2, BW)
    bank_full = interp_bank.astype(jnp.float32)
    transformed = jnp.einsum("rcv,kvq->krcq", blocks, bank_full).astype(jnp.bfloat16)
    table_rows = transformed.reshape(KINDS * NBLK, 2 * BW)
    shifts = shift_table()
    groups = IMAGES // IMG_DEV

    def visit(carry, group):
        image_grp, class_grp, index_grp, kind_grp = group
        ctf_gain = ctf_table[class_grp].astype(jnp.float32)
        posterior, seg_sums = score_group(table_rows, shifts, image_grp, ctf_gain, index_grp, kind_grp, NBLK)
        return carry + seg_sums, posterior

    start_sums = jnp.zeros((KINDS * NBLK, 3 * BW), jnp.float32)
    totals, posterior = lax.scan(visit, start_sums, (images.reshape(groups, IMG_DEV, 2, PIX), ctf_class.reshape(groups, IMG_DEV), block_index.reshape(groups, IMG_DEV, CAND, PB, TAPS), interp_kind.reshape(groups, IMG_DEV, CAND, PB, TAPS)))
    posterior = posterior.reshape(IMAGES, CAND)
    merged = jnp.einsum("kvcq,kwq->vcw", totals.reshape(KINDS, NBLK, 3, BW), bank_full, precision=lax.Precision.HIGHEST)
    data_map = merged[:, :2].reshape(NBLK, 2 * BW)
    weight_map = merged[:, 2]
    return data_map, weight_map, posterior
```

```python
import jax
import jax.numpy as jnp
import numpy as np
from jax import lax
from jax.experimental import pallas as pl
from jax.experimental.pallas import tpu as pltpu
from jax.sharding import PartitionSpec as P

LINE = 256
PLINES = 8
SIDE = 32
BW = 128
TAPS = 4
KINDS = 8
CAND = 64
PB = 16
NBLK = 1024
MESH = pl.DeviceIdType.MESH
VMEM = pltpu.VMEM
F32 = jnp.float32
BF16 = jnp.bfloat16
NT = (((1,), (1,)), ((), ()))
TN = (((0,), (0,)), ((), ()))


def line_table():
    fx = np.arange(LINE) - LINE // 2
    sx = np.arange(SIDE) - SIDE // 2
    ang = 2.0 * np.pi / LINE * ((fx[:, None] * sx[None, :]) % LINE)
    cos, sin = np.cos(ang), np.sin(ang)
    one = np.zeros((2, 2, BW, 2, SIDE))
    one[:, 0, :, 0] = cos.reshape(2, BW, SIDE)
    one[:, 1, :, 0] = -sin.reshape(2, BW, SIDE)
    one[:, 0, :, 1] = sin.reshape(2, BW, SIDE)
    one[:, 1, :, 1] = cos.reshape(2, BW, SIDE)
    both = np.zeros((2, 2, 2, BW, 2, 2, SIDE))
    both[0, :, :, :, 0] = one
    both[1, :, :, :, 1] = one
    return both.reshape(8 * BW, 4 * SIDE)


def across_table():
    fy = np.arange(PLINES) - PLINES // 2
    sy = np.arange(SIDE) - SIDE // 2
    ang = 2.0 * np.pi / LINE * ((fy[None, :] * sy[:, None]) % LINE)
    full = np.zeros((SIDE, SIDE, PLINES, 2, SIDE))
    for s in range(SIDE):
        full[:, s, :, 0, s] = np.cos(ang)
        full[:, s, :, 1, s] = -np.sin(ang)
    return full.reshape(SIDE * SIDE, PLINES * 2 * SIDE)


def gather_kernel(piece, full, send_sem, recv_sem, own_sem):
    p = lax.axis_index("particle")
    s = lax.axis_index("slab")
    x_lo = lax.rem(p // 2, 2)
    x_hi = s // 4

    def peer(d):
        other = lax.rem(s + d, 8)
        apart = other // 4 - x_hi
        return (p + apart * apart * (2 - 4 * x_lo), other)

    barrier = pltpu.get_barrier_semaphore()
    for d in range(1, 8):
        pl.semaphore_signal(barrier, inc=1, device_id=peer(d), device_id_type=MESH)
    own = pltpu.make_async_copy(piece, full.at[s], own_sem)
    own.start()
    pl.semaphore_wait(barrier, 7)
    sends = []
    for d in (6, 2, 5, 3, 7, 1, 4):
        copy = pltpu.make_async_remote_copy(
            src_ref=piece,
            dst_ref=full.at[s],
            send_sem=send_sem.at[d],
            recv_sem=recv_sem.at[d],
            device_id=peer(d),
            device_id_type=MESH,
        )
        copy.start()
        sends.append(copy)
    own.wait()
    for d in range(1, 8):
        source = lax.rem(s + 8 - d, 8)
        pltpu.make_async_remote_copy(
            src_ref=piece,
            dst_ref=full.at[source],
            send_sem=send_sem.at[d],
            recv_sem=recv_sem.at[d],
            device_id=peer(d),
            device_id_type=MESH,
        ).wait_recv()
    for copy in sends:
        copy.wait_send()


def split(v):
    hi = v.astype(BF16)
    return hi, (v - hi.astype(F32)).astype(BF16)


def match_kernel(
    rid, cls, blk, kind, refs, bank, img, ctf, fx, fy,
    sums, post_out,
    table, inter, proj, cross, hist, rows, parts,
):
    inter[pl.ds(0, NBLK, stride=2), :] = refs[:, :BW].astype(F32)
    inter[pl.ds(1, NBLK, stride=2), :] = refs[:, BW:].astype(F32)
    for k in range(KINDS):
        weight = bank[k]

        @pl.loop(0, 4)
        def _(step):
            lhs = inter[pl.ds(pl.multiple_of(step * 512, 512), 512), :].astype(BF16)
            out = jnp.dot(lhs, weight, preferred_element_type=F32)
            start = pl.multiple_of(k * 2 * NBLK + step * 512, 512)
            table[pl.ds(start, 512), :] = out.astype(BF16).astype(F32)

    lanes = lax.broadcasted_iota(jnp.int32, (16, 64), 1)
    which = lax.broadcasted_iota(jnp.int32, (16, 64), 0)
    pick = jnp.where(which == 0, cls[0], cls[1])
    onehot = (lanes == pick).astype(F32).astype(BF16)
    gain = jnp.dot(onehot, ctf[...], preferred_element_type=F32)
    pixel = img[...].astype(F32)
    scaled = []
    for i in range(2):
        g = gain[i : i + 1]
        ca = g * pixel[i, 0:1]
        cb = g * pixel[i, 1:2]
        scaled.append((ca, cb))
        for c, row in enumerate((ca, cb, g * g)):
            for p in range(PB):
                parts[pl.ds(c * 32 + i * PB + p, 1), :] = row[:, p * BW : (p + 1) * BW]
    both = jnp.concatenate(split(parts[...]), axis=0)
    for k in range(KINDS):
        out = lax.dot_general(both, bank[k], NT, preferred_element_type=F32)
        out = out[:96] + out[96:]
        for c in range(3):
            rows[c, pl.ds(k, 32, stride=KINDS), :] = out[c * 32 : (c + 1) * 32]

    @pl.loop(0, 32)
    def _(ip):
        @pl.loop(0, 4)
        def _(part):
            for u in range(16):
                j = part * 16 + u
                taken = [table[pl.ds(pl.multiple_of(rid[ip, t * CAND + j] * 2, 2), 2), :] for t in range(TAPS)]
                total = (taken[0] + taken[1]) + (taken[2] + taken[3])
                proj[pl.ds(pl.multiple_of(ip * 128 + j * 2, 2), 2), :] = total

    for i in range(2):
        ca, cb = scaled[i]
        for p in range(PB):
            a = ca[:, p * BW : (p + 1) * BW]
            b = cb[:, p * BW : (p + 1) * BW]
            start = (i * PB + p) * 2 * CAND
            u = proj[pl.ds(start, CAND, stride=2), :]
            w = proj[pl.ds(start + 1, CAND, stride=2), :]
            at = pl.ds(i * CAND, CAND)
            cross[at, pl.ds(p * 256, 128)] = (a * u + b * w).astype(BF16)
            cross[at, pl.ds(p * 256 + 128, 128)] = (b * u - a * w).astype(BF16)

    along = [
        jnp.dot(cross[:, g * 1024 : (g + 1) * 1024], fx[...], preferred_element_type=F32)
        for g in range(4)
    ]
    along = jnp.concatenate(along, axis=1)
    hi, lo = split(along)
    scores = lax.dot_general(fy[...], hi, NT, preferred_element_type=F32)
    scores = scores + lax.dot_general(fy[...], lo, NT, preferred_element_type=F32)
    energy = jnp.sum(scores * scores, axis=0, keepdims=True) * (1.0 / (SIDE * SIDE))
    lane = lax.broadcasted_iota(jnp.int32, (1, 128), 1)
    first = lane < CAND
    sum0 = jnp.sum(jnp.where(first, energy, 0.0), axis=1, keepdims=True)
    sum1 = jnp.sum(jnp.where(first, 0.0, energy), axis=1, keepdims=True)
    post = CAND * energy / (jnp.where(first, sum0, sum1) + 1e-6)
    post_out[...] = post
    turned = jnp.concatenate([post[:, CAND:], post[:, :CAND]], axis=1)
    weights = (jnp.where(first, post, turned), jnp.where(first, turned, post))

    row_id = lax.broadcasted_iota(jnp.int32, (64, 256), 0)
    col_id = lax.broadcasted_iota(jnp.int32, (128, 256), 0)
    for i in range(2):
        w2 = jnp.concatenate([weights[i], weights[i]], axis=1)
        w_hi = w2.astype(BF16).astype(F32)
        w_lo = w2 - w_hi

        @pl.loop(0, PB)
        def _(p):
            ip = i * PB + p
            v = blk[pl.ds(ip, 1), :]
            k = kind[pl.ds(ip, 1), :]
            high = ((v >> 5) & 1) * 4 + ((v >> 4) & 1) * 2 + ((v >> 6) & 1)
            low = ((v >> 2) & 3) * 32 + (v >> 7) * 4 + (v & 3)
            hit = row_id == high * KINDS + k
            left = jnp.concatenate(
                [jnp.where(hit, w_hi, 0.0).astype(BF16), jnp.where(hit, w_lo, 0.0).astype(BF16)], axis=0
            )
            right = jnp.where(col_id == low, 1.0, 0.0).astype(BF16)
            out = lax.dot_general(left, right, NT, preferred_element_type=F32)
            out = out[:64] + out[64:]
            at = pl.ds(pl.multiple_of(ip * KINDS, KINDS), KINDS)
            for h in range(8):
                hist[at, pl.ds(h * 128, 128)] = out[h * 8 : (h + 1) * 8]

    d_hi, d_lo = split(jnp.concatenate([rows[c] for c in range(3)], axis=1))
    d_both = jnp.concatenate([d_hi, d_lo], axis=1)
    for h in range(8):
        at = pl.ds(h * 128, 128)
        h_hi, h_lo = split(hist[:, at].T)
        out = jnp.dot(h_hi, d_both, preferred_element_type=F32)
        sums[at, :] = out[:, :384] + out[:, 384:] + jnp.dot(h_lo, d_hi, preferred_element_type=F32)


def scatter_kernel(
    sums, data, weight,
    near, s1, a1, b1, s2a, s2b, a2, b2, s3, r3,
    near_s, near_r, xs, xr, ys, yr, x2s, x2r, y2s, y2r, zs, zr,
):
    p = lax.axis_index("particle")
    s = lax.axis_index("slab")
    z, x_lo, core = p // 4, lax.rem(p // 2, 2), lax.rem(p, 2)
    x_hi, y = s // 4, lax.rem(s, 4)
    x = x_hi * 2 + x_lo

    sibling = (p + 1 - 2 * core, s)

    def x_peer(d):
        to = lax.rem(x + d, 4)
        return to, (p + (lax.rem(to, 2) - x_lo) * 2, s + (to // 2 - x_hi) * 4)

    def y_peer(d):
        to = lax.rem(y + d, 4)
        return to, (p, s + to - y)

    def z_peer(d):
        to = lax.rem(z + d, 8)
        return to, (p + (to - z) * 4, s)

    peers = [sibling] + [x_peer(d)[1] for d in (1, 2, 3)] + [y_peer(d)[1] for d in (1, 2, 3)]
    peers += [z_peer(d)[1] for d in range(1, 8)]
    barrier = pltpu.get_barrier_semaphore()
    for peer in peers:
        pl.semaphore_signal(barrier, inc=1, device_id=peer, device_id_type=MESH)
    pl.semaphore_wait(barrier, len(peers))

    def send(src, dst, ssem, rsem, peer):
        copy = pltpu.make_async_remote_copy(
            src_ref=src, dst_ref=dst, send_sem=ssem, recv_sem=rsem, device_id=peer, device_id_type=MESH
        )
        copy.start()
        return copy

    order = [lax.rem(x + d, 4) for d in (2, 1, 3, 0)]
    done = []
    first = []
    for n, to in enumerate(order):
        first.append(send(sums.at[1 - core, to], near.at[to], near_s.at[n], near_r.at[n], sibling))
    last = []
    for n, d in enumerate((2, 1, 3, 0)):
        to = order[n]
        first[n].wait_recv()
        s1[to] = sums[core, to] + near[to]
        if d:
            last.append(send(s1.at[to, :, pl.ds(0, 16)], a1.at[d], xs.at[d], xr.at[d], x_peer(d)[1]))
    for d in (2, 1, 3):
        to, peer = y_peer(d)
        done.append(send(s1.at[:, to, pl.ds(16, 16)], b1.at[d], ys.at[d], yr.at[d], peer))
    for copy in last:
        copy.wait_recv()
    s2a[...] = (s1[x, :, 0:16, :] + a1[1]) + (a1[2] + a1[3])
    second = []
    for d in (2, 1, 3):
        to, peer = y_peer(d)
        second.append(send(s2a.at[to], a2.at[d], y2s.at[d], y2r.at[d], peer))
    for copy in done:
        copy.wait_recv()
    s2b[...] = (s1[:, y, 16:32, :] + b1[1]) + (b1[2] + b1[3])
    for d in (2, 1, 3):
        to, peer = x_peer(d)
        second.append(send(s2b.at[to], b2.at[d], x2s.at[d], x2r.at[d], peer))
    for copy in second[:3]:
        copy.wait_recv()
    low = (s2a[y] + a2[1]) + (a2[2] + a2[3])
    for n in range(4):
        s3[n] = low[n * 4 : (n + 1) * 4]
    for copy in second[3:]:
        copy.wait_recv()
    high = (s2b[x] + b2[1]) + (b2[2] + b2[3])
    for n in range(4):
        s3[4 + n] = high[n * 4 : (n + 1) * 4]
    third = []
    for d in (4, 3, 5, 2, 6, 1, 7):
        to, peer = z_peer(d)
        third.append(send(s3.at[to], r3.at[d], zs.at[d], zr.at[d], peer))
    for copy in third:
        copy.wait_recv()
    total = s3[z]
    for d in range(1, 8):
        total = total + r3[d]
    data[...] = total[:, :256]
    weight[...] = total[:, 256:]
    for copy in first + last + done + second + third:
        copy.wait_send()


def whole():
    return pl.BlockSpec(memory_space=VMEM)


def local(ref_map, images, ctf_table, ctf_class, block_index, interp_kind, interp_bank):
    full = pl.pallas_call(
        gather_kernel,
        out_shape=jax.ShapeDtypeStruct((8, NBLK // 8, 2 * BW), BF16),
        in_specs=[whole()],
        out_specs=whole(),
        scratch_shapes=[
            pltpu.SemaphoreType.DMA((8,)),
            pltpu.SemaphoreType.DMA((8,)),
            pltpu.SemaphoreType.DMA,
        ],
        compiler_params=pltpu.CompilerParams(collective_id=0, has_side_effects=True),
        name="gather_map",
    )(ref_map)
    blk = jnp.transpose(block_index, (0, 2, 3, 1)).reshape(32, TAPS * CAND)
    kind = jnp.transpose(interp_kind, (0, 2, 3, 1)).reshape(32, TAPS * CAND)
    rid = kind * NBLK + blk
    smem = pl.BlockSpec(memory_space=pltpu.SMEM)
    sums, post = pl.pallas_call(
        match_kernel,
        out_shape=[
            jax.ShapeDtypeStruct((NBLK, 384), F32),
            jax.ShapeDtypeStruct((1, 128), F32),
        ],
        in_specs=[smem, smem] + [whole()] * 8,
        out_specs=[whole()] * 2,
        scratch_shapes=[
            VMEM((2 * KINDS * NBLK, BW), F32),
            VMEM((2 * NBLK, BW), F32),
            VMEM((4096, BW), F32),
            VMEM((128, 4096), BF16),
            VMEM((256, NBLK), F32),
            VMEM((3, 256, BW), F32),
            VMEM((96, BW), F32),
        ],
        compiler_params=pltpu.CompilerParams(vmem_limit_bytes=48 * 1024 * 1024),
        name="match",
    )(
        rid, ctf_class, blk, kind, full.reshape(NBLK, 2 * BW), interp_bank, images, ctf_table,
        jnp.asarray(line_table(), BF16), jnp.asarray(across_table(), BF16),
    )
    dma = pltpu.SemaphoreType.DMA
    data_map, weight_map = pl.pallas_call(
        scatter_kernel,
        out_shape=[
            jax.ShapeDtypeStruct((4, 256), F32),
            jax.ShapeDtypeStruct((4, 128), F32),
        ],
        in_specs=[whole()],
        out_specs=[whole()] * 2,
        scratch_shapes=[
            VMEM((4, 4, 32, 384), F32),
            VMEM((4, 4, 32, 384), F32),
            VMEM((4, 4, 16, 384), F32),
            VMEM((4, 4, 16, 384), F32),
            VMEM((4, 16, 384), F32),
            VMEM((4, 16, 384), F32),
            VMEM((4, 16, 384), F32),
            VMEM((4, 16, 384), F32),
            VMEM((8, 4, 384), F32),
            VMEM((8, 4, 384), F32),
            dma((4,)), dma((4,)), dma((4,)), dma((4,)), dma((4,)), dma((4,)),
            dma((4,)), dma((4,)), dma((4,)), dma((4,)), dma((8,)), dma((8,)),
        ],
        compiler_params=pltpu.CompilerParams(
            collective_id=1, has_side_effects=True, vmem_limit_bytes=32 * 1024 * 1024
        ),
        name="scatter_sums",
    )(sums.reshape(2, 4, 4, 32, 384))
    return (data_map, weight_map, post.reshape(2, CAND))


def solution(mesh):
    in_specs = (
        P("slab", None),
        P(("particle", "slab"), None, None),
        P(),
        P(("particle", "slab")),
        P(("particle", "slab"), None, None, None),
        P(("particle", "slab"), None, None, None),
        P(),
    )
    out_specs = (
        P(("particle", "slab"), None),
        P(("particle", "slab"), None),
        P(("particle", "slab"), None),
    )
    return jax.shard_map(local, mesh=mesh, in_specs=in_specs, out_specs=out_specs, check_vma=False)
```

```python
import jax
import jax.numpy as jnp
import numpy as np
from jax import lax
from jax.experimental import pallas as pl
from jax.experimental.pallas import tpu as pltpu
from jax.sharding import PartitionSpec as P

LINE = 256
PLINES = 8
SIDE = 32
BW = 128
TAPS = 4
KINDS = 8
CAND = 64
PB = 16
NBLK = 1024
MESH = pl.DeviceIdType.MESH
VMEM = pltpu.VMEM
F32 = jnp.float32
BF16 = jnp.bfloat16
NT = (((1,), (1,)), ((), ()))


def line_table():
    fx = np.arange(LINE) - LINE // 2
    sx = np.arange(SIDE) - SIDE // 2
    ang = 2.0 * np.pi / LINE * ((fx[:, None] * sx[None, :]) % LINE)
    cos, sin = np.cos(ang), np.sin(ang)
    one = np.zeros((2, 2, BW, 2, SIDE))
    one[:, 0, :, 0] = cos.reshape(2, BW, SIDE)
    one[:, 1, :, 0] = -sin.reshape(2, BW, SIDE)
    one[:, 0, :, 1] = sin.reshape(2, BW, SIDE)
    one[:, 1, :, 1] = cos.reshape(2, BW, SIDE)
    both = np.zeros((2, 2, 2, BW, 2, 2, SIDE))
    both[0, :, :, :, 0] = one
    both[1, :, :, :, 1] = one
    return both.reshape(8 * BW, 4 * SIDE)


def across_table():
    fy = np.arange(PLINES) - PLINES // 2
    sy = np.arange(SIDE) - SIDE // 2
    ang = 2.0 * np.pi / LINE * ((fy[None, :] * sy[:, None]) % LINE)
    full = np.zeros((SIDE, SIDE, PLINES, 2, SIDE))
    for s in range(SIDE):
        full[:, s, :, 0, s] = np.cos(ang)
        full[:, s, :, 1, s] = -np.sin(ang)
    return full.reshape(SIDE * SIDE, PLINES * 2 * SIDE)


def split(v):
    hi = v.astype(BF16)
    return hi, (v - hi.astype(F32)).astype(BF16)


def refine_kernel(
    piece, img_h, ctf_h, cls_h, blk_h, kind_h, bank_h, fx_h, fy_h,
    data, weight, post_out,
    img, ctf, cls, blk, kind, bank, fx, fy, own_sem,
    full, table, parts, rows, rid_v, rid, left, right,
    proj, cross, hist, gather_s, gather_r,
    sums, near, s1, a1, b1, s2a, s2b, a2, b2, s3, r3,
    near_s, near_r, xs, xr, ys, yr, x2s, x2r, y2s, y2r, zs, zr,
):
    p = lax.axis_index("particle")
    s = lax.axis_index("slab")
    z, x_lo, core = p // 4, lax.rem(p // 2, 2), lax.rem(p, 2)
    x_hi, y = s // 4, lax.rem(s, 4)
    x = x_hi * 2 + x_lo

    sibling = (p + 1 - 2 * core, s)

    def x_peer(d):
        to = lax.rem(x + d, 4)
        return to, (p + (lax.rem(to, 2) - x_lo) * 2, s + (to // 2 - x_hi) * 4)

    def y_peer(d):
        to = lax.rem(y + d, 4)
        return to, (p, s + to - y)

    def z_peer(d):
        to = lax.rem(z + d, 8)
        return to, (p + (to - z) * 4, s)

    def map_peer(d):
        other = lax.rem(s + d, 8)
        apart = other // 4 - x_hi
        return (p + apart * apart * (2 - 4 * x_lo), other)

    def send(src, dst, ssem, rsem, peer):
        copy = pltpu.make_async_remote_copy(
            src_ref=src, dst_ref=dst, send_sem=ssem, recv_sem=rsem, device_id=peer, device_id_type=MESH
        )
        copy.start()
        return copy

    peers = [sibling] + [x_peer(d)[1] for d in (1, 2, 3)] + [z_peer(d)[1] for d in range(1, 8)]
    peers += [map_peer(d) for d in range(1, 8)]
    barrier = pltpu.get_barrier_semaphore()
    for peer in peers:
        pl.semaphore_signal(barrier, inc=1, device_id=peer, device_id_type=MESH)
    pairs = [
        (blk_h, blk), (kind_h, kind), (img_h, img), (ctf_h, ctf), (cls_h, cls), (bank_h, bank),
        (piece, full.at[s]), (fx_h, fx), (fy_h, fy),
    ]
    loads = [pltpu.make_async_copy(a, b, own_sem.at[n]) for n, (a, b) in enumerate(pairs)]
    for load in loads:
        load.start()
    pl.semaphore_wait(barrier, len(peers))
    sends = []
    for d in (6, 2, 5, 3, 7, 1, 4):
        sends.append(send(piece, full.at[s], gather_s.at[d], gather_r.at[d], map_peer(d)))

    loads[0].wait()
    loads[1].wait()
    number = kind[...] * NBLK + blk[...]
    for h in range(2):
        pair = jnp.concatenate([number[:, 2 * h, :], number[:, 2 * h + 1, :]], axis=1)
        rid_v[pl.ds(h * 32, 32), :] = pair
    to_scalar = pltpu.make_async_copy(rid_v, rid, own_sem.at[len(pairs)])
    to_scalar.start()

    for load in loads[2:6]:
        load.wait()
    lanes = lax.broadcasted_iota(jnp.int32, (16, 64), 1)
    which = lax.broadcasted_iota(jnp.int32, (16, 64), 0)
    pick = jnp.where(which == 0, cls[0], cls[1])
    onehot = (lanes == pick).astype(F32).astype(BF16)
    gain = jnp.dot(onehot, ctf[...], preferred_element_type=F32)
    pixel = img[...].astype(F32)
    for i in range(2):
        g = gain[i : i + 1]
        for c, row in enumerate((g * pixel[i, 0:1], g * pixel[i, 1:2], g * g)):
            for b in range(PB):
                parts[pl.ds(c * 32 + i * PB + b, 1), :] = row[:, b * BW : (b + 1) * BW]
    both = jnp.concatenate(split(parts[...]), axis=0)
    for k in range(KINDS):
        out = lax.dot_general(both, bank[k], NT, preferred_element_type=F32)
        out = out[:96] + out[96:]
        for c in range(3):
            rows[c, pl.ds(k, 32, stride=KINDS), :] = out[c * 32 : (c + 1) * 32]

    row_id = lax.broadcasted_iota(jnp.int32, (64, 128), 0)
    col_id = lax.broadcasted_iota(jnp.int32, (128, 128), 0)

    @pl.loop(0, 32)
    def _(ip):
        for h in range(2):
            v = rid_v[pl.ds(h * 32 + ip, 1), :]
            high = ((v >> 5) & 1) * 4 + ((v >> 4) & 1) * 2 + ((v >> 6) & 1)
            low = ((v >> 2) & 3) * 32 + ((v >> 7) & 7) * 4 + (v & 3)
            at = pl.ds(h * 128, 128)
            left[ip, :, at] = jnp.where(row_id == high * KINDS + (v >> 10), 1.0, 0.0).astype(BF16)
            right[ip, :, at] = jnp.where(col_id == low, 1.0, 0.0).astype(BF16)

    def map_piece(source):
        lhs = jnp.concatenate([full[source, :, :BW], full[source, :, BW:]], axis=0)
        for k in range(0, KINDS, 2):
            out = jnp.dot(lhs, jnp.concatenate([bank[k], bank[k + 1]], axis=1), preferred_element_type=F32)
            for h in range(2):
                at = pl.ds(pl.multiple_of((k + h) * NBLK + source * BW, BW), BW)
                for c in range(2):
                    half = out[c * BW : (c + 1) * BW, h * BW : (h + 1) * BW]
                    table[c, at, :] = half.astype(BF16).astype(F32)

    loads[6].wait()
    map_piece(s)

    @pl.loop(1, 8)
    def _(d):
        source = lax.rem(s + 8 - d, 8)
        pltpu.make_async_remote_copy(
            src_ref=piece, dst_ref=full.at[source], send_sem=gather_s.at[d], recv_sem=gather_r.at[d],
            device_id=map_peer(d), device_id_type=MESH,
        ).wait_recv()
        map_piece(source)

    to_scalar.wait()
    loads[7].wait()
    loads[8].wait()

    def gather(i, b):
        ip = i * PB + b
        for j in range(CAND):
            taps = [rid[h * 32 + ip, q * CAND + j] for h in range(2) for q in range(2)]
            for c in range(2):
                taken = [table[c, r] for r in taps]
                total = (taken[0] + taken[1]) + (taken[2] + taken[3])
                proj[c, pl.ds(pl.multiple_of(b * CAND, CAND) + j, 1), :] = total.reshape(1, BW)

    def posterior(i):
        for b in range(PB):
            ca = parts[pl.ds(i * PB + b, 1), :]
            cb = parts[pl.ds(32 + i * PB + b, 1), :]
            u = proj[0, pl.ds(b * CAND, CAND), :]
            w = proj[1, pl.ds(b * CAND, CAND), :]
            cross[:, pl.ds(b * 256, 128)] = (ca * u + cb * w).astype(BF16)
            cross[:, pl.ds(b * 256 + 128, 128)] = (cb * u - ca * w).astype(BF16)
        along = [
            jnp.dot(cross[:, g * 1024 : (g + 1) * 1024], fx[...], preferred_element_type=F32)
            for g in range(4)
        ]
        along = jnp.concatenate(along, axis=1)
        both = jnp.concatenate(split(along), axis=0)
        scores = lax.dot_general(fy[...], both, NT, preferred_element_type=F32)
        scores = scores[:, :CAND] + scores[:, CAND:]
        energy = jnp.sum(scores * scores, axis=0, keepdims=True) * (1.0 / (SIDE * SIDE))
        post = CAND * energy / (jnp.sum(energy, axis=1, keepdims=True) + 1e-6)
        post_out[pl.ds(i, 1), :] = post
        pair = jnp.concatenate([post, post, post, post], axis=1)
        return split(pair)

    def histogram(i, b, w_hi, w_lo):
        ip = i * PB + b
        hit = left[ip]
        hits = jnp.concatenate([hit * w_hi, hit * w_lo], axis=0)
        out = lax.dot_general(hits, right[ip], NT, preferred_element_type=F32)
        out = out[:64] + out[64:]
        at = pl.ds(pl.multiple_of(ip * KINDS, KINDS), KINDS)
        for h in range(8):
            hist[at, pl.ds(h * 128, 128)] = out[h * 8 : (h + 1) * 8]

    @pl.loop(0, PB)
    def _(b):
        gather(0, b)

    first = posterior(0)

    @pl.loop(0, PB)
    def _(b):
        gather(1, b)
        histogram(0, b, *first)

    second = posterior(1)

    @pl.loop(0, PB)
    def _(b):
        histogram(1, b, *second)

    d_hi, d_lo = split(jnp.concatenate([rows[c] for c in range(3)], axis=1))
    d_both = jnp.concatenate([d_hi, d_lo], axis=1)

    def map_sums(of_core, to):
        start = pl.multiple_of((of_core * 4 + to) * 128, 128)
        h_hi, h_lo = split(hist[:, pl.ds(start, 128)].T)
        out = jnp.dot(h_hi, d_both, preferred_element_type=F32)
        out = out[:, :384] + out[:, 384:] + jnp.dot(h_lo, d_hi, preferred_element_type=F32)
        return out.reshape(4, 32, 384)

    order = (2, 1, 3, 0)
    to_near = []
    for n, d in enumerate(order):
        to = lax.rem(x + d, 4)
        sums[to] = map_sums(1 - core, to)
        to_near.append(send(sums.at[to], near.at[to], near_s.at[n], near_r.at[n], sibling))
    last = []
    for n, d in enumerate(order):
        to, peer = x_peer(d)
        mine = map_sums(core, to)
        to_near[n].wait_recv()
        s1[to] = mine + near[to]
        if d:
            last.append(send(s1.at[to, :, pl.ds(0, 16)], a1.at[d], xs.at[d], xr.at[d], peer))
    done = []
    for d in (2, 1, 3):
        to, peer = y_peer(d)
        done.append(send(s1.at[:, to, pl.ds(16, 16)], b1.at[d], ys.at[d], yr.at[d], peer))
    for copy in last:
        copy.wait_recv()
    s2a[...] = (s1[x, :, 0:16, :] + a1[1]) + (a1[2] + a1[3])
    then = []
    for d in (2, 1, 3):
        to, peer = y_peer(d)
        then.append(send(s2a.at[to], a2.at[d], y2s.at[d], y2r.at[d], peer))
    for copy in done:
        copy.wait_recv()
    s2b[...] = (s1[:, y, 16:32, :] + b1[1]) + (b1[2] + b1[3])
    for d in (2, 1, 3):
        to, peer = x_peer(d)
        then.append(send(s2b.at[to], b2.at[d], x2s.at[d], x2r.at[d], peer))
    for copy in then[:3]:
        copy.wait_recv()
    low = (s2a[y] + a2[1]) + (a2[2] + a2[3])
    for n in range(4):
        s3[n] = low[n * 4 : (n + 1) * 4]
    for copy in then[3:]:
        copy.wait_recv()
    high = (s2b[x] + b2[1]) + (b2[2] + b2[3])
    for n in range(4):
        s3[4 + n] = high[n * 4 : (n + 1) * 4]
    third = []
    for d in (4, 3, 5, 2, 6, 1, 7):
        to, peer = z_peer(d)
        third.append(send(s3.at[to], r3.at[d], zs.at[d], zr.at[d], peer))
    for copy in third:
        copy.wait_recv()
    total = s3[z]
    for d in range(1, 8):
        total = total + r3[d]
    data[...] = total[:, :256]
    weight[...] = total[:, 256:]
    for copy in sends + to_near + last + done + then + third:
        copy.wait_send()


def local(ref_map, images, ctf_table, ctf_class, block_index, interp_kind, interp_bank):
    blk = jnp.transpose(block_index, (0, 2, 3, 1)).reshape(32, TAPS, CAND)
    kind = jnp.transpose(interp_kind, (0, 2, 3, 1)).reshape(32, TAPS, CAND)
    dma = pltpu.SemaphoreType.DMA
    i32 = jnp.int32
    return pl.pallas_call(
        refine_kernel,
        out_shape=[
            jax.ShapeDtypeStruct((4, 256), F32),
            jax.ShapeDtypeStruct((4, 128), F32),
            jax.ShapeDtypeStruct((2, CAND), F32),
        ],
        in_specs=[pl.BlockSpec(memory_space=pltpu.HBM)] * 9,
        out_specs=[pl.BlockSpec(memory_space=VMEM)] * 3,
        scratch_shapes=[
            VMEM((2, 2, 2048), BF16),
            VMEM((64, 2048), BF16),
            pltpu.SMEM((2,), i32),
            VMEM((32, TAPS, CAND), i32),
            VMEM((32, TAPS, CAND), i32),
            VMEM((KINDS, BW, BW), BF16),
            VMEM((1024, 128), BF16),
            VMEM((1024, 512), BF16),
            dma((10,)),
            VMEM((8, BW, 2 * BW), BF16),
            VMEM((2, KINDS * NBLK, BW), F32),
            VMEM((96, BW), F32),
            VMEM((3, 256, BW), F32),
            VMEM((64, 128), i32),
            pltpu.SMEM((64, 128), i32),
            VMEM((32, 64, 256), BF16),
            VMEM((32, 128, 256), BF16),
            VMEM((2, CAND * PB, BW), F32),
            VMEM((CAND, 4096), BF16),
            VMEM((256, NBLK), F32),
            dma((8,)), dma((8,)),
            VMEM((4, 4, 32, 384), F32),
            VMEM((4, 4, 32, 384), F32),
            VMEM((4, 4, 32, 384), F32),
            VMEM((4, 4, 16, 384), F32),
            VMEM((4, 4, 16, 384), F32),
            VMEM((4, 16, 384), F32),
            VMEM((4, 16, 384), F32),
            VMEM((4, 16, 384), F32),
            VMEM((4, 16, 384), F32),
            VMEM((8, 4, 384), F32),
            VMEM((8, 4, 384), F32),
            dma((4,)), dma((4,)), dma((4,)), dma((4,)), dma((4,)), dma((4,)),
            dma((4,)), dma((4,)), dma((4,)), dma((4,)), dma((8,)), dma((8,)),
        ],
        compiler_params=pltpu.CompilerParams(
            collective_id=0, has_side_effects=True, vmem_limit_bytes=56 * 1024 * 1024
        ),
        name="refine",
    )(
        ref_map, images, ctf_table, ctf_class, blk, kind, interp_bank,
        jnp.asarray(line_table(), BF16), jnp.asarray(across_table(), BF16),
    )


def solution(mesh):
    in_specs = (
        P("slab", None),
        P(("particle", "slab"), None, None),
        P(),
        P(("particle", "slab")),
        P(("particle", "slab"), None, None, None),
        P(("particle", "slab"), None, None, None),
        P(),
    )
    out_specs = (
        P(("particle", "slab"), None),
        P(("particle", "slab"), None),
        P(("particle", "slab"), None),
    )
    return jax.shard_map(local, mesh=mesh, in_specs=in_specs, out_specs=out_specs, check_vma=False)
```

```python
import jax
import jax.numpy as jnp
import numpy as np
from jax import lax
from jax.experimental import pallas as pl
from jax.experimental.pallas import tpu as pltpu
from jax.sharding import PartitionSpec as P

LINE = 256
PLINES = 8
SIDE = 32
BW = 128
TAPS = 4
KINDS = 8
CAND = 64
PB = 16
NBLK = 1024
MESH = pl.DeviceIdType.MESH
VMEM = pltpu.VMEM
F32 = jnp.float32
BF16 = jnp.bfloat16
NT = (((1,), (1,)), ((), ()))


def line_table():
    fx = np.arange(LINE) - LINE // 2
    sx = np.arange(SIDE) - SIDE // 2
    ang = 2.0 * np.pi / LINE * ((fx[:, None] * sx[None, :]) % LINE)
    cos, sin = np.cos(ang), np.sin(ang)
    one = np.zeros((2, 2, BW, 2, SIDE))
    one[:, 0, :, 0] = cos.reshape(2, BW, SIDE)
    one[:, 1, :, 0] = -sin.reshape(2, BW, SIDE)
    one[:, 0, :, 1] = sin.reshape(2, BW, SIDE)
    one[:, 1, :, 1] = cos.reshape(2, BW, SIDE)
    both = np.zeros((2, 2, 2, BW, 2, 2, SIDE))
    both[0, :, :, :, 0] = one
    both[1, :, :, :, 1] = one
    return both.reshape(8 * BW, 4 * SIDE)


def across_table():
    fy = np.arange(PLINES) - PLINES // 2
    sy = np.arange(SIDE) - SIDE // 2
    ang = 2.0 * np.pi / LINE * ((fy[None, :] * sy[:, None]) % LINE)
    full = np.zeros((SIDE, SIDE, PLINES, 2, SIDE))
    for s in range(SIDE):
        full[:, s, :, 0, s] = np.cos(ang)
        full[:, s, :, 1, s] = -np.sin(ang)
    return full.reshape(SIDE * SIDE, PLINES * 2 * SIDE)


def split(v):
    hi = v.astype(BF16)
    return hi, (v - hi.astype(F32)).astype(BF16)


def refine_kernel(
    piece, img_h, ctf_h, cls_h, blk_h, kind_h, bank_h, fx_h, fy_h,
    out,
    img, ctf, cls, blk, kind, bank, fx, fy, own_sem,
    full, inter, table, parts, rows, rid_v, rid, left, right,
    proj, cross, hist, gather_s, gather_r,
    sums, near, s1, a1, b1, s2a, s2b, a2, b2, s3, r3,
    near_s, near_r, xs, xr, ys, yr, x2s, x2r, y2s, y2r, zs, zr, here,
):
    p = lax.axis_index("particle")
    s = lax.axis_index("slab")
    z, x_lo, core = p // 4, lax.rem(p // 2, 2), lax.rem(p, 2)
    x_hi, y = s // 4, lax.rem(s, 4)
    x = x_hi * 2 + x_lo

    sibling = (p + 1 - 2 * core, s)

    def x_peer(d):
        to = lax.rem(x + d, 4)
        return to, (p + (lax.rem(to, 2) - x_lo) * 2, s + (to // 2 - x_hi) * 4)

    def y_peer(d):
        to = lax.rem(y + d, 4)
        return to, (p, s + to - y)

    def z_peer(d):
        to = lax.rem(z + d, 8)
        return to, (p + (to - z) * 4, s)

    def map_peer(d):
        other = lax.rem(s + d, 8)
        apart = other // 4 - x_hi
        return (p + apart * apart * (2 - 4 * x_lo), other)

    def send(src, dst, ssem, rsem, peer):
        copy = pltpu.make_async_remote_copy(
            src_ref=src, dst_ref=dst, send_sem=ssem, recv_sem=rsem, device_id=peer, device_id_type=MESH
        )
        copy.start()
        return copy

    peers = [sibling] + [x_peer(d)[1] for d in (1, 2, 3)] + [z_peer(d)[1] for d in (1, 7)]
    peers += [map_peer(d) for d in range(1, 8)]
    barrier = pltpu.get_barrier_semaphore()
    for peer in peers:
        pl.semaphore_signal(barrier, inc=1, device_id=peer, device_id_type=MESH)
    pairs = [
        (blk_h, blk), (kind_h, kind), (img_h, img), (ctf_h, ctf), (cls_h, cls), (bank_h, bank),
        (piece, full.at[s]), (fx_h, fx), (fy_h, fy),
    ]
    loads = [pltpu.make_async_copy(a, b, own_sem.at[n]) for n, (a, b) in enumerate(pairs)]
    for load in loads:
        load.start()
    pl.semaphore_wait(barrier, len(peers))
    sends = []
    for d in (6, 2, 5, 3, 7, 1, 4):
        sends.append(send(piece, full.at[s], gather_s.at[d], gather_r.at[d], map_peer(d)))

    def tell(n):
        for side, d in enumerate((1, 7)):
            pl.semaphore_signal(here.at[n, side], inc=1, device_id=z_peer(d)[1], device_id_type=MESH)

    def hear(n):
        for side in range(2):
            pl.semaphore_wait(here.at[n, side], 1)

    tell(0)

    loads[0].wait()
    loads[1].wait()
    number = kind[...] * NBLK + blk[...]
    for h in range(2):
        pair = jnp.concatenate([number[:, 2 * h, :], number[:, 2 * h + 1, :]], axis=1)
        rid_v[pl.ds(h * 32, 32), :] = pair * 2
    to_scalar = pltpu.make_async_copy(rid_v, rid, own_sem.at[len(pairs)])
    to_scalar.start()

    for load in loads[2:6]:
        load.wait()
    lanes = lax.broadcasted_iota(jnp.int32, (16, 64), 1)
    which = lax.broadcasted_iota(jnp.int32, (16, 64), 0)
    pick = jnp.where(which == 0, cls[0], cls[1])
    onehot = (lanes == pick).astype(F32).astype(BF16)
    gain = jnp.dot(onehot, ctf[...], preferred_element_type=F32)
    pixel = img[...].astype(F32)
    for i in range(2):
        g = gain[i : i + 1]
        for c, row in enumerate((g * pixel[i, 0:1], g * pixel[i, 1:2], g * g)):
            for b in range(PB):
                parts[pl.ds(c * 32 + i * PB + b, 1), :] = row[:, b * BW : (b + 1) * BW]
    both = jnp.concatenate(split(parts[...]), axis=0)
    for k in range(KINDS):
        turned = lax.dot_general(both, bank[k], NT, preferred_element_type=F32)
        turned = turned[:96] + turned[96:]
        for c in range(3):
            rows[c, pl.ds(k, 32, stride=KINDS), :] = turned[c * 32 : (c + 1) * 32]

    row_id = lax.broadcasted_iota(jnp.int32, (64, 128), 0)
    col_id = lax.broadcasted_iota(jnp.int32, (128, 128), 0)

    @pl.loop(0, 32)
    def _(ip):
        for h in range(2):
            v = rid_v[pl.ds(h * 32 + ip, 1), :] >> 1
            high = ((v >> 5) & 1) * 4 + ((v >> 4) & 1) * 2 + ((v >> 6) & 1)
            low = ((v >> 2) & 3) * 32 + ((v >> 7) & 7) * 4 + (v & 3)
            at = pl.ds(h * 128, 128)
            left[ip, :, at] = jnp.where(row_id == high * KINDS + (v >> 10), 1.0, 0.0).astype(BF16)
            right[ip, :, at] = jnp.where(col_id == low, 1.0, 0.0).astype(BF16)

    hear(0)
    tell(1)

    def map_piece(source):
        inter[pl.ds(0, BW, stride=2), :] = full[source, :, :BW].astype(F32)
        inter[pl.ds(1, BW, stride=2), :] = full[source, :, BW:].astype(F32)
        lhs = inter[...].astype(BF16)
        for k in range(0, KINDS, 2):
            mapped = jnp.dot(lhs, jnp.concatenate([bank[k], bank[k + 1]], axis=1), preferred_element_type=F32)
            for h in range(2):
                at = pl.ds(pl.multiple_of((k + h) * 2 * NBLK + source * 256, 256), 256)
                table[at, :] = mapped[:, h * BW : (h + 1) * BW].astype(BF16).astype(F32)

    loads[6].wait()
    map_piece(s)

    @pl.loop(1, 8)
    def _(d):
        source = lax.rem(s + 8 - d, 8)
        pltpu.make_async_remote_copy(
            src_ref=piece, dst_ref=full.at[source], send_sem=gather_s.at[d], recv_sem=gather_r.at[d],
            device_id=map_peer(d), device_id_type=MESH,
        ).wait_recv()
        map_piece(source)

    hear(1)
    tell(2)
    to_scalar.wait()
    loads[7].wait()
    loads[8].wait()

    def gather(i, b):
        ip = i * PB + b
        for j in range(CAND):
            taps = [rid[h * 32 + ip, q * CAND + j] for h in range(2) for q in range(2)]
            for c in range(2):
                taken = [table[r + c] for r in taps]
                total = (taken[0] + taken[1]) + (taken[2] + taken[3])
                proj[c, pl.ds(pl.multiple_of(b * CAND, CAND) + j, 1), :] = total.reshape(1, BW)

    def posterior(i):
        for b in range(PB):
            ca = parts[pl.ds(i * PB + b, 1), :]
            cb = parts[pl.ds(32 + i * PB + b, 1), :]
            u = proj[0, pl.ds(b * CAND, CAND), :]
            w = proj[1, pl.ds(b * CAND, CAND), :]
            cross[:, pl.ds(b * 256, 128)] = (ca * u + cb * w).astype(BF16)
            cross[:, pl.ds(b * 256 + 128, 128)] = (cb * u - ca * w).astype(BF16)
        along = [
            jnp.dot(cross[:, g * 1024 : (g + 1) * 1024], fx[...], preferred_element_type=F32)
            for g in range(4)
        ]
        along = jnp.concatenate(along, axis=1)
        both = jnp.concatenate(split(along), axis=0)
        scores = lax.dot_general(fy[...], both, NT, preferred_element_type=F32)
        scores = scores[:, :CAND] + scores[:, CAND:]
        energy = jnp.sum(scores * scores, axis=0, keepdims=True) * (1.0 / (SIDE * SIDE))
        post = CAND * energy / (jnp.sum(energy, axis=1, keepdims=True) + 1e-6)
        out[pl.ds(4 + i, 1), pl.ds(0, CAND)] = post
        pair = jnp.concatenate([post, post, post, post], axis=1)
        return split(pair)

    def histogram(i, b, w_hi, w_lo):
        ip = i * PB + b
        hit = left[ip]
        hits = jnp.concatenate([hit * w_hi, hit * w_lo], axis=0)
        both = lax.dot_general(hits, right[ip], NT, preferred_element_type=F32)
        both = both[:64] + both[64:]
        at = pl.ds(pl.multiple_of(ip * KINDS, KINDS), KINDS)
        for h in range(8):
            hist[at, pl.ds(h * 128, 128)] = both[h * 8 : (h + 1) * 8]

    @pl.loop(0, PB)
    def _(b):
        gather(0, b)

    first = posterior(0)
    hear(2)

    @pl.loop(0, PB)
    def _(b):
        gather(1, b)
        histogram(0, b, *first)

    second = posterior(1)

    @pl.loop(0, PB, unroll=4)
    def _(b):
        histogram(1, b, *second)

    d_hi, d_lo = split(jnp.concatenate([rows[c] for c in range(3)], axis=1))
    d_both = jnp.concatenate([d_hi, d_lo], axis=1)

    def map_sums(of_core, to):
        start = pl.multiple_of((of_core * 4 + to) * 128, 128)
        h_hi, h_lo = split(hist[:, pl.ds(start, 128)].T)
        got = jnp.dot(h_hi, d_both, preferred_element_type=F32)
        got = got[:, :384] + got[:, 384:] + jnp.dot(h_lo, d_hi, preferred_element_type=F32)
        return got.reshape(4, 32, 384)

    order = (2, 1, 3, 0)
    to_near = []
    for n, d in enumerate(order):
        to = lax.rem(x + d, 4)
        sums[to] = map_sums(1 - core, to)
        to_near.append(send(sums.at[to], near.at[to], near_s.at[n], near_r.at[n], sibling))
    last = []
    for n, d in enumerate(order):
        to, peer = x_peer(d)
        mine = map_sums(core, to)
        to_near[n].wait_recv()
        s1[to] = mine + near[to]
        if d:
            last.append(send(s1.at[to, :, pl.ds(0, 16)], a1.at[d], xs.at[d], xr.at[d], peer))
    done = []
    for d in (2, 1, 3):
        to, peer = y_peer(d)
        done.append(send(s1.at[:, to, pl.ds(16, 16)], b1.at[d], ys.at[d], yr.at[d], peer))
    for copy in last:
        copy.wait_recv()
    s2a[...] = (s1[x, :, 0:16, :] + a1[1]) + (a1[2] + a1[3])
    then = []
    for d in (2, 1, 3):
        to, peer = y_peer(d)
        then.append(send(s2a.at[to], a2.at[d], y2s.at[d], y2r.at[d], peer))
    for copy in done:
        copy.wait_recv()
    s2b[...] = (s1[:, y, 16:32, :] + b1[1]) + (b1[2] + b1[3])
    for d in (2, 1, 3):
        to, peer = x_peer(d)
        then.append(send(s2b.at[to], b2.at[d], x2s.at[d], x2r.at[d], peer))
    for copy in then[:3]:
        copy.wait_recv()
    low = (s2a[y] + a2[1]) + (a2[2] + a2[3])
    for n in range(4):
        s3[n] = low[n * 4 : (n + 1) * 4]
    for copy in then[3:]:
        copy.wait_recv()
    high = (s2b[x] + b2[1]) + (b2[2] + b2[3])
    for n in range(4):
        s3[4 + n] = high[n * 4 : (n + 1) * 4]
    third = []
    for d in (4, 3, 5, 2, 6, 1, 7):
        to, peer = z_peer(d)
        third.append(send(s3.at[to], r3.at[d], zs.at[d], zr.at[d], peer))
    for copy in third:
        copy.wait_recv()
    total = s3[z]
    for d in range(1, 8):
        total = total + r3[d]
    out[0:4, :] = total
    for copy in sends + to_near + last + done + then + third:
        copy.wait_send()


def local(ref_map, images, ctf_table, ctf_class, block_index, interp_kind, interp_bank):
    blk = jnp.transpose(block_index, (0, 2, 3, 1)).reshape(32, TAPS, CAND)
    kind = jnp.transpose(interp_kind, (0, 2, 3, 1)).reshape(32, TAPS, CAND)
    dma = pltpu.SemaphoreType.DMA
    i32 = jnp.int32
    out = pl.pallas_call(
        refine_kernel,
        out_shape=jax.ShapeDtypeStruct((8, 384), F32),
        in_specs=[pl.BlockSpec(memory_space=pltpu.HBM)] * 9,
        out_specs=pl.BlockSpec(memory_space=VMEM),
        scratch_shapes=[
            VMEM((2, 2, 2048), BF16),
            VMEM((64, 2048), BF16),
            pltpu.SMEM((2,), i32),
            VMEM((32, TAPS, CAND), i32),
            VMEM((32, TAPS, CAND), i32),
            VMEM((KINDS, BW, BW), BF16),
            VMEM((1024, 128), BF16),
            VMEM((1024, 512), BF16),
            dma((10,)),
            VMEM((8, BW, 2 * BW), BF16),
            VMEM((2 * BW, BW), F32),
            VMEM((2 * KINDS * NBLK, BW), F32),
            VMEM((96, BW), F32),
            VMEM((3, 256, BW), F32),
            VMEM((64, 128), i32),
            pltpu.SMEM((64, 128), i32),
            VMEM((32, 64, 256), BF16),
            VMEM((32, 128, 256), BF16),
            VMEM((2, CAND * PB, BW), F32),
            VMEM((CAND, 4096), BF16),
            VMEM((256, NBLK), F32),
            dma((8,)), dma((8,)),
            VMEM((4, 4, 32, 384), F32),
            VMEM((4, 4, 32, 384), F32),
            VMEM((4, 4, 32, 384), F32),
            VMEM((4, 4, 16, 384), F32),
            VMEM((4, 4, 16, 384), F32),
            VMEM((4, 16, 384), F32),
            VMEM((4, 16, 384), F32),
            VMEM((4, 16, 384), F32),
            VMEM((4, 16, 384), F32),
            VMEM((8, 4, 384), F32),
            VMEM((8, 4, 384), F32),
            dma((4,)), dma((4,)), dma((4,)), dma((4,)), dma((4,)), dma((4,)),
            dma((4,)), dma((4,)), dma((4,)), dma((4,)), dma((8,)), dma((8,)),
            pltpu.SemaphoreType.REGULAR((3, 2)),
        ],
        compiler_params=pltpu.CompilerParams(
            collective_id=0, has_side_effects=True, vmem_limit_bytes=56 * 1024 * 1024
        ),
        name="refine",
    )(
        ref_map, images, ctf_table, ctf_class, blk, kind, interp_bank,
        jnp.asarray(line_table(), BF16), jnp.asarray(across_table(), BF16),
    )
    return (out[:4, :256], out[:4, 256:], out[4:6, :CAND])


def solution(mesh):
    in_specs = (
        P("slab", None),
        P(("particle", "slab"), None, None),
        P(),
        P(("particle", "slab")),
        P(("particle", "slab"), None, None, None),
        P(("particle", "slab"), None, None, None),
        P(),
    )
    out_specs = (
        P(("particle", "slab"), None),
        P(("particle", "slab"), None),
        P(("particle", "slab"), None),
    )
    return jax.shard_map(local, mesh=mesh, in_specs=in_specs, out_specs=out_specs, check_vma=False)
```

```python
import jax
import jax.numpy as jnp
import numpy as np
from jax import lax
from jax.experimental import pallas as pl
from jax.experimental.pallas import tpu as pltpu
from jax.sharding import PartitionSpec as P

LINE = 256
PLINES = 8
SIDE = 32
BW = 128
TAPS = 4
KINDS = 8
CAND = 64
PB = 16
NBLK = 1024
MESH = pl.DeviceIdType.MESH
ORDER = (1, 2, 3, 4, 5, 6, 7)
VMEM = pltpu.VMEM
F32 = jnp.float32
BF16 = jnp.bfloat16
NT = (((1,), (1,)), ((), ()))


def line_table():
    fx = np.arange(LINE) - LINE // 2
    sx = np.arange(SIDE) - SIDE // 2
    ang = 2.0 * np.pi / LINE * ((fx[:, None] * sx[None, :]) % LINE)
    cos, sin = np.cos(ang), np.sin(ang)
    one = np.zeros((2, 2, BW, 2, SIDE))
    one[:, 0, :, 0] = cos.reshape(2, BW, SIDE)
    one[:, 1, :, 0] = -sin.reshape(2, BW, SIDE)
    one[:, 0, :, 1] = sin.reshape(2, BW, SIDE)
    one[:, 1, :, 1] = cos.reshape(2, BW, SIDE)
    both = np.zeros((2, 2, 2, BW, 2, 2, SIDE))
    both[0, :, :, :, 0] = one
    both[1, :, :, :, 1] = one
    return both.reshape(8 * BW, 4 * SIDE)


def across_table():
    fy = np.arange(PLINES) - PLINES // 2
    sy = np.arange(SIDE) - SIDE // 2
    ang = 2.0 * np.pi / LINE * ((fy[None, :] * sy[:, None]) % LINE)
    full = np.zeros((SIDE, SIDE, PLINES, 2, SIDE))
    for s in range(SIDE):
        full[:, s, :, 0, s] = np.cos(ang)
        full[:, s, :, 1, s] = -np.sin(ang)
    return full.reshape(SIDE * SIDE, PLINES * 2 * SIDE)


def split(v):
    hi = v.astype(BF16)
    return hi, (v - hi.astype(F32)).astype(BF16)


def refine_kernel(
    piece, img_h, ctf_h, cls_h, blk_h, kind_h, bank_h, fx_h, fy_h,
    data, weight, post_out,
    img, ctf, cls, blk, kind, bank, fx, fy, own_sem,
    full, inter, table, parts, rows, rid_v, rid, left, right,
    proj, cross, hist, gather_s, gather_r, forward_s, forward_r,
    sums, near, s1, a1, b1, s2a, s2b, a2, b2, s3, r3,
    near_s, near_r, xs, xr, ys, yr, x2s, x2r, y2s, y2r, zs, zr, here,
):
    p = lax.axis_index("particle")
    s = lax.axis_index("slab")
    z, x_lo, core = p // 4, lax.rem(p // 2, 2), lax.rem(p, 2)
    x_hi, y = s // 4, lax.rem(s, 4)
    x = x_hi * 2 + x_lo

    sibling = (p + 1 - 2 * core, s)

    def x_peer(d):
        to = lax.rem(x + d, 4)
        return to, (p + (lax.rem(to, 2) - x_lo) * 2, s + (to // 2 - x_hi) * 4)

    def y_peer(d):
        to = lax.rem(y + d, 4)
        return to, (p, s + to - y)

    def z_peer(d):
        to = lax.rem(z + d, 8)
        return to, (p + (to - z) * 4, s)

    def map_peer(n, sign):
        flip = lax.rem(n, 2)
        to = lax.rem(y + 4 + sign * (n // 2), 4)
        return (p + flip * (2 - 4 * x_lo), (x_hi + flip * (1 - 2 * x_hi)) * 4 + to)

    def send(src, dst, ssem, rsem, peer):
        copy = pltpu.make_async_remote_copy(
            src_ref=src, dst_ref=dst, send_sem=ssem, recv_sem=rsem, device_id=peer, device_id_type=MESH
        )
        copy.start()
        return copy

    peers = [sibling] + [x_peer(d)[1] for d in (1, 2, 3)] + [z_peer(d)[1] for d in (1, 7)]
    peers += [map_peer(n, 1) for n in range(1, 8)]
    barrier = pltpu.get_barrier_semaphore()
    for peer in peers:
        pl.semaphore_signal(barrier, inc=1, device_id=peer, device_id_type=MESH)
    pairs = [
        (blk_h, blk), (kind_h, kind), (img_h, img), (ctf_h, ctf), (cls_h, cls), (bank_h, bank),
        (piece, full.at[s]), (fx_h, fx), (fy_h, fy),
    ]
    loads = [pltpu.make_async_copy(a, b, own_sem.at[n]) for n, (a, b) in enumerate(pairs)]
    for load in loads:
        load.start()
    pl.semaphore_wait(barrier, len(peers))
    half = pl.ds(pl.multiple_of(core * 64, 64), 64)
    sends = []
    for n in ORDER:
        sends.append(send(piece.at[half], full.at[s, half], gather_s.at[n], gather_r.at[n], map_peer(n, 1)))

    def tell(n):
        for side, d in enumerate((1, 7)):
            pl.semaphore_signal(here.at[n, side], inc=1, device_id=z_peer(d)[1], device_id_type=MESH)

    def hear(n):
        for side in range(2):
            pl.semaphore_wait(here.at[n, side], 1)

    tell(0)

    loads[0].wait()
    loads[1].wait()
    number = kind[...] * NBLK + blk[...]
    for h in range(2):
        pair = jnp.concatenate([number[:, 2 * h, :], number[:, 2 * h + 1, :]], axis=1)
        rid_v[pl.ds(h * 32, 32), :] = pair * 2
    to_scalar = pltpu.make_async_copy(rid_v, rid, own_sem.at[len(pairs)])
    to_scalar.start()

    for load in loads[2:6]:
        load.wait()
    lanes = lax.broadcasted_iota(jnp.int32, (16, 64), 1)
    which = lax.broadcasted_iota(jnp.int32, (16, 64), 0)
    pick = jnp.where(which == 0, cls[0], cls[1])
    onehot = (lanes == pick).astype(F32).astype(BF16)
    gain = jnp.dot(onehot, ctf[...], preferred_element_type=F32)
    pixel = img[...].astype(F32)
    for i in range(2):
        g = gain[i : i + 1]
        for c, row in enumerate((g * pixel[i, 0:1], g * pixel[i, 1:2], g * g)):
            for b in range(PB):
                parts[pl.ds(c * 32 + i * PB + b, 1), :] = row[:, b * BW : (b + 1) * BW]
    both = jnp.concatenate(split(parts[...]), axis=0)
    for k in range(KINDS):
        turned = lax.dot_general(both, bank[k], NT, preferred_element_type=F32)
        turned = turned[:96] + turned[96:]
        for c in range(3):
            rows[c, pl.ds(k, 32, stride=KINDS), :] = turned[c * 32 : (c + 1) * 32]

    row_id = lax.broadcasted_iota(jnp.int32, (64, 128), 0)
    col_id = lax.broadcasted_iota(jnp.int32, (128, 128), 0)

    @pl.loop(0, 32)
    def _(ip):
        for h in range(2):
            v = rid_v[pl.ds(h * 32 + ip, 1), :] >> 1
            high = ((v >> 5) & 1) * 4 + ((v >> 4) & 1) * 2 + ((v >> 6) & 1)
            low = ((v >> 2) & 3) * 32 + ((v >> 7) & 7) * 4 + (v & 3)
            at = pl.ds(h * 128, 128)
            left[ip, :, at] = jnp.where(row_id == high * KINDS + (v >> 10), 1.0, 0.0).astype(BF16)
            right[ip, :, at] = jnp.where(col_id == low, 1.0, 0.0).astype(BF16)

    def map_piece(source):
        inter[pl.ds(0, BW, stride=2), :] = full[source, :, :BW].astype(F32)
        inter[pl.ds(1, BW, stride=2), :] = full[source, :, BW:].astype(F32)
        lhs = inter[...].astype(BF16)
        for k in range(0, KINDS, 2):
            mapped = jnp.dot(lhs, jnp.concatenate([bank[k], bank[k + 1]], axis=1), preferred_element_type=F32)
            for h in range(2):
                at = pl.ds(pl.multiple_of((k + h) * 2 * NBLK + source * 256, 256), 256)
                table[at, :] = mapped[:, h * BW : (h + 1) * BW].astype(BF16).astype(F32)

    loads[6].wait()
    map_piece(s)

    def forward(n, rows):
        at = full.at[map_peer(n, -1)[1], rows]
        return pltpu.make_async_remote_copy(
            src_ref=at, dst_ref=at, send_sem=forward_s.at[n], recv_sem=forward_r.at[n],
            device_id=sibling, device_id_type=MESH,
        )

    other_half = pl.ds(pl.multiple_of((1 - core) * 64, 64), 64)
    for n in ORDER:
        peer = map_peer(n, -1)
        pltpu.make_async_remote_copy(
            src_ref=piece.at[half], dst_ref=full.at[peer[1], half], send_sem=gather_s.at[n],
            recv_sem=gather_r.at[n], device_id=peer, device_id_type=MESH,
        ).wait_recv()
        forward(n, half).start()

    @pl.loop(1, 8)
    def _(n):
        forward(n, other_half).wait_recv()
        map_piece(map_peer(n, -1)[1])

    for n in range(1, 8):
        forward(n, half).wait_send()

    hear(0)
    tell(1)
    to_scalar.wait()
    loads[7].wait()
    loads[8].wait()

    def gather(i, b):
        ip = i * PB + b
        for j in range(CAND):
            taps = [rid[h * 32 + ip, q * CAND + j] for h in range(2) for q in range(2)]
            taken = [table[pl.ds(r, 2), :] for r in taps]
            total = (taken[0] + taken[1]) + (taken[2] + taken[3])
            proj[pl.ds(pl.multiple_of(b * 2 * CAND, 2 * CAND) + 2 * j, 2), :] = total

    def posterior(i):
        for b in range(PB):
            ca = parts[pl.ds(i * PB + b, 1), :]
            cb = parts[pl.ds(32 + i * PB + b, 1), :]
            u = proj[pl.ds(b * 2 * CAND, CAND, stride=2), :]
            w = proj[pl.ds(b * 2 * CAND + 1, CAND, stride=2), :]
            cross[:, pl.ds(b * 256, 128)] = (ca * u + cb * w).astype(BF16)
            cross[:, pl.ds(b * 256 + 128, 128)] = (cb * u - ca * w).astype(BF16)
        along = [
            jnp.dot(cross[:, g * 1024 : (g + 1) * 1024], fx[...], preferred_element_type=F32)
            for g in range(4)
        ]
        along = jnp.concatenate(along, axis=1)
        both = jnp.concatenate(split(along), axis=0)
        scores = lax.dot_general(fy[...], both, NT, preferred_element_type=F32)
        scores = scores[:, :CAND] + scores[:, CAND:]
        energy = jnp.sum(scores * scores, axis=0, keepdims=True) * (1.0 / (SIDE * SIDE))
        post = CAND * energy / (jnp.sum(energy, axis=1, keepdims=True) + 1e-6)
        post_out[pl.ds(i, 1), :] = post
        pair = jnp.concatenate([post, post, post, post], axis=1)
        return split(pair)

    def histogram(i, b, w_hi, w_lo):
        ip = i * PB + b
        hit = left[ip]
        hits = jnp.concatenate([hit * w_hi, hit * w_lo], axis=0)
        both = lax.dot_general(hits, right[ip], NT, preferred_element_type=F32)
        both = both[:64] + both[64:]
        at = pl.ds(pl.multiple_of(ip * KINDS, KINDS), KINDS)
        for h in range(8):
            hist[at, pl.ds(h * 128, 128)] = both[h * 8 : (h + 1) * 8]

    @pl.loop(0, PB)
    def _(b):
        gather(0, b)

    first = posterior(0)
    hear(1)
    tell(2)

    @pl.loop(0, PB)
    def _(b):
        gather(1, b)

    second = posterior(1)
    hear(2)

    for i, pair in enumerate((first, second)):

        @pl.loop(0, PB, unroll=8)
        def _(b):
            histogram(i, b, *pair)

    d_hi, d_lo = split(jnp.concatenate([rows[c] for c in range(3)], axis=1))
    d_both = jnp.concatenate([d_hi, d_lo], axis=1)

    def map_sums(of_core, to):
        start = pl.multiple_of((of_core * 4 + to) * 128, 128)
        h_hi, h_lo = split(hist[:, pl.ds(start, 128)].T)
        got = jnp.dot(h_hi, d_both, preferred_element_type=F32)
        got = got[:, :384] + got[:, 384:] + jnp.dot(h_lo, d_hi, preferred_element_type=F32)
        return got.reshape(4, 32, 384)

    order = (2, 1, 3, 0)
    to_near = []
    for n, d in enumerate(order):
        to = lax.rem(x + d, 4)
        sums[to] = map_sums(1 - core, to)
        to_near.append(send(sums.at[to], near.at[to], near_s.at[n], near_r.at[n], sibling))
    last = []
    for n, d in enumerate(order):
        to, peer = x_peer(d)
        mine = map_sums(core, to)
        to_near[n].wait_recv()
        s1[to] = mine + near[to]
        if d:
            last.append(send(s1.at[to, :, pl.ds(0, 16)], a1.at[d], xs.at[d], xr.at[d], peer))
    done = []
    for d in (2, 1, 3):
        to, peer = y_peer(d)
        done.append(send(s1.at[:, to, pl.ds(16, 16)], b1.at[d], ys.at[d], yr.at[d], peer))
    for copy in last:
        copy.wait_recv()
    s2a[...] = (s1[x, :, 0:16, :] + a1[1]) + (a1[2] + a1[3])
    then = []
    for d in (2, 1, 3):
        to, peer = y_peer(d)
        then.append(send(s2a.at[to], a2.at[d], y2s.at[d], y2r.at[d], peer))
    for copy in done:
        copy.wait_recv()
    s2b[...] = (s1[:, y, 16:32, :] + b1[1]) + (b1[2] + b1[3])
    for d in (2, 1, 3):
        to, peer = x_peer(d)
        then.append(send(s2b.at[to], b2.at[d], x2s.at[d], x2r.at[d], peer))
    for copy in then[:3]:
        copy.wait_recv()
    low = (s2a[y] + a2[1]) + (a2[2] + a2[3])
    for n in range(4):
        s3[n] = low[n * 4 : (n + 1) * 4]
    for copy in then[3:]:
        copy.wait_recv()
    high = (s2b[x] + b2[1]) + (b2[2] + b2[3])
    for n in range(4):
        s3[4 + n] = high[n * 4 : (n + 1) * 4]
    third = []
    for d in (4, 3, 5, 2, 6, 1, 7):
        to, peer = z_peer(d)
        third.append(send(s3.at[to], r3.at[d], zs.at[d], zr.at[d], peer))
    for copy in third:
        copy.wait_recv()
    total = s3[z]
    for d in range(1, 8):
        total = total + r3[d]
    data[...] = total[:, :256]
    weight[...] = total[:, 256:]
    for copy in sends + to_near + last + done + then + third:
        copy.wait_send()


def local(ref_map, images, ctf_table, ctf_class, block_index, interp_kind, interp_bank):
    blk = jnp.transpose(block_index, (0, 2, 3, 1)).reshape(32, TAPS, CAND)
    kind = jnp.transpose(interp_kind, (0, 2, 3, 1)).reshape(32, TAPS, CAND)
    dma = pltpu.SemaphoreType.DMA
    i32 = jnp.int32
    return pl.pallas_call(
        refine_kernel,
        out_shape=[
            jax.ShapeDtypeStruct((4, 256), F32),
            jax.ShapeDtypeStruct((4, 128), F32),
            jax.ShapeDtypeStruct((2, CAND), F32),
        ],
        in_specs=[pl.BlockSpec(memory_space=pltpu.HBM)] * 9,
        out_specs=[pl.BlockSpec(memory_space=VMEM)] * 3,
        scratch_shapes=[
            VMEM((2, 2, 2048), BF16),
            VMEM((64, 2048), BF16),
            pltpu.SMEM((2,), i32),
            VMEM((32, TAPS, CAND), i32),
            VMEM((32, TAPS, CAND), i32),
            VMEM((KINDS, BW, BW), BF16),
            VMEM((1024, 128), BF16),
            VMEM((1024, 512), BF16),
            dma((10,)),
            VMEM((8, BW, 2 * BW), BF16),
            VMEM((2 * BW, BW), F32),
            VMEM((2 * KINDS * NBLK, BW), F32),
            VMEM((96, BW), F32),
            VMEM((3, 256, BW), F32),
            VMEM((64, 128), i32),
            pltpu.SMEM((64, 128), i32),
            VMEM((32, 64, 256), BF16),
            VMEM((32, 128, 256), BF16),
            VMEM((2 * CAND * PB, BW), F32),
            VMEM((CAND, 4096), BF16),
            VMEM((256, NBLK), F32),
            dma((8,)), dma((8,)), dma((8,)), dma((8,)),
            VMEM((4, 4, 32, 384), F32),
            VMEM((4, 4, 32, 384), F32),
            VMEM((4, 4, 32, 384), F32),
            VMEM((4, 4, 16, 384), F32),
            VMEM((4, 4, 16, 384), F32),
            VMEM((4, 16, 384), F32),
            VMEM((4, 16, 384), F32),
            VMEM((4, 16, 384), F32),
            VMEM((4, 16, 384), F32),
            VMEM((8, 4, 384), F32),
            VMEM((8, 4, 384), F32),
            dma((4,)), dma((4,)), dma((4,)), dma((4,)), dma((4,)), dma((4,)),
            dma((4,)), dma((4,)), dma((4,)), dma((4,)), dma((8,)), dma((8,)),
            pltpu.SemaphoreType.REGULAR((3, 2)),
        ],
        compiler_params=pltpu.CompilerParams(
            collective_id=0, has_side_effects=True, vmem_limit_bytes=56 * 1024 * 1024
        ),
        name="refine",
    )(
        ref_map, images, ctf_table, ctf_class, blk, kind, interp_bank,
        jnp.asarray(line_table(), BF16), jnp.asarray(across_table(), BF16),
    )


def solution(mesh):
    in_specs = (
        P("slab", None),
        P(("particle", "slab"), None, None),
        P(),
        P(("particle", "slab")),
        P(("particle", "slab"), None, None, None),
        P(("particle", "slab"), None, None, None),
        P(),
    )
    out_specs = (
        P(("particle", "slab"), None),
        P(("particle", "slab"), None),
        P(("particle", "slab"), None),
    )
    return jax.shard_map(local, mesh=mesh, in_specs=in_specs, out_specs=out_specs, check_vma=False)
```

```python
import jax
import jax.numpy as jnp
import numpy as np
from jax import lax
from jax.experimental import pallas as pl
from jax.experimental.pallas import tpu as pltpu
from jax.sharding import PartitionSpec as P

LINE = 256
PLINES = 8
SIDE = 32
BW = 128
TAPS = 4
KINDS = 8
CAND = 64
PB = 16
NBLK = 1024
MESH = pl.DeviceIdType.MESH
SLOTS = 4
ORDER = (1, 2, 3, 4, 5, 6, 7)
VMEM = pltpu.VMEM
F32 = jnp.float32
BF16 = jnp.bfloat16
NT = (((1,), (1,)), ((), ()))


def line_table():
    fx = np.arange(LINE) - LINE // 2
    sx = np.arange(SIDE) - SIDE // 2
    ang = 2.0 * np.pi / LINE * ((fx[:, None] * sx[None, :]) % LINE)
    cos, sin = np.cos(ang), np.sin(ang)
    one = np.zeros((2, 2, BW, 2, SIDE))
    one[:, 0, :, 0] = cos.reshape(2, BW, SIDE)
    one[:, 1, :, 0] = -sin.reshape(2, BW, SIDE)
    one[:, 0, :, 1] = sin.reshape(2, BW, SIDE)
    one[:, 1, :, 1] = cos.reshape(2, BW, SIDE)
    both = np.zeros((2, 2, 2, BW, 2, 2, SIDE))
    both[0, :, :, :, 0] = one
    both[1, :, :, :, 1] = one
    return both.reshape(8 * BW, 4 * SIDE)


def across_table():
    fy = np.arange(PLINES) - PLINES // 2
    sy = np.arange(SIDE) - SIDE // 2
    ang = 2.0 * np.pi / LINE * ((fy[None, :] * sy[:, None]) % LINE)
    full = np.zeros((SIDE, SIDE, PLINES, 2, SIDE))
    for s in range(SIDE):
        full[:, s, :, 0, s] = np.cos(ang)
        full[:, s, :, 1, s] = -np.sin(ang)
    return full.reshape(SIDE * SIDE, PLINES * 2 * SIDE)


def split(v):
    hi = v.astype(BF16)
    return hi, (v - hi.astype(F32)).astype(BF16)


def refine_kernel(
    piece, img_h, ctf_h, cls_h, blk_h, kind_h, bank_h, fx_h, fy_h,
    data, weight, post_out,
    img, ctf, cls, blk, kind, bank, fx, fy, own_sem,
    full, inter, table, parts, rows, rid_v, rids, rid_s, left, right,
    proj, cross, hist, gather_s, gather_r, forward_s, forward_r,
    sums, near, s1, a1, b1, s2a, s2b, a2, b2, s3, r3,
    near_s, near_r, xs, xr, ys, yr, x2s, x2r, y2s, y2r, zs, zr, here,
):
    p = lax.axis_index("particle")
    s = lax.axis_index("slab")
    z, x_lo, core = p // 4, lax.rem(p // 2, 2), lax.rem(p, 2)
    x_hi, y = s // 4, lax.rem(s, 4)
    x = x_hi * 2 + x_lo

    sibling = (p + 1 - 2 * core, s)

    def x_peer(d):
        to = lax.rem(x + d, 4)
        return to, (p + (lax.rem(to, 2) - x_lo) * 2, s + (to // 2 - x_hi) * 4)

    def y_peer(d):
        to = lax.rem(y + d, 4)
        return to, (p, s + to - y)

    def z_peer(d):
        to = lax.rem(z + d, 8)
        return to, (p + (to - z) * 4, s)

    def map_peer(n, sign):
        flip = lax.rem(n, 2)
        to = lax.rem(y + 4 + sign * (n // 2), 4)
        return (p + flip * (2 - 4 * x_lo), (x_hi + flip * (1 - 2 * x_hi)) * 4 + to)

    def send(src, dst, ssem, rsem, peer):
        copy = pltpu.make_async_remote_copy(
            src_ref=src, dst_ref=dst, send_sem=ssem, recv_sem=rsem, device_id=peer, device_id_type=MESH
        )
        copy.start()
        return copy

    peers = [sibling] + [x_peer(d)[1] for d in (1, 2, 3)] + [z_peer(d)[1] for d in (1, 7)]
    peers += [map_peer(n, 1) for n in range(1, 8)]
    barrier = pltpu.get_barrier_semaphore()
    for peer in peers:
        pl.semaphore_signal(barrier, inc=1, device_id=peer, device_id_type=MESH)
    pairs = [
        (blk_h, blk), (kind_h, kind), (img_h, img), (ctf_h, ctf), (cls_h, cls), (bank_h, bank),
        (piece, full.at[s]), (fx_h, fx), (fy_h, fy),
    ]
    loads = [pltpu.make_async_copy(a, b, own_sem.at[n]) for n, (a, b) in enumerate(pairs)]
    for load in loads:
        load.start()
    pl.semaphore_wait(barrier, len(peers))
    half = pl.ds(pl.multiple_of(core * 64, 64), 64)
    sends = []
    for n in ORDER:
        sends.append(send(piece.at[half], full.at[s, half], gather_s.at[n], gather_r.at[n], map_peer(n, 1)))

    def tell(n):
        for side, d in enumerate((1, 7)):
            pl.semaphore_signal(here.at[n, side], inc=1, device_id=z_peer(d)[1], device_id_type=MESH)

    def hear(n):
        for side in range(2):
            pl.semaphore_wait(here.at[n, side], 1)

    tell(0)

    loads[0].wait()
    loads[1].wait()
    number = kind[...] * NBLK + blk[...]
    for h in range(2):
        pair = jnp.concatenate([number[:, 2 * h, :], number[:, 2 * h + 1, :]], axis=1)
        rid_v[:, h, :] = pair * 2

    def fetch(u, ip):
        return pltpu.make_async_copy(rid_v.at[ip], rids[u], rid_s.at[u])

    for u in range(SLOTS):
        fetch(u, u).start()

    for load in loads[2:6]:
        load.wait()
    lanes = lax.broadcasted_iota(jnp.int32, (16, 64), 1)
    which = lax.broadcasted_iota(jnp.int32, (16, 64), 0)
    pick = jnp.where(which == 0, cls[0], cls[1])
    onehot = (lanes == pick).astype(F32).astype(BF16)
    gain = jnp.dot(onehot, ctf[...], preferred_element_type=F32)
    pixel = img[...].astype(F32)
    for i in range(2):
        g = gain[i : i + 1]
        for c, row in enumerate((g * pixel[i, 0:1], g * pixel[i, 1:2], g * g)):
            for b in range(PB):
                parts[pl.ds(c * 32 + i * PB + b, 1), :] = row[:, b * BW : (b + 1) * BW]
    both = jnp.concatenate(split(parts[...]), axis=0)
    for k in range(KINDS):
        turned = lax.dot_general(both, bank[k], NT, preferred_element_type=F32)
        turned = turned[:96] + turned[96:]
        for c in range(3):
            rows[c, pl.ds(k, 32, stride=KINDS), :] = turned[c * 32 : (c + 1) * 32]

    row_id = lax.broadcasted_iota(jnp.int32, (64, 128), 0)
    col_id = lax.broadcasted_iota(jnp.int32, (128, 128), 0)

    @pl.loop(0, 32)
    def _(ip):
        for h in range(2):
            v = rid_v[ip, pl.ds(h, 1), :] >> 1
            high = ((v >> 5) & 1) * 4 + ((v >> 4) & 1) * 2 + ((v >> 6) & 1)
            low = ((v >> 2) & 3) * 32 + ((v >> 7) & 7) * 4 + (v & 3)
            at = pl.ds(h * 128, 128)
            left[ip, :, at] = jnp.where(row_id == high * KINDS + (v >> 10), 1.0, 0.0).astype(BF16)
            right[ip, :, at] = jnp.where(col_id == low, 1.0, 0.0).astype(BF16)

    def map_piece(source):
        inter[pl.ds(0, BW, stride=2), :] = full[source, :, :BW].astype(F32)
        inter[pl.ds(1, BW, stride=2), :] = full[source, :, BW:].astype(F32)
        lhs = inter[...].astype(BF16)
        for k in range(0, KINDS, 2):
            mapped = jnp.dot(lhs, jnp.concatenate([bank[k], bank[k + 1]], axis=1), preferred_element_type=F32)
            for h in range(2):
                at = pl.ds(pl.multiple_of((k + h) * 2 * NBLK + source * 256, 256), 256)
                table[at, :] = mapped[:, h * BW : (h + 1) * BW].astype(BF16).astype(F32)

    loads[6].wait()
    map_piece(s)

    def forward(n, rows):
        at = full.at[map_peer(n, -1)[1], rows]
        return pltpu.make_async_remote_copy(
            src_ref=at, dst_ref=at, send_sem=forward_s.at[n], recv_sem=forward_r.at[n],
            device_id=sibling, device_id_type=MESH,
        )

    other_half = pl.ds(pl.multiple_of((1 - core) * 64, 64), 64)
    def pass_on(n):
        peer = map_peer(n, -1)
        pltpu.make_async_remote_copy(
            src_ref=piece.at[half], dst_ref=full.at[peer[1], half], send_sem=gather_s.at[n],
            recv_sem=gather_r.at[n], device_id=peer, device_id_type=MESH,
        ).wait_recv()
        forward(n, half).start()

    def use(n):
        forward(n, other_half).wait_recv()
        map_piece(map_peer(n, -1)[1])

    pass_on(1)

    @pl.loop(1, 7)
    def _(n):
        pass_on(n + 1)
        use(n)

    use(7)
    for n in range(1, 8):
        forward(n, half).wait_send()

    hear(0)
    tell(1)
    loads[7].wait()
    loads[8].wait()

    @pl.loop(0, 2)
    def _(i):
        @pl.loop(0, PB // SLOTS)
        def _(g):
            for u in range(SLOTS):
                b = g * SLOTS + u
                ip = i * PB + b
                fetch(u, ip).wait()
                for j in range(CAND):
                    taken = [table[pl.ds(rids[u][h, q * CAND + j], 2), :] for h in range(2) for q in range(2)]
                    total = (taken[0] + taken[1]) + (taken[2] + taken[3])
                    proj[pl.ds(pl.multiple_of(b * 2 * CAND, 2 * CAND) + 2 * j, 2), :] = total
                fetch(u, lax.rem(ip + SLOTS, 32)).start()

        for b in range(PB):
            ca = parts[pl.ds(i * PB + b, 1), :]
            cb = parts[pl.ds(32 + i * PB + b, 1), :]
            u = proj[pl.ds(b * 2 * CAND, CAND, stride=2), :]
            w = proj[pl.ds(b * 2 * CAND + 1, CAND, stride=2), :]
            at = pl.ds(b // 4 * CAND, CAND)
            cross[at, pl.ds(b % 4 * 256, 128)] = (ca * u + cb * w).astype(BF16)
            cross[at, pl.ds(b % 4 * 256 + 128, 128)] = (cb * u - ca * w).astype(BF16)
        along = jnp.dot(cross[...], fx[...], preferred_element_type=F32)
        along = jnp.concatenate([along[g * CAND : (g + 1) * CAND] for g in range(4)], axis=1)
        both = jnp.concatenate(split(along), axis=0)
        scores = lax.dot_general(fy[...], both, NT, preferred_element_type=F32)
        scores = scores[:, :CAND] + scores[:, CAND:]
        energy = jnp.sum(scores * scores, axis=0, keepdims=True) * (1.0 / (SIDE * SIDE))
        post_out[pl.ds(i, 1), :] = CAND * energy / (jnp.sum(energy, axis=1, keepdims=True) + 1e-6)

    for u in range(SLOTS):
        fetch(u, u).wait()
    hear(1)
    tell(2)

    def histogram(i, b, w_hi, w_lo):
        ip = i * PB + b
        hit = left[ip]
        hits = jnp.concatenate([hit * w_hi, hit * w_lo], axis=0)
        both = lax.dot_general(hits, right[ip], NT, preferred_element_type=F32)
        both = both[:64] + both[64:]
        at = pl.ds(pl.multiple_of(ip * KINDS, KINDS), KINDS)
        for h in range(8):
            hist[at, pl.ds(h * 128, 128)] = both[h * 8 : (h + 1) * 8]

    for i in range(2):
        post = post_out[pl.ds(i, 1), :]
        pair = split(jnp.concatenate([post, post, post, post], axis=1))

        @pl.loop(0, PB, unroll=8)
        def _(b):
            histogram(i, b, *pair)

    d_hi, d_lo = split(jnp.concatenate([rows[c] for c in range(3)], axis=1))
    d_both = jnp.concatenate([d_hi, d_lo], axis=1)

    def map_sums(of_core, to):
        start = pl.multiple_of((of_core * 4 + to) * 128, 128)
        h_hi, h_lo = split(hist[:, pl.ds(start, 128)].T)
        got = jnp.dot(h_hi, d_both, preferred_element_type=F32)
        got = got[:, :384] + got[:, 384:] + jnp.dot(h_lo, d_hi, preferred_element_type=F32)
        return got.reshape(4, 32, 384)

    order = (2, 1, 3, 0)
    to_near = []
    for n, d in enumerate(order):
        to = lax.rem(x + d, 4)
        sums[to] = map_sums(1 - core, to)
        to_near.append(send(sums.at[to], near.at[to], near_s.at[n], near_r.at[n], sibling))
    last = []
    for n, d in enumerate(order):
        to, peer = x_peer(d)
        mine = map_sums(core, to)
        to_near[n].wait_recv()
        s1[to] = mine + near[to]
        if d:
            last.append(send(s1.at[to, :, pl.ds(0, 16)], a1.at[d], xs.at[d], xr.at[d], peer))
    done = []
    for d in (2, 1, 3):
        to, peer = y_peer(d)
        done.append(send(s1.at[:, to, pl.ds(16, 16)], b1.at[d], ys.at[d], yr.at[d], peer))
    for copy in last:
        copy.wait_recv()
    s2a[...] = (s1[x, :, 0:16, :] + a1[1]) + (a1[2] + a1[3])
    then = []
    for d in (2, 1, 3):
        to, peer = y_peer(d)
        then.append(send(s2a.at[to], a2.at[d], y2s.at[d], y2r.at[d], peer))
    for copy in done:
        copy.wait_recv()
    s2b[...] = (s1[:, y, 16:32, :] + b1[1]) + (b1[2] + b1[3])
    for d in (2, 1, 3):
        to, peer = x_peer(d)
        then.append(send(s2b.at[to], b2.at[d], x2s.at[d], x2r.at[d], peer))
    for copy in then[:3]:
        copy.wait_recv()
    low = (s2a[y] + a2[1]) + (a2[2] + a2[3])
    for n in range(4):
        s3[n] = low[n * 4 : (n + 1) * 4]
    for copy in then[3:]:
        copy.wait_recv()
    high = (s2b[x] + b2[1]) + (b2[2] + b2[3])
    for n in range(4):
        s3[4 + n] = high[n * 4 : (n + 1) * 4]
    hear(2)
    third = []
    for d in (4, 3, 5, 2, 6, 1, 7):
        to, peer = z_peer(d)
        third.append(send(s3.at[to], r3.at[d], zs.at[d], zr.at[d], peer))
    for copy in third:
        copy.wait_recv()
    total = s3[z]
    for d in range(1, 8):
        total = total + r3[d]
    data[...] = total[:, :256]
    weight[...] = total[:, 256:]
    for copy in sends + to_near + last + done + then + third:
        copy.wait_send()


def local(ref_map, images, ctf_table, ctf_class, block_index, interp_kind, interp_bank):
    blk = jnp.transpose(block_index, (0, 2, 3, 1)).reshape(32, TAPS, CAND)
    kind = jnp.transpose(interp_kind, (0, 2, 3, 1)).reshape(32, TAPS, CAND)
    dma = pltpu.SemaphoreType.DMA
    i32 = jnp.int32
    return pl.pallas_call(
        refine_kernel,
        out_shape=[
            jax.ShapeDtypeStruct((4, 256), F32),
            jax.ShapeDtypeStruct((4, 128), F32),
            jax.ShapeDtypeStruct((2, CAND), F32),
        ],
        in_specs=[pl.BlockSpec(memory_space=pltpu.HBM)] * 9,
        out_specs=[pl.BlockSpec(memory_space=VMEM)] * 3,
        scratch_shapes=[
            VMEM((2, 2, 2048), BF16),
            VMEM((64, 2048), BF16),
            pltpu.SMEM((2,), i32),
            VMEM((32, TAPS, CAND), i32),
            VMEM((32, TAPS, CAND), i32),
            VMEM((KINDS, BW, BW), BF16),
            VMEM((1024, 128), BF16),
            VMEM((1024, 512), BF16),
            dma((10,)),
            VMEM((8, BW, 2 * BW), BF16),
            VMEM((2 * BW, BW), F32),
            VMEM((2 * KINDS * NBLK, BW), F32),
            VMEM((96, BW), F32),
            VMEM((3, 256, BW), F32),
            VMEM((32, 2, 128), i32),
            [pltpu.SMEM((2, 128), i32)] * SLOTS,
            dma((SLOTS,)),
            VMEM((32, 64, 256), BF16),
            VMEM((32, 128, 256), BF16),
            VMEM((2 * CAND * PB, BW), F32),
            VMEM((4 * CAND, 1024), BF16),
            VMEM((256, NBLK), F32),
            dma((8,)), dma((8,)), dma((8,)), dma((8,)),
            VMEM((4, 4, 32, 384), F32),
            VMEM((4, 4, 32, 384), F32),
            VMEM((4, 4, 32, 384), F32),
            VMEM((4, 4, 16, 384), F32),
            VMEM((4, 4, 16, 384), F32),
            VMEM((4, 16, 384), F32),
            VMEM((4, 16, 384), F32),
            VMEM((4, 16, 384), F32),
            VMEM((4, 16, 384), F32),
            VMEM((8, 4, 384), F32),
            VMEM((8, 4, 384), F32),
            dma((4,)), dma((4,)), dma((4,)), dma((4,)), dma((4,)), dma((4,)),
            dma((4,)), dma((4,)), dma((4,)), dma((4,)), dma((8,)), dma((8,)),
            pltpu.SemaphoreType.REGULAR((3, 2)),
        ],
        compiler_params=pltpu.CompilerParams(
            collective_id=0, has_side_effects=True, vmem_limit_bytes=56 * 1024 * 1024
        ),
        name="refine",
    )(
        ref_map, images, ctf_table, ctf_class, blk, kind, interp_bank,
        jnp.asarray(line_table(), BF16), jnp.asarray(across_table(), BF16),
    )


def solution(mesh):
    in_specs = (
        P("slab", None),
        P(("particle", "slab"), None, None),
        P(),
        P(("particle", "slab")),
        P(("particle", "slab"), None, None, None),
        P(("particle", "slab"), None, None, None),
        P(),
    )
    out_specs = (
        P(("particle", "slab"), None),
        P(("particle", "slab"), None),
        P(("particle", "slab"), None),
    )
    return jax.shard_map(local, mesh=mesh, in_specs=in_specs, out_specs=out_specs, check_vma=False)
```

```python
import jax
import jax.numpy as jnp
import numpy as np
from jax import lax
from jax.experimental import pallas as pl
from jax.experimental.pallas import tpu as pltpu
from jax.sharding import PartitionSpec as P

LINE = 256
PLINES = 8
SIDE = 32
BW = 128
TAPS = 4
KINDS = 8
CAND = 64
PB = 16
NBLK = 1024
MESH = pl.DeviceIdType.MESH
SLOTS = 4
ORDER = (1, 2, 3, 4, 5, 6, 7)
VMEM = pltpu.VMEM
F32 = jnp.float32
BF16 = jnp.bfloat16
NT = (((1,), (1,)), ((), ()))


def line_table():
    fx = np.arange(LINE) - LINE // 2
    sx = np.arange(SIDE) - SIDE // 2
    ang = 2.0 * np.pi / LINE * ((fx[:, None] * sx[None, :]) % LINE)
    cos, sin = np.cos(ang), np.sin(ang)
    one = np.zeros((2, 2, BW, 2, SIDE))
    one[:, 0, :, 0] = cos.reshape(2, BW, SIDE)
    one[:, 1, :, 0] = -sin.reshape(2, BW, SIDE)
    one[:, 0, :, 1] = sin.reshape(2, BW, SIDE)
    one[:, 1, :, 1] = cos.reshape(2, BW, SIDE)
    both = np.zeros((2, 2, 2, BW, 2, 2, SIDE))
    both[0, :, :, :, 0] = one
    both[1, :, :, :, 1] = one
    return both.reshape(8 * BW, 4 * SIDE)


def across_table():
    fy = np.arange(PLINES) - PLINES // 2
    sy = np.arange(SIDE) - SIDE // 2
    ang = 2.0 * np.pi / LINE * ((fy[None, :] * sy[:, None]) % LINE)
    full = np.zeros((SIDE, SIDE, PLINES, 2, SIDE))
    for s in range(SIDE):
        full[:, s, :, 0, s] = np.cos(ang)
        full[:, s, :, 1, s] = -np.sin(ang)
    return full.reshape(SIDE * SIDE, PLINES * 2 * SIDE)


def split(v):
    hi = v.astype(BF16)
    return hi, (v - hi.astype(F32)).astype(BF16)


def refine_kernel(
    piece, img_h, ctf_h, cls_h, blk_h, kind_h, bank_h, fx_h, fy_h,
    data, weight, post_out,
    img, ctf, cls, blk, kind, bank, fx, fy, own_sem,
    full, inter, table, parts, rows, rid_v, rids, rid_s, left, right,
    proj, cross, hist, gather_s, gather_r, forward_s, forward_r,
    sums, near, s1, a1, b1, s2a, s2b, a2, b2, s3, r3,
    near_s, near_r, xs, xr, ys, yr, x2s, x2r, y2s, y2r, zs, zr, here,
):
    p = lax.axis_index("particle")
    s = lax.axis_index("slab")
    z, x_lo, core = p // 4, lax.rem(p // 2, 2), lax.rem(p, 2)
    x_hi, y = s // 4, lax.rem(s, 4)
    x = x_hi * 2 + x_lo

    sibling = (p + 1 - 2 * core, s)

    def x_peer(d):
        to = lax.rem(x + d, 4)
        return to, (p + (lax.rem(to, 2) - x_lo) * 2, s + (to // 2 - x_hi) * 4)

    def y_peer(d):
        to = lax.rem(y + d, 4)
        return to, (p, s + to - y)

    def z_peer(d):
        to = lax.rem(z + d, 8)
        return to, (p + (to - z) * 4, s)

    def map_peer(n, sign):
        flip = lax.rem(n, 2)
        to = lax.rem(y + 4 + sign * (n // 2), 4)
        return (p + flip * (2 - 4 * x_lo), (x_hi + flip * (1 - 2 * x_hi)) * 4 + to)

    def send(src, dst, ssem, rsem, peer):
        copy = pltpu.make_async_remote_copy(
            src_ref=src, dst_ref=dst, send_sem=ssem, recv_sem=rsem, device_id=peer, device_id_type=MESH
        )
        copy.start()
        return copy

    peers = [sibling] + [x_peer(d)[1] for d in (1, 2, 3)] + [z_peer(d)[1] for d in (1, 7)]
    peers += [map_peer(n, 1) for n in range(1, 8)]
    barrier = pltpu.get_barrier_semaphore()
    for peer in peers:
        pl.semaphore_signal(barrier, inc=1, device_id=peer, device_id_type=MESH)
    pairs = [
        (blk_h, blk), (kind_h, kind), (img_h, img), (ctf_h, ctf), (cls_h, cls), (bank_h, bank),
        (piece, full.at[s]), (fx_h, fx), (fy_h, fy),
    ]
    loads = [pltpu.make_async_copy(a, b, own_sem.at[n]) for n, (a, b) in enumerate(pairs)]
    for load in loads:
        load.start()
    pl.semaphore_wait(barrier, len(peers))
    half = pl.ds(pl.multiple_of(core * 64, 64), 64)
    sends = []
    for n in ORDER:
        sends.append(send(piece.at[half], full.at[s, half], gather_s.at[n], gather_r.at[n], map_peer(n, 1)))

    def tell(n):
        for side, d in enumerate((1, 7)):
            pl.semaphore_signal(here.at[n, side], inc=1, device_id=z_peer(d)[1], device_id_type=MESH)

    def hear(n):
        for side in range(2):
            pl.semaphore_wait(here.at[n, side], 1)

    tell(0)

    loads[0].wait()
    loads[1].wait()
    number = kind[...] * NBLK + blk[...]
    for h in range(2):
        pair = jnp.concatenate([number[:, 2 * h, :], number[:, 2 * h + 1, :]], axis=1)
        rid_v[:, h, :] = pair * 2

    def fetch(u, two):
        return pltpu.make_async_copy(rid_v.at[pl.ds(two * 2, 2)], rids[u], rid_s.at[u])

    for u in range(SLOTS):
        fetch(u, u).start()

    for load in loads[2:6]:
        load.wait()
    lanes = lax.broadcasted_iota(jnp.int32, (16, 64), 1)
    which = lax.broadcasted_iota(jnp.int32, (16, 64), 0)
    pick = jnp.where(which == 0, cls[0], cls[1])
    onehot = (lanes == pick).astype(F32).astype(BF16)
    gain = jnp.dot(onehot, ctf[...], preferred_element_type=F32)
    pixel = img[...].astype(F32)
    for i in range(2):
        g = gain[i : i + 1]
        for c, row in enumerate((g * pixel[i, 0:1], g * pixel[i, 1:2], g * g)):
            for b in range(PB):
                parts[pl.ds(c * 32 + i * PB + b, 1), :] = row[:, b * BW : (b + 1) * BW]
    both = jnp.concatenate(split(parts[...]), axis=0)
    for k in range(KINDS):
        turned = lax.dot_general(both, bank[k], NT, preferred_element_type=F32)
        turned = turned[:96] + turned[96:]
        for c in range(3):
            rows[c, pl.ds(k, 32, stride=KINDS), :] = turned[c * 32 : (c + 1) * 32]

    row_id = lax.broadcasted_iota(jnp.int32, (64, 128), 0)
    col_id = lax.broadcasted_iota(jnp.int32, (128, 128), 0)

    @pl.loop(0, 32)
    def _(ip):
        for h in range(2):
            v = rid_v[ip, pl.ds(h, 1), :] >> 1
            high = ((v >> 5) & 1) * 4 + ((v >> 4) & 1) * 2 + ((v >> 6) & 1)
            low = ((v >> 2) & 3) * 32 + ((v >> 7) & 7) * 4 + (v & 3)
            at = pl.ds(h * 128, 128)
            left[ip, :, at] = jnp.where(row_id == high * KINDS + (v >> 10), 1.0, 0.0).astype(BF16)
            right[ip, :, at] = jnp.where(col_id == low, 1.0, 0.0).astype(BF16)

    def map_piece(source):
        inter[pl.ds(0, BW, stride=2), :] = full[source, :, :BW].astype(F32)
        inter[pl.ds(1, BW, stride=2), :] = full[source, :, BW:].astype(F32)
        lhs = inter[...].astype(BF16)
        for k in range(0, KINDS, 2):
            mapped = jnp.dot(lhs, jnp.concatenate([bank[k], bank[k + 1]], axis=1), preferred_element_type=F32)
            for h in range(2):
                at = pl.ds(pl.multiple_of((k + h) * 2 * NBLK + source * 256, 256), 256)
                table[at, :] = mapped[:, h * BW : (h + 1) * BW].astype(BF16).astype(F32)

    loads[6].wait()
    map_piece(s)

    def forward(n, rows):
        at = full.at[map_peer(n, -1)[1], rows]
        return pltpu.make_async_remote_copy(
            src_ref=at, dst_ref=at, send_sem=forward_s.at[n], recv_sem=forward_r.at[n],
            device_id=sibling, device_id_type=MESH,
        )

    other_half = pl.ds(pl.multiple_of((1 - core) * 64, 64), 64)
    def pass_on(n):
        peer = map_peer(n, -1)
        pltpu.make_async_remote_copy(
            src_ref=piece.at[half], dst_ref=full.at[peer[1], half], send_sem=gather_s.at[n],
            recv_sem=gather_r.at[n], device_id=peer, device_id_type=MESH,
        ).wait_recv()
        forward(n, half).start()

    def use(n):
        forward(n, other_half).wait_recv()
        map_piece(map_peer(n, -1)[1])

    pass_on(1)

    @pl.loop(1, 7)
    def _(n):
        pass_on(n + 1)
        use(n)

    use(7)
    for n in range(1, 8):
        forward(n, half).wait_send()

    hear(0)
    tell(1)
    loads[7].wait()
    loads[8].wait()

    @pl.loop(0, 16 // SLOTS)
    def _(step):
        for u in range(SLOTS):
            two = step * SLOTS + u
            i = two // 8
            fetch(u, two).wait()
            for v in range(2):
                start = (u * 2 + v) * 2 * CAND
                for j in range(CAND):
                    taken = [table[pl.ds(rids[u][v, h, q * CAND + j], 2), :] for h in range(2) for q in range(2)]
                    proj[pl.ds(start + 2 * j, 2), :] = (taken[0] + taken[1]) + (taken[2] + taken[3])
                ca = parts[pl.ds(two * 2 + v, 1), :]
                cb = parts[pl.ds(32 + two * 2 + v, 1), :]
                re = proj[pl.ds(start, CAND, stride=2), :]
                im = proj[pl.ds(start + 1, CAND, stride=2), :]
                group = lax.rem(two, 8) // 2
                at = pl.ds(pl.multiple_of(group * 2 * CAND + i * CAND, CAND), CAND)
                lane = ((u % 2) * 2 + v) * 256
                cross[at, pl.ds(lane, 128)] = (ca * re + cb * im).astype(BF16)
                cross[at, pl.ds(lane + 128, 128)] = (cb * re - ca * im).astype(BF16)
            fetch(u, lax.rem(two + SLOTS, 16)).start()

    along = jnp.dot(cross[...], fx[...], preferred_element_type=F32)
    along = jnp.concatenate([along[g * 2 * CAND : (g + 1) * 2 * CAND] for g in range(4)], axis=1)
    both = jnp.concatenate(split(along), axis=0)
    squares = jnp.zeros((8, 2 * CAND), F32)
    for n in range(8):
        scores = lax.dot_general(fy[n * 128 : (n + 1) * 128, :], both, NT, preferred_element_type=F32)
        scores = scores[:, : 2 * CAND] + scores[:, 2 * CAND :]
        squares = squares + jnp.sum((scores * scores).reshape(16, 8, 2 * CAND), axis=0)
    energy = jnp.sum(squares, axis=0, keepdims=True) * (1.0 / (SIDE * SIDE))
    lane_id = lax.broadcasted_iota(jnp.int32, (1, 2 * CAND), 1)
    first = lane_id < CAND
    sum0 = jnp.sum(jnp.where(first, energy, 0.0), axis=1, keepdims=True)
    sum1 = jnp.sum(jnp.where(first, 0.0, energy), axis=1, keepdims=True)
    post = CAND * energy / (jnp.where(first, sum0, sum1) + 1e-6)
    turned = jnp.concatenate([post[:, CAND:], post[:, :CAND]], axis=1)
    post_out[0:1, :] = post[:, :CAND]
    post_out[1:2, :] = turned[:, :CAND]
    weights = (jnp.where(first, post, turned), jnp.where(first, turned, post))

    for u in range(SLOTS):
        fetch(u, u).wait()
    hear(1)
    tell(2)

    def histogram(i, b, w_hi, w_lo):
        ip = i * PB + b
        hit = left[ip]
        hits = jnp.concatenate([hit * w_hi, hit * w_lo], axis=0)
        both = lax.dot_general(hits, right[ip], NT, preferred_element_type=F32)
        both = both[:64] + both[64:]
        at = pl.ds(pl.multiple_of(ip * KINDS, KINDS), KINDS)
        for h in range(8):
            hist[at, pl.ds(h * 128, 128)] = both[h * 8 : (h + 1) * 8]

    for i in range(2):
        pair = split(jnp.concatenate([weights[i], weights[i]], axis=1))

        @pl.loop(0, PB, unroll=8)
        def _(b):
            histogram(i, b, *pair)

    d_hi, d_lo = split(jnp.concatenate([rows[c] for c in range(3)], axis=1))
    d_both = jnp.concatenate([d_hi, d_lo], axis=1)

    def map_sums(of_core, to):
        start = pl.multiple_of((of_core * 4 + to) * 128, 128)
        h_hi, h_lo = split(hist[:, pl.ds(start, 128)].T)
        got = jnp.dot(h_hi, d_both, preferred_element_type=F32)
        got = got[:, :384] + got[:, 384:] + jnp.dot(h_lo, d_hi, preferred_element_type=F32)
        return got.reshape(4, 32, 384)

    order = (2, 1, 3, 0)
    to_near = []
    for n, d in enumerate(order):
        to = lax.rem(x + d, 4)
        sums[to] = map_sums(1 - core, to)
        to_near.append(send(sums.at[to], near.at[to], near_s.at[n], near_r.at[n], sibling))
    last = []
    for n, d in enumerate(order):
        to, peer = x_peer(d)
        mine = map_sums(core, to)
        to_near[n].wait_recv()
        s1[to] = mine + near[to]
        if d:
            last.append(send(s1.at[to, :, pl.ds(0, 16)], a1.at[d], xs.at[d], xr.at[d], peer))
    done = []
    for d in (2, 1, 3):
        to, peer = y_peer(d)
        done.append(send(s1.at[:, to, pl.ds(16, 16)], b1.at[d], ys.at[d], yr.at[d], peer))
    for copy in last:
        copy.wait_recv()
    s2a[...] = (s1[x, :, 0:16, :] + a1[1]) + (a1[2] + a1[3])
    then = []
    for d in (2, 1, 3):
        to, peer = y_peer(d)
        then.append(send(s2a.at[to], a2.at[d], y2s.at[d], y2r.at[d], peer))
    for copy in done:
        copy.wait_recv()
    s2b[...] = (s1[:, y, 16:32, :] + b1[1]) + (b1[2] + b1[3])
    for d in (2, 1, 3):
        to, peer = x_peer(d)
        then.append(send(s2b.at[to], b2.at[d], x2s.at[d], x2r.at[d], peer))
    for copy in then[:3]:
        copy.wait_recv()
    low = (s2a[y] + a2[1]) + (a2[2] + a2[3])
    for n in range(4):
        s3[n] = low[n * 4 : (n + 1) * 4]
    for copy in then[3:]:
        copy.wait_recv()
    high = (s2b[x] + b2[1]) + (b2[2] + b2[3])
    for n in range(4):
        s3[4 + n] = high[n * 4 : (n + 1) * 4]
    hear(2)
    third = []
    for d in (4, 3, 5, 2, 6, 1, 7):
        to, peer = z_peer(d)
        third.append(send(s3.at[to], r3.at[d], zs.at[d], zr.at[d], peer))
    for copy in third:
        copy.wait_recv()
    total = s3[z]
    for d in range(1, 8):
        total = total + r3[d]
    data[...] = total[:, :256]
    weight[...] = total[:, 256:]
    for copy in sends + to_near + last + done + then + third:
        copy.wait_send()


def local(ref_map, images, ctf_table, ctf_class, block_index, interp_kind, interp_bank):
    blk = jnp.transpose(block_index, (0, 2, 3, 1)).reshape(32, TAPS, CAND)
    kind = jnp.transpose(interp_kind, (0, 2, 3, 1)).reshape(32, TAPS, CAND)
    dma = pltpu.SemaphoreType.DMA
    i32 = jnp.int32
    return pl.pallas_call(
        refine_kernel,
        out_shape=[
            jax.ShapeDtypeStruct((4, 256), F32),
            jax.ShapeDtypeStruct((4, 128), F32),
            jax.ShapeDtypeStruct((2, CAND), F32),
        ],
        in_specs=[pl.BlockSpec(memory_space=pltpu.HBM)] * 9,
        out_specs=[pl.BlockSpec(memory_space=VMEM)] * 3,
        scratch_shapes=[
            VMEM((2, 2, 2048), BF16),
            VMEM((64, 2048), BF16),
            pltpu.SMEM((2,), i32),
            VMEM((32, TAPS, CAND), i32),
            VMEM((32, TAPS, CAND), i32),
            VMEM((KINDS, BW, BW), BF16),
            VMEM((1024, 128), BF16),
            VMEM((1024, 512), BF16),
            dma((10,)),
            VMEM((8, BW, 2 * BW), BF16),
            VMEM((2 * BW, BW), F32),
            VMEM((2 * KINDS * NBLK, BW), F32),
            VMEM((96, BW), F32),
            VMEM((3, 256, BW), F32),
            VMEM((32, 2, 128), i32),
            [pltpu.SMEM((2, 2, 128), i32)] * SLOTS,
            dma((SLOTS,)),
            VMEM((32, 64, 256), BF16),
            VMEM((32, 128, 256), BF16),
            VMEM((SLOTS * 4 * CAND, BW), F32),
            VMEM((8 * CAND, 1024), BF16),
            VMEM((256, NBLK), F32),
            dma((8,)), dma((8,)), dma((8,)), dma((8,)),
            VMEM((4, 4, 32, 384), F32),
            VMEM((4, 4, 32, 384), F32),
            VMEM((4, 4, 32, 384), F32),
            VMEM((4, 4, 16, 384), F32),
            VMEM((4, 4, 16, 384), F32),
            VMEM((4, 16, 384), F32),
            VMEM((4, 16, 384), F32),
            VMEM((4, 16, 384), F32),
            VMEM((4, 16, 384), F32),
            VMEM((8, 4, 384), F32),
            VMEM((8, 4, 384), F32),
            dma((4,)), dma((4,)), dma((4,)), dma((4,)), dma((4,)), dma((4,)),
            dma((4,)), dma((4,)), dma((4,)), dma((4,)), dma((8,)), dma((8,)),
            pltpu.SemaphoreType.REGULAR((3, 2)),
        ],
        compiler_params=pltpu.CompilerParams(
            collective_id=0, has_side_effects=True, vmem_limit_bytes=56 * 1024 * 1024
        ),
        name="refine",
    )(
        ref_map, images, ctf_table, ctf_class, blk, kind, interp_bank,
        jnp.asarray(line_table(), BF16), jnp.asarray(across_table(), BF16),
    )


def solution(mesh):
    in_specs = (
        P("slab", None),
        P(("particle", "slab"), None, None),
        P(),
        P(("particle", "slab")),
        P(("particle", "slab"), None, None, None),
        P(("particle", "slab"), None, None, None),
        P(),
    )
    out_specs = (
        P(("particle", "slab"), None),
        P(("particle", "slab"), None),
        P(("particle", "slab"), None),
    )
    return jax.shard_map(local, mesh=mesh, in_specs=in_specs, out_specs=out_specs, check_vma=False)
```

```python
import math

import jax
import jax.numpy as jnp
import numpy as np
from jax import lax
from jax.experimental import pallas as pl
from jax.experimental.pallas import tpu as pltpu
from jax.sharding import PartitionSpec as P

LINE = 256
PLINES = 8
SIDE = 32
BW = 128
TAPS = 4
KINDS = 8
CAND = 64
PB = 16
NBLK = 1024
MESH = pl.DeviceIdType.MESH
SLOTS = 4
FLOOR = -34
STEPS = 585
ORDER = (1, 2, 3, 4, 5, 6, 7)
VMEM = pltpu.VMEM
F32 = jnp.float32
BF16 = jnp.bfloat16
NT = (((1,), (1,)), ((), ()))


def line_table():
    fx = np.arange(LINE) - LINE // 2
    sx = np.arange(SIDE) - SIDE // 2
    ang = 2.0 * np.pi / LINE * ((fx[:, None] * sx[None, :]) % LINE)
    cos, sin = np.cos(ang), np.sin(ang)
    one = np.zeros((2, 2, BW, 2, SIDE))
    one[:, 0, :, 0] = cos.reshape(2, BW, SIDE)
    one[:, 1, :, 0] = -sin.reshape(2, BW, SIDE)
    one[:, 0, :, 1] = sin.reshape(2, BW, SIDE)
    one[:, 1, :, 1] = cos.reshape(2, BW, SIDE)
    both = np.zeros((2, 2, 2, BW, 2, 2, SIDE))
    both[0, :, :, :, 0] = one
    both[1, :, :, :, 1] = one
    return both.reshape(8 * BW, 4 * SIDE)


def across_table():
    fy = np.arange(PLINES) - PLINES // 2
    sy = np.arange(SIDE) - SIDE // 2
    ang = 2.0 * np.pi / LINE * ((fy[None, :] * sy[:, None]) % LINE)
    full = np.zeros((SIDE, SIDE, PLINES, 2, SIDE))
    for s in range(SIDE):
        full[:, s, :, 0, s] = np.cos(ang)
        full[:, s, :, 1, s] = -np.sin(ang)
    return full.reshape(SIDE * SIDE, PLINES * 2 * SIDE)


def split(v):
    hi = v.astype(BF16)
    return hi, (v - hi.astype(F32)).astype(BF16)


def encode(v):
    size = jnp.log(jnp.maximum(jnp.abs(v), 2.0 ** (FLOOR - 1))) * (STEPS / math.log(2.0)) - FLOOR * STEPS
    size = jnp.maximum(size, 0.0) + 0.5
    return jnp.where(v < 0, -size, size).astype(jnp.int32).astype(jnp.int16)


def decode(code):
    step = code.astype(jnp.int32).astype(F32)
    size = jnp.exp(jnp.abs(step) * (math.log(2.0) / STEPS) + FLOOR * math.log(2.0))
    return jnp.where(step > 0, size, jnp.where(step < 0, -size, 0.0))


def refine_kernel(
    piece, img_h, ctf_h, cls_h, blk_h, kind_h, bank_h, fx_h, fy_h,
    data, weight, post_out,
    img, ctf, cls, blk, kind, bank, fx, fy, own_sem,
    full, inter, table, parts, rows, rid_v, rids, rid_s, left, right,
    proj, cross, hist, gather_s, gather_r, forward_s, forward_r,
    sums, near, mine, coded, coming, s3, r3,
    near_s, near_r, plane_s, plane_r, zs, zr, here,
):
    p = lax.axis_index("particle")
    s = lax.axis_index("slab")
    z, x_lo, core = p // 4, lax.rem(p // 2, 2), lax.rem(p, 2)
    x_hi, y = s // 4, lax.rem(s, 4)
    x = x_hi * 2 + x_lo

    sibling = (p + 1 - 2 * core, s)

    def x_peer(d):
        to = lax.rem(x + d, 4)
        return to, (p + (lax.rem(to, 2) - x_lo) * 2, s + (to // 2 - x_hi) * 4)

    def plane_peer(dx, dy):
        to_x, to_y = lax.rem(x + dx, 4), lax.rem(y + dy, 4)
        return to_x, to_y, (p + (lax.rem(to_x, 2) - x_lo) * 2, to_x // 2 * 4 + to_y)

    def z_peer(d):
        to = lax.rem(z + d, 8)
        return to, (p + (to - z) * 4, s)

    def map_peer(n, sign):
        flip = lax.rem(n, 2)
        to = lax.rem(y + 4 + sign * (n // 2), 4)
        return (p + flip * (2 - 4 * x_lo), (x_hi + flip * (1 - 2 * x_hi)) * 4 + to)

    def send(src, dst, ssem, rsem, peer):
        copy = pltpu.make_async_remote_copy(
            src_ref=src, dst_ref=dst, send_sem=ssem, recv_sem=rsem, device_id=peer, device_id_type=MESH
        )
        copy.start()
        return copy

    peers = [sibling] + [x_peer(d)[1] for d in (1, 2, 3)] + [z_peer(d)[1] for d in (1, 7)]
    peers += [map_peer(n, 1) for n in range(1, 8)]
    barrier = pltpu.get_barrier_semaphore()
    for peer in peers:
        pl.semaphore_signal(barrier, inc=1, device_id=peer, device_id_type=MESH)
    pairs = [
        (blk_h, blk), (kind_h, kind), (img_h, img), (ctf_h, ctf), (cls_h, cls), (bank_h, bank),
        (piece, full.at[s]), (fx_h, fx), (fy_h, fy),
    ]
    loads = [pltpu.make_async_copy(a, b, own_sem.at[n]) for n, (a, b) in enumerate(pairs)]
    for load in loads:
        load.start()
    pl.semaphore_wait(barrier, len(peers))
    half = pl.ds(pl.multiple_of(core * 64, 64), 64)
    sends = []
    for n in ORDER:
        sends.append(send(piece.at[half], full.at[s, half], gather_s.at[n], gather_r.at[n], map_peer(n, 1)))

    def tell(n):
        for side, d in enumerate((1, 7)):
            pl.semaphore_signal(here.at[n, side], inc=1, device_id=z_peer(d)[1], device_id_type=MESH)

    def hear(n):
        for side in range(2):
            pl.semaphore_wait(here.at[n, side], 1)

    tell(0)

    loads[0].wait()
    loads[1].wait()
    number = kind[...] * NBLK + blk[...]
    for h in range(2):
        pair = jnp.concatenate([number[:, 2 * h, :], number[:, 2 * h + 1, :]], axis=1)
        rid_v[:, h, :] = pair * 2

    def fetch(u, two):
        return pltpu.make_async_copy(rid_v.at[pl.ds(two * 2, 2)], rids[u], rid_s.at[u])

    for u in range(SLOTS):
        fetch(u, u).start()

    for load in loads[2:6]:
        load.wait()
    lanes = lax.broadcasted_iota(jnp.int32, (16, 64), 1)
    which = lax.broadcasted_iota(jnp.int32, (16, 64), 0)
    pick = jnp.where(which == 0, cls[0], cls[1])
    onehot = (lanes == pick).astype(F32).astype(BF16)
    gain = jnp.dot(onehot, ctf[...], preferred_element_type=F32)
    pixel = img[...].astype(F32)
    for i in range(2):
        g = gain[i : i + 1]
        for c, row in enumerate((g * pixel[i, 0:1], g * pixel[i, 1:2], g * g)):
            for b in range(PB):
                parts[pl.ds(c * 32 + i * PB + b, 1), :] = row[:, b * BW : (b + 1) * BW]
    both = jnp.concatenate(split(parts[...]), axis=0)
    for k in range(KINDS):
        turned = lax.dot_general(both, bank[k], NT, preferred_element_type=F32)
        turned = turned[:96] + turned[96:]
        for c in range(3):
            rows[c, pl.ds(k, 32, stride=KINDS), :] = turned[c * 32 : (c + 1) * 32]

    row_id = lax.broadcasted_iota(jnp.int32, (64, 128), 0)
    col_id = lax.broadcasted_iota(jnp.int32, (128, 128), 0)

    @pl.loop(0, 32)
    def _(ip):
        for h in range(2):
            v = rid_v[ip, pl.ds(h, 1), :] >> 1
            high = ((v >> 5) & 1) * 4 + ((v >> 4) & 1) * 2 + ((v >> 6) & 1)
            low = ((v >> 2) & 3) * 32 + ((v >> 7) & 7) * 4 + (v & 3)
            at = pl.ds(h * 128, 128)
            left[ip, :, at] = jnp.where(row_id == high * KINDS + (v >> 10), 1.0, 0.0).astype(BF16)
            right[ip, :, at] = jnp.where(col_id == low, 1.0, 0.0).astype(BF16)

    def map_piece(source):
        inter[pl.ds(0, BW, stride=2), :] = full[source, :, :BW].astype(F32)
        inter[pl.ds(1, BW, stride=2), :] = full[source, :, BW:].astype(F32)
        lhs = inter[...].astype(BF16)
        for k in range(0, KINDS, 2):
            mapped = jnp.dot(lhs, jnp.concatenate([bank[k], bank[k + 1]], axis=1), preferred_element_type=F32)
            for h in range(2):
                at = pl.ds(pl.multiple_of((k + h) * 2 * NBLK + source * 256, 256), 256)
                table[at, :] = mapped[:, h * BW : (h + 1) * BW].astype(BF16).astype(F32)

    loads[6].wait()
    map_piece(s)

    def forward(n, rows):
        at = full.at[map_peer(n, -1)[1], rows]
        return pltpu.make_async_remote_copy(
            src_ref=at, dst_ref=at, send_sem=forward_s.at[n], recv_sem=forward_r.at[n],
            device_id=sibling, device_id_type=MESH,
        )

    other_half = pl.ds(pl.multiple_of((1 - core) * 64, 64), 64)
    def pass_on(n):
        peer = map_peer(n, -1)
        pltpu.make_async_remote_copy(
            src_ref=piece.at[half], dst_ref=full.at[peer[1], half], send_sem=gather_s.at[n],
            recv_sem=gather_r.at[n], device_id=peer, device_id_type=MESH,
        ).wait_recv()
        forward(n, half).start()

    def use(n):
        forward(n, other_half).wait_recv()
        map_piece(map_peer(n, -1)[1])

    pass_on(1)

    @pl.loop(1, 7)
    def _(n):
        pass_on(n + 1)
        use(n)

    use(7)
    for n in range(1, 8):
        forward(n, half).wait_send()

    hear(0)
    tell(1)
    loads[7].wait()
    loads[8].wait()

    @pl.loop(0, 16 // SLOTS)
    def _(step):
        for u in range(SLOTS):
            two = step * SLOTS + u
            i = two // 8
            fetch(u, two).wait()
            for v in range(2):
                start = (u * 2 + v) * 2 * CAND
                for j in range(CAND):
                    taken = [table[pl.ds(rids[u][v, h, q * CAND + j], 2), :] for h in range(2) for q in range(2)]
                    proj[pl.ds(start + 2 * j, 2), :] = (taken[0] + taken[1]) + (taken[2] + taken[3])
                ca = parts[pl.ds(two * 2 + v, 1), :]
                cb = parts[pl.ds(32 + two * 2 + v, 1), :]
                re = proj[pl.ds(start, CAND, stride=2), :]
                im = proj[pl.ds(start + 1, CAND, stride=2), :]
                group = lax.rem(two, 8) // 2
                at = pl.ds(pl.multiple_of(group * 2 * CAND + i * CAND, CAND), CAND)
                lane = ((u % 2) * 2 + v) * 256
                cross[at, pl.ds(lane, 128)] = (ca * re + cb * im).astype(BF16)
                cross[at, pl.ds(lane + 128, 128)] = (cb * re - ca * im).astype(BF16)
            fetch(u, lax.rem(two + SLOTS, 16)).start()

    along = jnp.dot(cross[...], fx[...], preferred_element_type=F32)
    along = jnp.concatenate([along[g * 2 * CAND : (g + 1) * 2 * CAND] for g in range(4)], axis=1)
    both = jnp.concatenate(split(along), axis=0)
    squares = jnp.zeros((8, 2 * CAND), F32)
    for n in range(8):
        scores = lax.dot_general(fy[n * 128 : (n + 1) * 128, :], both, NT, preferred_element_type=F32)
        scores = scores[:, : 2 * CAND] + scores[:, 2 * CAND :]
        squares = squares + jnp.sum((scores * scores).reshape(16, 8, 2 * CAND), axis=0)
    energy = jnp.sum(squares, axis=0, keepdims=True) * (1.0 / (SIDE * SIDE))
    lane_id = lax.broadcasted_iota(jnp.int32, (1, 2 * CAND), 1)
    first = lane_id < CAND
    sum0 = jnp.sum(jnp.where(first, energy, 0.0), axis=1, keepdims=True)
    sum1 = jnp.sum(jnp.where(first, 0.0, energy), axis=1, keepdims=True)
    post = CAND * energy / (jnp.where(first, sum0, sum1) + 1e-6)
    turned = jnp.concatenate([post[:, CAND:], post[:, :CAND]], axis=1)
    post_out[0:1, :] = post[:, :CAND]
    post_out[1:2, :] = turned[:, :CAND]
    weights = (jnp.where(first, post, turned), jnp.where(first, turned, post))

    for u in range(SLOTS):
        fetch(u, u).wait()
    hear(1)
    tell(2)

    def histogram(i, b, w_hi, w_lo):
        ip = i * PB + b
        hit = left[ip]
        hits = jnp.concatenate([hit * w_hi, hit * w_lo], axis=0)
        both = lax.dot_general(hits, right[ip], NT, preferred_element_type=F32)
        both = both[:64] + both[64:]
        at = pl.ds(pl.multiple_of(ip * KINDS, KINDS), KINDS)
        for h in range(8):
            hist[at, pl.ds(h * 128, 128)] = both[h * 8 : (h + 1) * 8]

    for i in range(2):
        pair = split(jnp.concatenate([weights[i], weights[i]], axis=1))

        @pl.loop(0, PB, unroll=8)
        def _(b):
            histogram(i, b, *pair)

    d_hi, d_lo = split(jnp.concatenate([rows[c] for c in range(3)], axis=1))
    d_both = jnp.concatenate([d_hi, d_lo], axis=1)

    def map_sums(of_core, to):
        start = pl.multiple_of((of_core * 4 + to) * 128, 128)
        h_hi, h_lo = split(hist[:, pl.ds(start, 128)].T)
        got = jnp.dot(h_hi, d_both, preferred_element_type=F32)
        got = got[:, :384] + got[:, 384:] + jnp.dot(h_lo, d_hi, preferred_element_type=F32)
        return got.reshape(4, 32, 384)

    order = (2, 1, 3, 0)
    to_near = []
    for n, d in enumerate(order):
        to = lax.rem(x + d, 4)
        sums[to] = map_sums(1 - core, to)
        to_near.append(send(sums.at[to], near.at[to], near_s.at[n], near_r.at[n], sibling))
    then = []
    for n, dx in enumerate(order):
        to = lax.rem(x + dx, 4)
        total = map_sums(core, to)
        to_near[n].wait_recv()
        total = total + near[to]
        if dx == 0:
            mine[...] = total
        coded[to] = encode(total)
        for dy in (2, 1, 3, 0):
            if dx or dy:
                to_x, to_y, peer = plane_peer(dx, dy)
                at = coming.at[dx, dy]
                then.append(send(coded.at[to_x, to_y], at, plane_s.at[dx, dy], plane_r.at[dx, dy], peer))
    total = mine[y]
    at = 0
    for dx in order:
        for dy in (2, 1, 3, 0):
            if dx or dy:
                then[at].wait_recv()
                total = total + decode(coming[dx, dy])
                at += 1
    for n in range(8):
        s3[n] = total[n * 4 : (n + 1) * 4]
    hear(2)
    third = []
    for d in (4, 3, 5, 2, 6, 1, 7):
        to, peer = z_peer(d)
        third.append(send(s3.at[to], r3.at[d], zs.at[d], zr.at[d], peer))
    for copy in third:
        copy.wait_recv()
    total = s3[z]
    for d in range(1, 8):
        total = total + r3[d]
    data[...] = total[:, :256]
    weight[...] = total[:, 256:]
    for copy in sends + to_near + then + third:
        copy.wait_send()


def local(ref_map, images, ctf_table, ctf_class, block_index, interp_kind, interp_bank):
    blk = jnp.transpose(block_index, (0, 2, 3, 1)).reshape(32, TAPS, CAND)
    kind = jnp.transpose(interp_kind, (0, 2, 3, 1)).reshape(32, TAPS, CAND)
    dma = pltpu.SemaphoreType.DMA
    i32 = jnp.int32
    return pl.pallas_call(
        refine_kernel,
        out_shape=[
            jax.ShapeDtypeStruct((4, 256), F32),
            jax.ShapeDtypeStruct((4, 128), F32),
            jax.ShapeDtypeStruct((2, CAND), F32),
        ],
        in_specs=[pl.BlockSpec(memory_space=pltpu.HBM)] * 9,
        out_specs=[pl.BlockSpec(memory_space=VMEM)] * 3,
        scratch_shapes=[
            VMEM((2, 2, 2048), BF16),
            VMEM((64, 2048), BF16),
            pltpu.SMEM((2,), i32),
            VMEM((32, TAPS, CAND), i32),
            VMEM((32, TAPS, CAND), i32),
            VMEM((KINDS, BW, BW), BF16),
            VMEM((1024, 128), BF16),
            VMEM((1024, 512), BF16),
            dma((10,)),
            VMEM((8, BW, 2 * BW), BF16),
            VMEM((2 * BW, BW), F32),
            VMEM((2 * KINDS * NBLK, BW), F32),
            VMEM((96, BW), F32),
            VMEM((3, 256, BW), F32),
            VMEM((32, 2, 128), i32),
            [pltpu.SMEM((2, 2, 128), i32)] * SLOTS,
            dma((SLOTS,)),
            VMEM((32, 64, 256), BF16),
            VMEM((32, 128, 256), BF16),
            VMEM((SLOTS * 4 * CAND, BW), F32),
            VMEM((8 * CAND, 1024), BF16),
            VMEM((256, NBLK), F32),
            dma((8,)), dma((8,)), dma((8,)), dma((8,)),
            VMEM((4, 4, 32, 384), F32),
            VMEM((4, 4, 32, 384), F32),
            VMEM((4, 32, 384), F32),
            VMEM((4, 4, 32, 384), jnp.int16),
            VMEM((4, 4, 32, 384), jnp.int16),
            VMEM((8, 4, 384), F32),
            VMEM((8, 4, 384), F32),
            dma((4,)), dma((4,)), dma((4, 4)), dma((4, 4)), dma((8,)), dma((8,)),
            pltpu.SemaphoreType.REGULAR((3, 2)),
        ],
        compiler_params=pltpu.CompilerParams(
            collective_id=0, has_side_effects=True, vmem_limit_bytes=56 * 1024 * 1024
        ),
        name="refine",
    )(
        ref_map, images, ctf_table, ctf_class, blk, kind, interp_bank,
        jnp.asarray(line_table(), BF16), jnp.asarray(across_table(), BF16),
    )


def solution(mesh):
    in_specs = (
        P("slab", None),
        P(("particle", "slab"), None, None),
        P(),
        P(("particle", "slab")),
        P(("particle", "slab"), None, None, None),
        P(("particle", "slab"), None, None, None),
        P(),
    )
    out_specs = (
        P(("particle", "slab"), None),
        P(("particle", "slab"), None),
        P(("particle", "slab"), None),
    )
    return jax.shard_map(local, mesh=mesh, in_specs=in_specs, out_specs=out_specs, check_vma=False)
```

```python
import math

import jax
import jax.numpy as jnp
import numpy as np
from jax import lax
from jax.experimental import pallas as pl
from jax.experimental.pallas import tpu as pltpu
from jax.sharding import PartitionSpec as P

LINE = 256
PLINES = 8
SIDE = 32
BW = 128
TAPS = 4
KINDS = 8
CAND = 64
PB = 16
NBLK = 1024
MESH = pl.DeviceIdType.MESH
SLOTS = 4
OCTAVES = 44
STEPS = 744
LN2 = math.log(2.0)
ORDER = (1, 2, 3, 4, 5, 6, 7)
VMEM = pltpu.VMEM
F32 = jnp.float32
BF16 = jnp.bfloat16
NT = (((1,), (1,)), ((), ()))


def line_table():
    fx = np.arange(LINE) - LINE // 2
    sx = np.arange(SIDE) - SIDE // 2
    ang = 2.0 * np.pi / LINE * ((fx[:, None] * sx[None, :]) % LINE)
    cos, sin = np.cos(ang), np.sin(ang)
    one = np.zeros((2, 2, BW, 2, SIDE))
    one[:, 0, :, 0] = cos.reshape(2, BW, SIDE)
    one[:, 1, :, 0] = -sin.reshape(2, BW, SIDE)
    one[:, 0, :, 1] = sin.reshape(2, BW, SIDE)
    one[:, 1, :, 1] = cos.reshape(2, BW, SIDE)
    both = np.zeros((2, 2, 2, BW, 2, 2, SIDE))
    both[0, :, :, :, 0] = one
    both[1, :, :, :, 1] = one
    return both.reshape(8 * BW, 4 * SIDE)


def across_table():
    fy = np.arange(PLINES) - PLINES // 2
    sy = np.arange(SIDE) - SIDE // 2
    ang = 2.0 * np.pi / LINE * ((fy[None, :] * sy[:, None]) % LINE)
    full = np.zeros((SIDE, SIDE, PLINES, 2, SIDE))
    for s in range(SIDE):
        full[:, s, :, 0, s] = np.cos(ang)
        full[:, s, :, 1, s] = -np.sin(ang)
    return full.reshape(SIDE * SIDE, PLINES * 2 * SIDE)


def split(v):
    hi = v.astype(BF16)
    return hi, (v - hi.astype(F32)).astype(BF16)


def encode(v):
    size = jnp.abs(v)
    top = jnp.max(jnp.max(size, axis=0), axis=0, keepdims=True)
    base = jnp.log(jnp.maximum(top, 1e-37)) - OCTAVES * LN2
    size = (jnp.log(jnp.maximum(size, 1e-37)) - base) * (STEPS / LN2)
    size = jnp.maximum(size, 0.0) + 0.5
    return jnp.where(v < 0, -size, size).astype(jnp.int32).astype(jnp.int16), base


def decode(code, base):
    step = code.astype(jnp.int32).astype(F32)
    size = jnp.exp(jnp.abs(step) * (LN2 / STEPS) + base)
    return jnp.where(step > 0, size, jnp.where(step < 0, -size, 0.0))


def refine_kernel(
    piece, img_h, ctf_h, cls_h, blk_h, kind_h, bank_h, fx_h, fy_h,
    data, weight, post_out,
    img, ctf, cls, blk, kind, bank, fx, fy, own_sem,
    full, inter, table, parts, rows, rid_v, rids, rid_s, left, right,
    proj, cross, hist, gather_s, gather_r, forward_s, forward_r,
    sums, near, mine, coded, coming, bases, their_bases, s3, r3,
    near_s, near_r, plane_s, plane_r, base_s, base_r, zs, zr, here,
):
    p = lax.axis_index("particle")
    s = lax.axis_index("slab")
    z, x_lo, core = p // 4, lax.rem(p // 2, 2), lax.rem(p, 2)
    x_hi, y = s // 4, lax.rem(s, 4)
    x = x_hi * 2 + x_lo

    sibling = (p + 1 - 2 * core, s)

    def x_peer(d):
        to = lax.rem(x + d, 4)
        return to, (p + (lax.rem(to, 2) - x_lo) * 2, s + (to // 2 - x_hi) * 4)

    def plane_peer(dx, dy):
        to_x, to_y = lax.rem(x + dx, 4), lax.rem(y + dy, 4)
        return to_x, to_y, (p + (lax.rem(to_x, 2) - x_lo) * 2, to_x // 2 * 4 + to_y)

    def z_peer(d):
        to = lax.rem(z + d, 8)
        return to, (p + (to - z) * 4, s)

    def map_peer(n, sign):
        flip = lax.rem(n, 2)
        to = lax.rem(y + 4 + sign * (n // 2), 4)
        return (p + flip * (2 - 4 * x_lo), (x_hi + flip * (1 - 2 * x_hi)) * 4 + to)

    def send(src, dst, ssem, rsem, peer):
        copy = pltpu.make_async_remote_copy(
            src_ref=src, dst_ref=dst, send_sem=ssem, recv_sem=rsem, device_id=peer, device_id_type=MESH
        )
        copy.start()
        return copy

    peers = [sibling] + [x_peer(d)[1] for d in (1, 2, 3)] + [z_peer(d)[1] for d in (1, 7)]
    peers += [map_peer(n, 1) for n in range(1, 8)]
    barrier = pltpu.get_barrier_semaphore()
    for peer in peers:
        pl.semaphore_signal(barrier, inc=1, device_id=peer, device_id_type=MESH)
    pairs = [
        (blk_h, blk), (kind_h, kind), (img_h, img), (ctf_h, ctf), (cls_h, cls), (bank_h, bank),
        (piece, full.at[s]), (fx_h, fx), (fy_h, fy),
    ]
    loads = [pltpu.make_async_copy(a, b, own_sem.at[n]) for n, (a, b) in enumerate(pairs)]
    for load in loads:
        load.start()
    pl.semaphore_wait(barrier, len(peers))
    half = pl.ds(pl.multiple_of(core * 64, 64), 64)
    sends = []
    for n in ORDER:
        sends.append(send(piece.at[half], full.at[s, half], gather_s.at[n], gather_r.at[n], map_peer(n, 1)))

    def tell(n):
        for side, d in enumerate((1, 7)):
            pl.semaphore_signal(here.at[n, side], inc=1, device_id=z_peer(d)[1], device_id_type=MESH)

    def hear(n):
        for side in range(2):
            pl.semaphore_wait(here.at[n, side], 1)

    tell(0)

    loads[0].wait()
    loads[1].wait()
    number = kind[...] * NBLK + blk[...]
    for h in range(2):
        pair = jnp.concatenate([number[:, 2 * h, :], number[:, 2 * h + 1, :]], axis=1)
        rid_v[:, h, :] = pair * 2

    def fetch(u, two):
        return pltpu.make_async_copy(rid_v.at[pl.ds(two * 2, 2)], rids[u], rid_s.at[u])

    for u in range(SLOTS):
        fetch(u, u).start()

    for load in loads[2:6]:
        load.wait()
    lanes = lax.broadcasted_iota(jnp.int32, (16, 64), 1)
    which = lax.broadcasted_iota(jnp.int32, (16, 64), 0)
    pick = jnp.where(which == 0, cls[0], cls[1])
    onehot = (lanes == pick).astype(F32).astype(BF16)
    gain = jnp.dot(onehot, ctf[...], preferred_element_type=F32)
    pixel = img[...].astype(F32)
    for i in range(2):
        g = gain[i : i + 1]
        for c, row in enumerate((g * pixel[i, 0:1], g * pixel[i, 1:2], g * g)):
            for b in range(PB):
                parts[pl.ds(c * 32 + i * PB + b, 1), :] = row[:, b * BW : (b + 1) * BW]
    both = jnp.concatenate(split(parts[...]), axis=0)
    for k in range(KINDS):
        turned = lax.dot_general(both, bank[k], NT, preferred_element_type=F32)
        turned = turned[:96] + turned[96:]
        for c in range(3):
            rows[c, pl.ds(k, 32, stride=KINDS), :] = turned[c * 32 : (c + 1) * 32]

    row_id = lax.broadcasted_iota(jnp.int32, (64, 128), 0)
    col_id = lax.broadcasted_iota(jnp.int32, (128, 128), 0)

    @pl.loop(0, 32)
    def _(ip):
        for h in range(2):
            v = rid_v[ip, pl.ds(h, 1), :] >> 1
            high = ((v >> 5) & 1) * 4 + ((v >> 4) & 1) * 2 + ((v >> 6) & 1)
            low = ((v >> 2) & 3) * 32 + ((v >> 7) & 7) * 4 + (v & 3)
            at = pl.ds(h * 128, 128)
            left[ip, :, at] = jnp.where(row_id == high * KINDS + (v >> 10), 1.0, 0.0).astype(BF16)
            right[ip, :, at] = jnp.where(col_id == low, 1.0, 0.0).astype(BF16)

    def map_piece(source):
        inter[pl.ds(0, BW, stride=2), :] = full[source, :, :BW].astype(F32)
        inter[pl.ds(1, BW, stride=2), :] = full[source, :, BW:].astype(F32)
        lhs = inter[...].astype(BF16)
        for k in range(0, KINDS, 2):
            mapped = jnp.dot(lhs, jnp.concatenate([bank[k], bank[k + 1]], axis=1), preferred_element_type=F32)
            for h in range(2):
                at = pl.ds(pl.multiple_of((k + h) * 2 * NBLK + source * 256, 256), 256)
                table[at, :] = mapped[:, h * BW : (h + 1) * BW].astype(BF16).astype(F32)

    loads[6].wait()
    map_piece(s)

    def forward(n, rows):
        at = full.at[map_peer(n, -1)[1], rows]
        return pltpu.make_async_remote_copy(
            src_ref=at, dst_ref=at, send_sem=forward_s.at[n], recv_sem=forward_r.at[n],
            device_id=sibling, device_id_type=MESH,
        )

    other_half = pl.ds(pl.multiple_of((1 - core) * 64, 64), 64)
    def pass_on(n):
        peer = map_peer(n, -1)
        pltpu.make_async_remote_copy(
            src_ref=piece.at[half], dst_ref=full.at[peer[1], half], send_sem=gather_s.at[n],
            recv_sem=gather_r.at[n], device_id=peer, device_id_type=MESH,
        ).wait_recv()
        forward(n, half).start()

    def use(n):
        forward(n, other_half).wait_recv()
        map_piece(map_peer(n, -1)[1])

    pass_on(1)

    @pl.loop(1, 7)
    def _(n):
        pass_on(n + 1)
        use(n)

    use(7)
    for n in range(1, 8):
        forward(n, half).wait_send()

    hear(0)
    tell(1)
    loads[7].wait()
    loads[8].wait()

    @pl.loop(0, 16 // SLOTS)
    def _(step):
        for u in range(SLOTS):
            two = step * SLOTS + u
            i = two // 8
            fetch(u, two).wait()
            for v in range(2):
                start = (u * 2 + v) * 2 * CAND
                for j in range(CAND):
                    taken = [table[pl.ds(rids[u][v, h, q * CAND + j], 2), :] for h in range(2) for q in range(2)]
                    proj[pl.ds(start + 2 * j, 2), :] = (taken[0] + taken[1]) + (taken[2] + taken[3])
                ca = parts[pl.ds(two * 2 + v, 1), :]
                cb = parts[pl.ds(32 + two * 2 + v, 1), :]
                re = proj[pl.ds(start, CAND, stride=2), :]
                im = proj[pl.ds(start + 1, CAND, stride=2), :]
                group = lax.rem(two, 8) // 2
                at = pl.ds(pl.multiple_of(group * 2 * CAND + i * CAND, CAND), CAND)
                lane = ((u % 2) * 2 + v) * 256
                cross[at, pl.ds(lane, 128)] = (ca * re + cb * im).astype(BF16)
                cross[at, pl.ds(lane + 128, 128)] = (cb * re - ca * im).astype(BF16)
            fetch(u, lax.rem(two + SLOTS, 16)).start()

    along = jnp.dot(cross[...], fx[...], preferred_element_type=F32)
    along = jnp.concatenate([along[g * 2 * CAND : (g + 1) * 2 * CAND] for g in range(4)], axis=1)
    both = jnp.concatenate(split(along), axis=0)
    squares = jnp.zeros((8, 2 * CAND), F32)
    for n in range(8):
        scores = lax.dot_general(fy[n * 128 : (n + 1) * 128, :], both, NT, preferred_element_type=F32)
        scores = scores[:, : 2 * CAND] + scores[:, 2 * CAND :]
        squares = squares + jnp.sum((scores * scores).reshape(16, 8, 2 * CAND), axis=0)
    energy = jnp.sum(squares, axis=0, keepdims=True) * (1.0 / (SIDE * SIDE))
    lane_id = lax.broadcasted_iota(jnp.int32, (1, 2 * CAND), 1)
    first = lane_id < CAND
    sum0 = jnp.sum(jnp.where(first, energy, 0.0), axis=1, keepdims=True)
    sum1 = jnp.sum(jnp.where(first, 0.0, energy), axis=1, keepdims=True)
    post = CAND * energy / (jnp.where(first, sum0, sum1) + 1e-6)
    turned = jnp.concatenate([post[:, CAND:], post[:, :CAND]], axis=1)
    post_out[0:1, :] = post[:, :CAND]
    post_out[1:2, :] = turned[:, :CAND]
    weights = (jnp.where(first, post, turned), jnp.where(first, turned, post))

    for u in range(SLOTS):
        fetch(u, u).wait()
    hear(1)
    tell(2)

    def histogram(i, b, w_hi, w_lo):
        ip = i * PB + b
        hit = left[ip]
        hits = jnp.concatenate([hit * w_hi, hit * w_lo], axis=0)
        both = lax.dot_general(hits, right[ip], NT, preferred_element_type=F32)
        both = both[:64] + both[64:]
        at = pl.ds(pl.multiple_of(ip * KINDS, KINDS), KINDS)
        for h in range(8):
            hist[at, pl.ds(h * 128, 128)] = both[h * 8 : (h + 1) * 8]

    for i in range(2):
        pair = split(jnp.concatenate([weights[i], weights[i]], axis=1))

        @pl.loop(0, PB, unroll=8)
        def _(b):
            histogram(i, b, *pair)

    d_hi, d_lo = split(jnp.concatenate([rows[c] for c in range(3)], axis=1))
    d_both = jnp.concatenate([d_hi, d_lo], axis=1)

    def map_sums(of_core, to):
        start = pl.multiple_of((of_core * 4 + to) * 128, 128)
        h_hi, h_lo = split(hist[:, pl.ds(start, 128)].T)
        got = jnp.dot(h_hi, d_both, preferred_element_type=F32)
        got = got[:, :384] + got[:, 384:] + jnp.dot(h_lo, d_hi, preferred_element_type=F32)
        return got.reshape(4, 32, 384)

    order = (2, 1, 3, 0)
    to_near = []
    for n, d in enumerate(order):
        to = lax.rem(x + d, 4)
        sums[to] = map_sums(1 - core, to)
        to_near.append(send(sums.at[to], near.at[to], near_s.at[n], near_r.at[n], sibling))
    then, with_it = [], []
    for n, dx in enumerate(order):
        to = lax.rem(x + dx, 4)
        total = map_sums(core, to)
        to_near[n].wait_recv()
        total = total + near[to]
        if dx == 0:
            mine[...] = total
        coded[to], bases[to] = encode(total)
        for dy in (2, 1, 3, 0):
            if dx or dy:
                to_x, to_y, peer = plane_peer(dx, dy)
                at = their_bases.at[dx, dy]
                with_it.append(send(bases.at[to_x], at, base_s.at[dx, dy], base_r.at[dx, dy], peer))
                at = coming.at[dx, dy]
                then.append(send(coded.at[to_x, to_y], at, plane_s.at[dx, dy], plane_r.at[dx, dy], peer))
    total = mine[y]
    at = 0
    for dx in order:
        for dy in (2, 1, 3, 0):
            if dx or dy:
                with_it[at].wait_recv()
                then[at].wait_recv()
                total = total + decode(coming[dx, dy], their_bases[dx, dy])
                at += 1
    for n in range(8):
        s3[n] = total[n * 4 : (n + 1) * 4]
    hear(2)
    third = []
    for d in (4, 3, 5, 2, 6, 1, 7):
        to, peer = z_peer(d)
        third.append(send(s3.at[to], r3.at[d], zs.at[d], zr.at[d], peer))
    for copy in third:
        copy.wait_recv()
    total = s3[z]
    for d in range(1, 8):
        total = total + r3[d]
    data[...] = total[:, :256]
    weight[...] = total[:, 256:]
    for copy in sends + to_near + then + with_it + third:
        copy.wait_send()


def local(ref_map, images, ctf_table, ctf_class, block_index, interp_kind, interp_bank):
    blk = jnp.transpose(block_index, (0, 2, 3, 1)).reshape(32, TAPS, CAND)
    kind = jnp.transpose(interp_kind, (0, 2, 3, 1)).reshape(32, TAPS, CAND)
    dma = pltpu.SemaphoreType.DMA
    i32 = jnp.int32
    return pl.pallas_call(
        refine_kernel,
        out_shape=[
            jax.ShapeDtypeStruct((4, 256), F32),
            jax.ShapeDtypeStruct((4, 128), F32),
            jax.ShapeDtypeStruct((2, CAND), F32),
        ],
        in_specs=[pl.BlockSpec(memory_space=pltpu.HBM)] * 9,
        out_specs=[pl.BlockSpec(memory_space=VMEM)] * 3,
        scratch_shapes=[
            VMEM((2, 2, 2048), BF16),
            VMEM((64, 2048), BF16),
            pltpu.SMEM((2,), i32),
            VMEM((32, TAPS, CAND), i32),
            VMEM((32, TAPS, CAND), i32),
            VMEM((KINDS, BW, BW), BF16),
            VMEM((1024, 128), BF16),
            VMEM((1024, 512), BF16),
            dma((10,)),
            VMEM((8, BW, 2 * BW), BF16),
            VMEM((2 * BW, BW), F32),
            VMEM((2 * KINDS * NBLK, BW), F32),
            VMEM((96, BW), F32),
            VMEM((3, 256, BW), F32),
            VMEM((32, 2, 128), i32),
            [pltpu.SMEM((2, 2, 128), i32)] * SLOTS,
            dma((SLOTS,)),
            VMEM((32, 64, 256), BF16),
            VMEM((32, 128, 256), BF16),
            VMEM((SLOTS * 4 * CAND, BW), F32),
            VMEM((8 * CAND, 1024), BF16),
            VMEM((256, NBLK), F32),
            dma((8,)), dma((8,)), dma((8,)), dma((8,)),
            VMEM((4, 4, 32, 384), F32),
            VMEM((4, 4, 32, 384), F32),
            VMEM((4, 32, 384), F32),
            VMEM((4, 4, 32, 384), jnp.int16),
            VMEM((4, 4, 32, 384), jnp.int16),
            VMEM((4, 1, 384), F32),
            VMEM((4, 4, 1, 384), F32),
            VMEM((8, 4, 384), F32),
            VMEM((8, 4, 384), F32),
            dma((4,)), dma((4,)), dma((4, 4)), dma((4, 4)), dma((4, 4)), dma((4, 4)),
            dma((8,)), dma((8,)),
            pltpu.SemaphoreType.REGULAR((3, 2)),
        ],
        compiler_params=pltpu.CompilerParams(
            collective_id=0, has_side_effects=True, vmem_limit_bytes=56 * 1024 * 1024
        ),
        name="refine",
    )(
        ref_map, images, ctf_table, ctf_class, blk, kind, interp_bank,
        jnp.asarray(line_table(), BF16), jnp.asarray(across_table(), BF16),
    )


def solution(mesh):
    in_specs = (
        P("slab", None),
        P(("particle", "slab"), None, None),
        P(),
        P(("particle", "slab")),
        P(("particle", "slab"), None, None, None),
        P(("particle", "slab"), None, None, None),
        P(),
    )
    out_specs = (
        P(("particle", "slab"), None),
        P(("particle", "slab"), None),
        P(("particle", "slab"), None),
    )
    return jax.shard_map(local, mesh=mesh, in_specs=in_specs, out_specs=out_specs, check_vma=False)
```

```python
import math

import jax
import jax.numpy as jnp
import numpy as np
from jax import lax
from jax.experimental import pallas as pl
from jax.experimental.pallas import tpu as pltpu
from jax.sharding import PartitionSpec as P

LINE = 256
PLINES = 8
SIDE = 32
BW = 128
TAPS = 4
KINDS = 8
CAND = 64
PB = 16
NBLK = 1024
MESH = pl.DeviceIdType.MESH
SLOTS = 4
OCTAVES = 44
STEPS = 744
LN2 = math.log(2.0)
ORDER = (1, 2, 3, 4, 5, 6, 7)
VMEM = pltpu.VMEM
F32 = jnp.float32
BF16 = jnp.bfloat16
NT = (((1,), (1,)), ((), ()))


def line_table():
    fx = np.arange(LINE) - LINE // 2
    sx = np.arange(SIDE) - SIDE // 2
    ang = 2.0 * np.pi / LINE * ((fx[:, None] * sx[None, :]) % LINE)
    cos, sin = np.cos(ang), np.sin(ang)
    one = np.zeros((2, 2, BW, 2, SIDE))
    one[:, 0, :, 0] = cos.reshape(2, BW, SIDE)
    one[:, 1, :, 0] = -sin.reshape(2, BW, SIDE)
    one[:, 0, :, 1] = sin.reshape(2, BW, SIDE)
    one[:, 1, :, 1] = cos.reshape(2, BW, SIDE)
    both = np.zeros((2, 2, 2, BW, 2, 2, SIDE))
    both[0, :, :, :, 0] = one
    both[1, :, :, :, 1] = one
    return both.reshape(8 * BW, 4 * SIDE)


def across_table():
    fy = np.arange(PLINES) - PLINES // 2
    sy = np.arange(SIDE) - SIDE // 2
    ang = 2.0 * np.pi / LINE * ((fy[None, :] * sy[:, None]) % LINE)
    full = np.zeros((SIDE, SIDE, PLINES, 2, SIDE))
    for s in range(SIDE):
        full[:, s, :, 0, s] = np.cos(ang)
        full[:, s, :, 1, s] = -np.sin(ang)
    return full.reshape(SIDE * SIDE, PLINES * 2 * SIDE)


def split(v):
    hi = v.astype(BF16)
    return hi, (v - hi.astype(F32)).astype(BF16)


def encode(v):
    size = jnp.abs(v)
    top = jnp.max(jnp.max(size, axis=0), axis=0, keepdims=True)
    base = jnp.log(jnp.maximum(top, 1e-37)) - OCTAVES * LN2
    size = (jnp.log(jnp.maximum(size, 1e-37)) - base) * (STEPS / LN2)
    size = jnp.maximum(size, 0.0) + 0.5
    return jnp.where(v < 0, -size, size).astype(jnp.int32).astype(jnp.int16), base


def decode(code, base):
    step = code.astype(jnp.int32).astype(F32)
    size = jnp.exp(jnp.abs(step) * (LN2 / STEPS) + base)
    return jnp.where(step > 0, size, jnp.where(step < 0, -size, 0.0))


def refine_kernel(
    piece, img_h, ctf_h, cls_h, blk_h, kind_h, bank_h, fx_h, fy_h,
    data, weight, post_out,
    img, ctf, cls, blk, kind, bank, fx, fy, own_sem,
    full, inter, table, parts, rows, rid_v, rids, rid_s, left, right,
    proj, cross, hist, gather_s, gather_r, forward_s, forward_r,
    sums, near, mine, coded, coming, bases, their_bases, s3, r3,
    near_s, near_r, plane_s, plane_r, base_s, base_r, zs, zr, here,
):
    p = lax.axis_index("particle")
    s = lax.axis_index("slab")
    z, x_lo, core = p // 4, lax.rem(p // 2, 2), lax.rem(p, 2)
    x_hi, y = s // 4, lax.rem(s, 4)
    x = x_hi * 2 + x_lo

    sibling = (p + 1 - 2 * core, s)

    def x_peer(d):
        to = lax.rem(x + d, 4)
        return to, (p + (lax.rem(to, 2) - x_lo) * 2, s + (to // 2 - x_hi) * 4)

    def plane_peer(dx, dy):
        to_x, to_y = lax.rem(x + dx, 4), lax.rem(y + dy, 4)
        return to_x, to_y, (p + (lax.rem(to_x, 2) - x_lo) * 2, to_x // 2 * 4 + to_y)

    def z_peer(d):
        to = lax.rem(z + d, 8)
        return to, (p + (to - z) * 4, s)

    def map_peer(n, sign):
        flip = lax.rem(n, 2)
        to = lax.rem(y + 4 + sign * (n // 2), 4)
        return (p + flip * (2 - 4 * x_lo), (x_hi + flip * (1 - 2 * x_hi)) * 4 + to)

    def send(src, dst, ssem, rsem, peer):
        copy = pltpu.make_async_remote_copy(
            src_ref=src, dst_ref=dst, send_sem=ssem, recv_sem=rsem, device_id=peer, device_id_type=MESH
        )
        copy.start()
        return copy

    peers = [sibling] + [x_peer(d)[1] for d in (1, 2, 3)] + [z_peer(d)[1] for d in (1, 7)]
    peers += [map_peer(n, 1) for n in range(1, 8)]
    barrier = pltpu.get_barrier_semaphore()
    for peer in peers:
        pl.semaphore_signal(barrier, inc=1, device_id=peer, device_id_type=MESH)
    pairs = [
        (blk_h, blk), (kind_h, kind), (img_h, img), (ctf_h, ctf), (cls_h, cls), (bank_h, bank),
        (piece, full.at[s]), (fx_h, fx), (fy_h, fy),
    ]
    loads = [pltpu.make_async_copy(a, b, own_sem.at[n]) for n, (a, b) in enumerate(pairs)]
    for load in loads:
        load.start()
    pl.semaphore_wait(barrier, len(peers))
    half = pl.ds(pl.multiple_of(core * 64, 64), 64)
    sends = []
    for n in ORDER:
        sends.append(send(piece.at[half], full.at[s, half], gather_s.at[n], gather_r.at[n], map_peer(n, 1)))

    def tell(n):
        for side, d in enumerate((1, 7)):
            pl.semaphore_signal(here.at[n, side], inc=1, device_id=z_peer(d)[1], device_id_type=MESH)

    def hear(n):
        for side in range(2):
            pl.semaphore_wait(here.at[n, side], 1)

    tell(0)

    loads[0].wait()
    loads[1].wait()
    number = kind[...] * NBLK + blk[...]
    for h in range(2):
        pair = jnp.concatenate([number[:, 2 * h, :], number[:, 2 * h + 1, :]], axis=1)
        rid_v[:, h, :] = pair * 2

    def fetch(u, two):
        return pltpu.make_async_copy(rid_v.at[pl.ds(two * 2, 2)], rids[u], rid_s.at[u])

    for u in range(SLOTS):
        fetch(u, u).start()

    for load in loads[2:6]:
        load.wait()
    lanes = lax.broadcasted_iota(jnp.int32, (16, 64), 1)
    which = lax.broadcasted_iota(jnp.int32, (16, 64), 0)
    pick = jnp.where(which == 0, cls[0], cls[1])
    onehot = (lanes == pick).astype(F32).astype(BF16)
    gain = jnp.dot(onehot, ctf[...], preferred_element_type=F32)
    pixel = img[...].astype(F32)
    for i in range(2):
        g = gain[i : i + 1]
        for c, row in enumerate((g * pixel[i, 0:1], g * pixel[i, 1:2], g * g)):
            for b in range(PB):
                parts[pl.ds(c * 32 + i * PB + b, 1), :] = row[:, b * BW : (b + 1) * BW]
    both = jnp.concatenate(split(parts[...]), axis=0)
    for k in range(KINDS):
        turned = lax.dot_general(both, bank[k], NT, preferred_element_type=F32)
        turned = turned[:96] + turned[96:]
        for c in range(3):
            rows[c, pl.ds(k, 32, stride=KINDS), :] = turned[c * 32 : (c + 1) * 32]

    row_id = lax.broadcasted_iota(jnp.int32, (64, 128), 0)
    col_id = lax.broadcasted_iota(jnp.int32, (128, 128), 0)

    @pl.loop(0, 32)
    def _(ip):
        for h in range(2):
            v = rid_v[ip, pl.ds(h, 1), :] >> 1
            high = ((v >> 5) & 1) * 4 + ((v >> 4) & 1) * 2 + ((v >> 6) & 1)
            low = ((v >> 2) & 3) * 32 + ((v >> 7) & 7) * 4 + (v & 3)
            at = pl.ds(h * 128, 128)
            left[ip, :, at] = jnp.where(row_id == high * KINDS + (v >> 10), 1.0, 0.0).astype(BF16)
            right[ip, :, at] = jnp.where(col_id == low, 1.0, 0.0).astype(BF16)

    def map_piece(source):
        inter[pl.ds(0, BW, stride=2), :] = full[source, :, :BW].astype(F32)
        inter[pl.ds(1, BW, stride=2), :] = full[source, :, BW:].astype(F32)
        lhs = inter[...].astype(BF16)
        for k in range(0, KINDS, 2):
            mapped = jnp.dot(lhs, jnp.concatenate([bank[k], bank[k + 1]], axis=1), preferred_element_type=F32)
            for h in range(2):
                at = pl.ds(pl.multiple_of((k + h) * 2 * NBLK + source * 256, 256), 256)
                table[at, :] = mapped[:, h * BW : (h + 1) * BW].astype(BF16).astype(F32)

    loads[6].wait()
    map_piece(s)

    def forward(n, rows):
        at = full.at[map_peer(n, -1)[1], rows]
        return pltpu.make_async_remote_copy(
            src_ref=at, dst_ref=at, send_sem=forward_s.at[n], recv_sem=forward_r.at[n],
            device_id=sibling, device_id_type=MESH,
        )

    other_half = pl.ds(pl.multiple_of((1 - core) * 64, 64), 64)
    def pass_on(n):
        peer = map_peer(n, -1)
        pltpu.make_async_remote_copy(
            src_ref=piece.at[half], dst_ref=full.at[peer[1], half], send_sem=gather_s.at[n],
            recv_sem=gather_r.at[n], device_id=peer, device_id_type=MESH,
        ).wait_recv()
        forward(n, half).start()

    def use(n):
        forward(n, other_half).wait_recv()
        map_piece(map_peer(n, -1)[1])

    pass_on(1)

    @pl.loop(1, 7)
    def _(n):
        pass_on(n + 1)
        use(n)

    use(7)
    for n in range(1, 8):
        forward(n, half).wait_send()

    hear(0)
    tell(1)
    loads[7].wait()
    loads[8].wait()

    @pl.loop(0, 16 // SLOTS)
    def _(step):
        for u in range(SLOTS):
            two = step * SLOTS + u
            i = two // 8
            fetch(u, two).wait()
            for v in range(2):
                start = (u * 2 + v) * 2 * CAND
                for j in range(CAND):
                    taken = [table[pl.ds(rids[u][v, h, q * CAND + j], 2), :] for h in range(2) for q in range(2)]
                    proj[pl.ds(start + 2 * j, 2), :] = (taken[0] + taken[1]) + (taken[2] + taken[3])
                ca = parts[pl.ds(two * 2 + v, 1), :]
                cb = parts[pl.ds(32 + two * 2 + v, 1), :]
                re = proj[pl.ds(start, CAND, stride=2), :]
                im = proj[pl.ds(start + 1, CAND, stride=2), :]
                group = lax.rem(two, 8) // 2
                at = pl.ds(pl.multiple_of(group * 2 * CAND + i * CAND, CAND), CAND)
                lane = ((u % 2) * 2 + v) * 256
                cross[at, pl.ds(lane, 128)] = (ca * re + cb * im).astype(BF16)
                cross[at, pl.ds(lane + 128, 128)] = (cb * re - ca * im).astype(BF16)
            fetch(u, lax.rem(two + SLOTS, 16)).start()

    along = jnp.dot(cross[...], fx[...], preferred_element_type=F32)
    along = jnp.concatenate([along[g * 2 * CAND : (g + 1) * 2 * CAND] for g in range(4)], axis=1)
    both = jnp.concatenate(split(along), axis=0)
    squares = jnp.zeros((8, 2 * CAND), F32)
    for n in range(8):
        scores = lax.dot_general(fy[n * 128 : (n + 1) * 128, :], both, NT, preferred_element_type=F32)
        scores = scores[:, : 2 * CAND] + scores[:, 2 * CAND :]
        squares = squares + jnp.sum((scores * scores).reshape(16, 8, 2 * CAND), axis=0)
    energy = jnp.sum(squares, axis=0, keepdims=True) * (1.0 / (SIDE * SIDE))
    lane_id = lax.broadcasted_iota(jnp.int32, (1, 2 * CAND), 1)
    first = lane_id < CAND
    sum0 = jnp.sum(jnp.where(first, energy, 0.0), axis=1, keepdims=True)
    sum1 = jnp.sum(jnp.where(first, 0.0, energy), axis=1, keepdims=True)
    post = CAND * energy / (jnp.where(first, sum0, sum1) + 1e-6)
    turned = jnp.concatenate([post[:, CAND:], post[:, :CAND]], axis=1)
    post_out[0:1, :] = post[:, :CAND]
    post_out[1:2, :] = turned[:, :CAND]
    weights = (jnp.where(first, post, turned), jnp.where(first, turned, post))

    for u in range(SLOTS):
        fetch(u, u).wait()
    hear(1)
    tell(2)

    def histogram(i, b, w_hi, w_lo):
        ip = i * PB + b
        hit = left[ip]
        hits = jnp.concatenate([hit * w_hi, hit * w_lo], axis=0)
        both = lax.dot_general(hits, right[ip], NT, preferred_element_type=F32)
        both = both[:64] + both[64:]
        at = pl.ds(pl.multiple_of(ip * KINDS, KINDS), KINDS)
        for h in range(8):
            hist[at, pl.ds(h * 128, 128)] = both[h * 8 : (h + 1) * 8]

    for i in range(2):
        pair = split(jnp.concatenate([weights[i], weights[i]], axis=1))

        @pl.loop(0, PB, unroll=8)
        def _(b):
            histogram(i, b, *pair)

    d_hi, d_lo = split(jnp.concatenate([rows[c] for c in range(3)], axis=1))
    d_both = jnp.concatenate([d_hi, d_lo], axis=1)

    def map_sums(of_core, to):
        start = pl.multiple_of((of_core * 4 + to) * 128, 128)
        h_hi, h_lo = split(hist[:, pl.ds(start, 128)].T)
        got = jnp.dot(h_hi, d_both, preferred_element_type=F32)
        got = got[:, :384] + got[:, 384:] + jnp.dot(h_lo, d_hi, preferred_element_type=F32)
        return got.reshape(4, 32, 384)

    order = (2, 1, 3, 0)
    to_near = []
    for n, d in enumerate(order):
        to = lax.rem(x + d, 4)
        sums[to] = map_sums(1 - core, to)
        to_near.append(send(sums.at[to], near.at[to], near_s.at[n], near_r.at[n], sibling))
    then, with_it = [], []
    for n, dx in enumerate(order):
        to = lax.rem(x + dx, 4)
        total = map_sums(core, to)
        to_near[n].wait_recv()
        total = total + near[to]
        if dx == 0:
            mine[...] = total
        coded[to], bases[to] = encode(total)
        for dy in (2, 1, 3, 0):
            if dx or dy:
                to_x, to_y, peer = plane_peer(dx, dy)
                at = their_bases.at[dx, dy]
                with_it.append(send(bases.at[to_x], at, base_s.at[dx, dy], base_r.at[dx, dy], peer))
                at = coming.at[dx, dy]
                then.append(send(coded.at[to_x, to_y], at, plane_s.at[dx, dy], plane_r.at[dx, dy], peer))
    total = mine[y]
    at = 0
    for dx in order:
        for dy in (2, 1, 3, 0):
            if dx or dy:
                with_it[at].wait_recv()
                then[at].wait_recv()
                total = total + decode(coming[dx, dy], their_bases[dx, dy])
                at += 1
    for n in range(8):
        s3[n] = total[n * 4 : (n + 1) * 4]
    hear(2)
    third = []
    for d in (4, 3, 5, 2, 6, 1, 7):
        to, peer = z_peer(d)
        third.append(send(s3.at[to], r3.at[d], zs.at[d], zr.at[d], peer))
    for copy in third:
        copy.wait_recv()
    total = s3[z]
    for d in range(1, 8):
        total = total + r3[d]
    data[...] = total[:, :256]
    weight[...] = total[:, 256:]
    for copy in sends + to_near + then + with_it + third:
        copy.wait_send()


def finish_kernel(data, weight, post, data_out, weight_out, post_out, sem):
    copies = [
        pltpu.make_async_copy(data, data_out, sem.at[0]),
        pltpu.make_async_copy(weight, weight_out, sem.at[1]),
        pltpu.make_async_copy(post, post_out, sem.at[2]),
    ]
    for copy in copies:
        copy.start()
    for copy in copies:
        copy.wait()


def local(ref_map, images, ctf_table, ctf_class, block_index, interp_kind, interp_bank):
    blk = jnp.transpose(block_index, (0, 2, 3, 1)).reshape(32, TAPS, CAND)
    kind = jnp.transpose(interp_kind, (0, 2, 3, 1)).reshape(32, TAPS, CAND)
    dma = pltpu.SemaphoreType.DMA
    i32 = jnp.int32
    shapes = [
        jax.ShapeDtypeStruct((4, 256), F32),
        jax.ShapeDtypeStruct((4, 128), F32),
        jax.ShapeDtypeStruct((2, CAND), F32),
    ]
    results = pl.pallas_call(
        refine_kernel,
        out_shape=shapes,
        in_specs=[pl.BlockSpec(memory_space=pltpu.HBM)] * 9,
        out_specs=[pl.BlockSpec(memory_space=VMEM)] * 3,
        scratch_shapes=[
            VMEM((2, 2, 2048), BF16),
            VMEM((64, 2048), BF16),
            pltpu.SMEM((2,), i32),
            VMEM((32, TAPS, CAND), i32),
            VMEM((32, TAPS, CAND), i32),
            VMEM((KINDS, BW, BW), BF16),
            VMEM((1024, 128), BF16),
            VMEM((1024, 512), BF16),
            dma((10,)),
            VMEM((8, BW, 2 * BW), BF16),
            VMEM((2 * BW, BW), F32),
            VMEM((2 * KINDS * NBLK, BW), F32),
            VMEM((96, BW), F32),
            VMEM((3, 256, BW), F32),
            VMEM((32, 2, 128), i32),
            [pltpu.SMEM((2, 2, 128), i32)] * SLOTS,
            dma((SLOTS,)),
            VMEM((32, 64, 256), BF16),
            VMEM((32, 128, 256), BF16),
            VMEM((SLOTS * 4 * CAND, BW), F32),
            VMEM((8 * CAND, 1024), BF16),
            VMEM((256, NBLK), F32),
            dma((8,)), dma((8,)), dma((8,)), dma((8,)),
            VMEM((4, 4, 32, 384), F32),
            VMEM((4, 4, 32, 384), F32),
            VMEM((4, 32, 384), F32),
            VMEM((4, 4, 32, 384), jnp.int16),
            VMEM((4, 4, 32, 384), jnp.int16),
            VMEM((4, 1, 384), F32),
            VMEM((4, 4, 1, 384), F32),
            VMEM((8, 4, 384), F32),
            VMEM((8, 4, 384), F32),
            dma((4,)), dma((4,)), dma((4, 4)), dma((4, 4)), dma((4, 4)), dma((4, 4)),
            dma((8,)), dma((8,)),
            pltpu.SemaphoreType.REGULAR((3, 2)),
        ],
        compiler_params=pltpu.CompilerParams(
            collective_id=0, has_side_effects=True, vmem_limit_bytes=56 * 1024 * 1024
        ),
        name="refine",
    )(
        ref_map, images, ctf_table, ctf_class, blk, kind, interp_bank,
        jnp.asarray(line_table(), BF16), jnp.asarray(across_table(), BF16),
    )
    return pl.pallas_call(
        finish_kernel,
        out_shape=shapes,
        in_specs=[pl.BlockSpec(memory_space=pltpu.HBM)] * 3,
        out_specs=[pl.BlockSpec(memory_space=pltpu.HBM)] * 3,
        scratch_shapes=[dma((3,))],
        compiler_params=pltpu.CompilerParams(vmem_limit_bytes=56 * 1024 * 1024),
        name="finish",
    )(*results)


def solution(mesh):
    in_specs = (
        P("slab", None),
        P(("particle", "slab"), None, None),
        P(),
        P(("particle", "slab")),
        P(("particle", "slab"), None, None, None),
        P(("particle", "slab"), None, None, None),
        P(),
    )
    out_specs = (
        P(("particle", "slab"), None),
        P(("particle", "slab"), None),
        P(("particle", "slab"), None),
    )
    return jax.shard_map(local, mesh=mesh, in_specs=in_specs, out_specs=out_specs, check_vma=False)
```

```python
import math

import jax
import jax.numpy as jnp
import numpy as np
from jax import lax
from jax.experimental import pallas as pl
from jax.experimental.pallas import tpu as pltpu
from jax.sharding import PartitionSpec as P

LINE = 256
PLINES = 8
SIDE = 32
BW = 128
TAPS = 4
KINDS = 8
CAND = 64
PB = 16
NBLK = 1024
MESH = pl.DeviceIdType.MESH
SLOTS = 4
OCTAVES = 44
STEPS = 744
LN2 = math.log(2.0)
ORDER = (5, 4, 3, 2, 7, 6, 1)
VMEM = pltpu.VMEM
F32 = jnp.float32
BF16 = jnp.bfloat16
NT = (((1,), (1,)), ((), ()))


def line_table():
    fx = np.arange(LINE) - LINE // 2
    sx = np.arange(SIDE) - SIDE // 2
    ang = 2.0 * np.pi / LINE * ((fx[:, None] * sx[None, :]) % LINE)
    cos, sin = np.cos(ang), np.sin(ang)
    one = np.zeros((2, 2, BW, 2, SIDE))
    one[:, 0, :, 0] = cos.reshape(2, BW, SIDE)
    one[:, 1, :, 0] = -sin.reshape(2, BW, SIDE)
    one[:, 0, :, 1] = sin.reshape(2, BW, SIDE)
    one[:, 1, :, 1] = cos.reshape(2, BW, SIDE)
    both = np.zeros((2, 2, 2, BW, 2, 2, SIDE))
    both[0, :, :, :, 0] = one
    both[1, :, :, :, 1] = one
    return both.reshape(8 * BW, 4 * SIDE)


def across_table():
    fy = np.arange(PLINES) - PLINES // 2
    sy = np.arange(SIDE) - SIDE // 2
    ang = 2.0 * np.pi / LINE * ((fy[None, :] * sy[:, None]) % LINE)
    full = np.zeros((SIDE, SIDE, PLINES, 2, SIDE))
    for s in range(SIDE):
        full[:, s, :, 0, s] = np.cos(ang)
        full[:, s, :, 1, s] = -np.sin(ang)
    return full.reshape(SIDE * SIDE, PLINES * 2 * SIDE)


def split(v):
    hi = v.astype(BF16)
    return hi, (v - hi.astype(F32)).astype(BF16)


def encode(v):
    size = jnp.abs(v)
    top = jnp.max(jnp.max(size, axis=0), axis=0, keepdims=True)
    base = jnp.log(jnp.maximum(top, 1e-37)) - OCTAVES * LN2
    size = (jnp.log(jnp.maximum(size, 1e-37)) - base) * (STEPS / LN2)
    size = jnp.maximum(size, 0.0) + 0.5
    return jnp.where(v < 0, -size, size).astype(jnp.int32).astype(jnp.int16), base


def decode(code, base):
    step = code.astype(jnp.int32).astype(F32)
    size = jnp.exp(jnp.abs(step) * (LN2 / STEPS) + base)
    return jnp.where(step > 0, size, jnp.where(step < 0, -size, 0.0))


def refine_kernel(
    piece, img_h, ctf_h, cls_h, blk_h, kind_h, bank_h, fx_h, fy_h,
    data, weight, post_out,
    img, ctf, cls, blk, kind, bank, fx, fy, own_sem,
    full, inter, table, parts, rows, rid_v, rids, rid_s, left, right,
    proj, cross, hist, gather_s, gather_r, forward_s, forward_r,
    sums, near, mine, coded, coming, bases, their_bases, s3, r3,
    near_s, near_r, plane_s, plane_r, base_s, base_r, zs, zr, here,
):
    p = lax.axis_index("particle")
    s = lax.axis_index("slab")
    z, x_lo, core = p // 4, lax.rem(p // 2, 2), lax.rem(p, 2)
    x_hi, y = s // 4, lax.rem(s, 4)
    x = x_hi * 2 + x_lo

    sibling = (p + 1 - 2 * core, s)

    def x_peer(d):
        to = lax.rem(x + d, 4)
        return to, (p + (lax.rem(to, 2) - x_lo) * 2, s + (to // 2 - x_hi) * 4)

    def plane_peer(dx, dy):
        to_x, to_y = lax.rem(x + dx, 4), lax.rem(y + dy, 4)
        return to_x, to_y, (p + (lax.rem(to_x, 2) - x_lo) * 2, to_x // 2 * 4 + to_y)

    def z_peer(d):
        to = lax.rem(z + d, 8)
        return to, (p + (to - z) * 4, s)

    def map_peer(n, sign):
        flip = lax.rem(n, 2)
        to = lax.rem(y + 4 + sign * (n // 2), 4)
        return (p + flip * (2 - 4 * x_lo), (x_hi + flip * (1 - 2 * x_hi)) * 4 + to)

    def send(src, dst, ssem, rsem, peer):
        copy = pltpu.make_async_remote_copy(
            src_ref=src, dst_ref=dst, send_sem=ssem, recv_sem=rsem, device_id=peer, device_id_type=MESH
        )
        copy.start()
        return copy

    peers = [sibling] + [x_peer(d)[1] for d in (1, 2, 3)] + [z_peer(d)[1] for d in (1, 7)]
    peers += [map_peer(n, 1) for n in range(1, 8)]
    barrier = pltpu.get_barrier_semaphore()
    for peer in peers:
        pl.semaphore_signal(barrier, inc=1, device_id=peer, device_id_type=MESH)
    pairs = [
        (blk_h, blk), (kind_h, kind), (img_h, img), (ctf_h, ctf), (cls_h, cls), (bank_h, bank),
        (piece, full.at[s]), (fx_h, fx), (fy_h, fy),
    ]
    loads = [pltpu.make_async_copy(a, b, own_sem.at[n]) for n, (a, b) in enumerate(pairs)]
    for load in loads:
        load.start()
    pl.semaphore_wait(barrier, len(peers))
    half = pl.ds(pl.multiple_of(core * 64, 64), 64)
    sends = []
    for n in ORDER:
        sends.append(send(piece.at[half], full.at[s, half], gather_s.at[n], gather_r.at[n], map_peer(n, 1)))

    def tell(n):
        for side, d in enumerate((1, 7)):
            pl.semaphore_signal(here.at[n, side], inc=1, device_id=z_peer(d)[1], device_id_type=MESH)

    def hear(n):
        for side in range(2):
            pl.semaphore_wait(here.at[n, side], 1)

    tell(0)

    loads[0].wait()
    loads[1].wait()
    number = kind[...] * NBLK + blk[...]
    for h in range(2):
        pair = jnp.concatenate([number[:, 2 * h, :], number[:, 2 * h + 1, :]], axis=1)
        rid_v[:, h, :] = pair * 2

    def fetch(u, two):
        return pltpu.make_async_copy(rid_v.at[pl.ds(two * 2, 2)], rids[u], rid_s.at[u])

    for u in range(SLOTS):
        fetch(u, u).start()

    for load in loads[2:6]:
        load.wait()
    lanes = lax.broadcasted_iota(jnp.int32, (16, 64), 1)
    which = lax.broadcasted_iota(jnp.int32, (16, 64), 0)
    pick = jnp.where(which == 0, cls[0], cls[1])
    onehot = (lanes == pick).astype(F32).astype(BF16)
    gain = jnp.dot(onehot, ctf[...], preferred_element_type=F32)
    pixel = img[...].astype(F32)
    for i in range(2):
        g = gain[i : i + 1]
        for c, row in enumerate((g * pixel[i, 0:1], g * pixel[i, 1:2], g * g)):
            for b in range(PB):
                parts[pl.ds(c * 32 + i * PB + b, 1), :] = row[:, b * BW : (b + 1) * BW]
    both = jnp.concatenate(split(parts[...]), axis=0)
    for k in range(KINDS):
        turned = lax.dot_general(both, bank[k], NT, preferred_element_type=F32)
        turned = turned[:96] + turned[96:]
        for c in range(3):
            rows[c, pl.ds(k, 32, stride=KINDS), :] = turned[c * 32 : (c + 1) * 32]

    row_id = lax.broadcasted_iota(jnp.int32, (64, 128), 0)
    col_id = lax.broadcasted_iota(jnp.int32, (128, 128), 0)

    @pl.loop(0, 32)
    def _(ip):
        for h in range(2):
            v = rid_v[ip, pl.ds(h, 1), :] >> 1
            high = ((v >> 5) & 1) * 4 + ((v >> 4) & 1) * 2 + ((v >> 6) & 1)
            low = ((v >> 2) & 3) * 32 + ((v >> 7) & 7) * 4 + (v & 3)
            at = pl.ds(h * 128, 128)
            left[ip, :, at] = jnp.where(row_id == high * KINDS + (v >> 10), 1.0, 0.0).astype(BF16)
            right[ip, :, at] = jnp.where(col_id == low, 1.0, 0.0).astype(BF16)

    def map_piece(source):
        inter[pl.ds(0, BW, stride=2), :] = full[source, :, :BW].astype(F32)
        inter[pl.ds(1, BW, stride=2), :] = full[source, :, BW:].astype(F32)
        lhs = inter[...].astype(BF16)
        for k in range(0, KINDS, 2):
            mapped = jnp.dot(lhs, jnp.concatenate([bank[k], bank[k + 1]], axis=1), preferred_element_type=F32)
            for h in range(2):
                at = pl.ds(pl.multiple_of((k + h) * 2 * NBLK + source * 256, 256), 256)
                table[at, :] = mapped[:, h * BW : (h + 1) * BW].astype(BF16).astype(F32)

    loads[6].wait()
    map_piece(s)

    def forward(n, rows):
        at = full.at[map_peer(n, -1)[1], rows]
        return pltpu.make_async_remote_copy(
            src_ref=at, dst_ref=at, send_sem=forward_s.at[n], recv_sem=forward_r.at[n],
            device_id=sibling, device_id_type=MESH,
        )

    other_half = pl.ds(pl.multiple_of((1 - core) * 64, 64), 64)
    def pass_on(n):
        peer = map_peer(n, -1)
        pltpu.make_async_remote_copy(
            src_ref=piece.at[half], dst_ref=full.at[peer[1], half], send_sem=gather_s.at[n],
            recv_sem=gather_r.at[n], device_id=peer, device_id_type=MESH,
        ).wait_recv()
        forward(n, half).start()

    def use(n):
        forward(n, other_half).wait_recv()
        map_piece(map_peer(n, -1)[1])

    def nth(k):
        return lax.rem(2 * k - 1, 7) + 1

    pass_on(2)

    @pl.loop(1, 7)
    def _(k):
        pass_on(nth(k + 1))
        use(nth(k))

    use(7)
    for n in range(1, 8):
        forward(n, half).wait_send()

    hear(0)
    tell(1)
    loads[7].wait()
    loads[8].wait()

    @pl.loop(0, 16 // SLOTS)
    def _(step):
        for u in range(SLOTS):
            two = step * SLOTS + u
            i = two // 8
            fetch(u, two).wait()
            for v in range(2):
                start = (u * 2 + v) * 2 * CAND
                for j in range(CAND):
                    taken = [table[pl.ds(rids[u][v, h, q * CAND + j], 2), :] for h in range(2) for q in range(2)]
                    proj[pl.ds(start + 2 * j, 2), :] = (taken[0] + taken[1]) + (taken[2] + taken[3])
                ca = parts[pl.ds(two * 2 + v, 1), :]
                cb = parts[pl.ds(32 + two * 2 + v, 1), :]
                re = proj[pl.ds(start, CAND, stride=2), :]
                im = proj[pl.ds(start + 1, CAND, stride=2), :]
                group = lax.rem(two, 8) // 2
                at = pl.ds(pl.multiple_of(group * 2 * CAND + i * CAND, CAND), CAND)
                lane = ((u % 2) * 2 + v) * 256
                cross[at, pl.ds(lane, 128)] = (ca * re + cb * im).astype(BF16)
                cross[at, pl.ds(lane + 128, 128)] = (cb * re - ca * im).astype(BF16)
            fetch(u, lax.rem(two + SLOTS, 16)).start()

    along = jnp.dot(cross[...], fx[...], preferred_element_type=F32)
    along = jnp.concatenate([along[g * 2 * CAND : (g + 1) * 2 * CAND] for g in range(4)], axis=1)
    both = jnp.concatenate(split(along), axis=0)
    squares = jnp.zeros((8, 2 * CAND), F32)
    for n in range(8):
        scores = lax.dot_general(fy[n * 128 : (n + 1) * 128, :], both, NT, preferred_element_type=F32)
        scores = scores[:, : 2 * CAND] + scores[:, 2 * CAND :]
        squares = squares + jnp.sum((scores * scores).reshape(16, 8, 2 * CAND), axis=0)
    energy = jnp.sum(squares, axis=0, keepdims=True) * (1.0 / (SIDE * SIDE))
    lane_id = lax.broadcasted_iota(jnp.int32, (1, 2 * CAND), 1)
    first = lane_id < CAND
    sum0 = jnp.sum(jnp.where(first, energy, 0.0), axis=1, keepdims=True)
    sum1 = jnp.sum(jnp.where(first, 0.0, energy), axis=1, keepdims=True)
    post = CAND * energy / (jnp.where(first, sum0, sum1) + 1e-6)
    turned = jnp.concatenate([post[:, CAND:], post[:, :CAND]], axis=1)
    post_out[0:1, :] = post[:, :CAND]
    post_out[1:2, :] = turned[:, :CAND]
    weights = (jnp.where(first, post, turned), jnp.where(first, turned, post))

    for u in range(SLOTS):
        fetch(u, u).wait()
    hear(1)
    tell(2)

    def histogram(i, b, w_hi, w_lo):
        ip = i * PB + b
        hit = left[ip]
        hits = jnp.concatenate([hit * w_hi, hit * w_lo], axis=0)
        both = lax.dot_general(hits, right[ip], NT, preferred_element_type=F32)
        both = both[:64] + both[64:]
        at = pl.ds(pl.multiple_of(ip * KINDS, KINDS), KINDS)
        for h in range(8):
            hist[at, pl.ds(h * 128, 128)] = both[h * 8 : (h + 1) * 8]

    for i in range(2):
        pair = split(jnp.concatenate([weights[i], weights[i]], axis=1))

        @pl.loop(0, PB, unroll=8)
        def _(b):
            histogram(i, b, *pair)

    d_hi, d_lo = split(jnp.concatenate([rows[c] for c in range(3)], axis=1))
    d_both = jnp.concatenate([d_hi, d_lo], axis=1)

    def map_sums(of_core, to):
        start = pl.multiple_of((of_core * 4 + to) * 128, 128)
        h_hi, h_lo = split(hist[:, pl.ds(start, 128)].T)
        got = jnp.dot(h_hi, d_both, preferred_element_type=F32)
        got = got[:, :384] + got[:, 384:] + jnp.dot(h_lo, d_hi, preferred_element_type=F32)
        return got.reshape(4, 32, 384)

    order = (2, 1, 3, 0)
    to_near = []
    for n, d in enumerate(order):
        to = lax.rem(x + d, 4)
        sums[to] = map_sums(1 - core, to)
        to_near.append(send(sums.at[to], near.at[to], near_s.at[n], near_r.at[n], sibling))
    then, with_it = [], []
    for n, dx in enumerate(order):
        to = lax.rem(x + dx, 4)
        total = map_sums(core, to)
        to_near[n].wait_recv()
        total = total + near[to]
        if dx == 0:
            mine[...] = total
        coded[to], bases[to] = encode(total)
        for dy in (2, 1, 3, 0):
            if dx or dy:
                to_x, to_y, peer = plane_peer(dx, dy)
                at = their_bases.at[dx, dy]
                with_it.append(send(bases.at[to_x], at, base_s.at[dx, dy], base_r.at[dx, dy], peer))
                at = coming.at[dx, dy]
                then.append(send(coded.at[to_x, to_y], at, plane_s.at[dx, dy], plane_r.at[dx, dy], peer))
    total = mine[y]
    at = 0
    for dx in order:
        for dy in (2, 1, 3, 0):
            if dx or dy:
                with_it[at].wait_recv()
                then[at].wait_recv()
                total = total + decode(coming[dx, dy], their_bases[dx, dy])
                at += 1
    for n in range(8):
        s3[n] = total[n * 4 : (n + 1) * 4]
    hear(2)
    third = []
    for d in (4, 3, 5, 2, 6, 1, 7):
        to, peer = z_peer(d)
        third.append(send(s3.at[to], r3.at[d], zs.at[d], zr.at[d], peer))
    for copy in third:
        copy.wait_recv()
    total = s3[z]
    for d in range(1, 8):
        total = total + r3[d]
    data[...] = total[:, :256]
    weight[...] = total[:, 256:]
    for copy in sends + to_near + then + with_it + third:
        copy.wait_send()


def finish_kernel(data, weight, post, data_out, weight_out, post_out, sem):
    copies = [
        pltpu.make_async_copy(data, data_out, sem.at[0]),
        pltpu.make_async_copy(weight, weight_out, sem.at[1]),
        pltpu.make_async_copy(post, post_out, sem.at[2]),
    ]
    for copy in copies:
        copy.start()
    for copy in copies:
        copy.wait()


def local(ref_map, images, ctf_table, ctf_class, block_index, interp_kind, interp_bank):
    blk = jnp.transpose(block_index, (0, 2, 3, 1)).reshape(32, TAPS, CAND)
    kind = jnp.transpose(interp_kind, (0, 2, 3, 1)).reshape(32, TAPS, CAND)
    dma = pltpu.SemaphoreType.DMA
    i32 = jnp.int32
    shapes = [
        jax.ShapeDtypeStruct((4, 256), F32),
        jax.ShapeDtypeStruct((4, 128), F32),
        jax.ShapeDtypeStruct((2, CAND), F32),
    ]
    results = pl.pallas_call(
        refine_kernel,
        out_shape=shapes,
        in_specs=[pl.BlockSpec(memory_space=pltpu.HBM)] * 9,
        out_specs=[pl.BlockSpec(memory_space=VMEM)] * 3,
        scratch_shapes=[
            VMEM((2, 2, 2048), BF16),
            VMEM((64, 2048), BF16),
            pltpu.SMEM((2,), i32),
            VMEM((32, TAPS, CAND), i32),
            VMEM((32, TAPS, CAND), i32),
            VMEM((KINDS, BW, BW), BF16),
            VMEM((1024, 128), BF16),
            VMEM((1024, 512), BF16),
            dma((10,)),
            VMEM((8, BW, 2 * BW), BF16),
            VMEM((2 * BW, BW), F32),
            VMEM((2 * KINDS * NBLK, BW), F32),
            VMEM((96, BW), F32),
            VMEM((3, 256, BW), F32),
            VMEM((32, 2, 128), i32),
            [pltpu.SMEM((2, 2, 128), i32)] * SLOTS,
            dma((SLOTS,)),
            VMEM((32, 64, 256), BF16),
            VMEM((32, 128, 256), BF16),
            VMEM((SLOTS * 4 * CAND, BW), F32),
            VMEM((8 * CAND, 1024), BF16),
            VMEM((256, NBLK), F32),
            dma((8,)), dma((8,)), dma((8,)), dma((8,)),
            VMEM((4, 4, 32, 384), F32),
            VMEM((4, 4, 32, 384), F32),
            VMEM((4, 32, 384), F32),
            VMEM((4, 4, 32, 384), jnp.int16),
            VMEM((4, 4, 32, 384), jnp.int16),
            VMEM((4, 1, 384), F32),
            VMEM((4, 4, 1, 384), F32),
            VMEM((8, 4, 384), F32),
            VMEM((8, 4, 384), F32),
            dma((4,)), dma((4,)), dma((4, 4)), dma((4, 4)), dma((4, 4)), dma((4, 4)),
            dma((8,)), dma((8,)),
            pltpu.SemaphoreType.REGULAR((3, 2)),
        ],
        compiler_params=pltpu.CompilerParams(
            collective_id=0, has_side_effects=True, vmem_limit_bytes=56 * 1024 * 1024
        ),
        name="refine",
    )(
        ref_map, images, ctf_table, ctf_class, blk, kind, interp_bank,
        jnp.asarray(line_table(), BF16), jnp.asarray(across_table(), BF16),
    )
    return pl.pallas_call(
        finish_kernel,
        out_shape=shapes,
        in_specs=[pl.BlockSpec(memory_space=pltpu.HBM)] * 3,
        out_specs=[pl.BlockSpec(memory_space=pltpu.HBM)] * 3,
        scratch_shapes=[dma((3,))],
        compiler_params=pltpu.CompilerParams(vmem_limit_bytes=56 * 1024 * 1024),
        name="finish",
    )(*results)


def solution(mesh):
    in_specs = (
        P("slab", None),
        P(("particle", "slab"), None, None),
        P(),
        P(("particle", "slab")),
        P(("particle", "slab"), None, None, None),
        P(("particle", "slab"), None, None, None),
        P(),
    )
    out_specs = (
        P(("particle", "slab"), None),
        P(("particle", "slab"), None),
        P(("particle", "slab"), None),
    )
    return jax.shard_map(local, mesh=mesh, in_specs=in_specs, out_specs=out_specs, check_vma=False)
```

```python
import math

import jax
import jax.numpy as jnp
import numpy as np
from jax import lax
from jax.experimental import pallas as pl
from jax.experimental.pallas import tpu as pltpu
from jax.sharding import PartitionSpec as P

LINE = 256
PLINES = 8
SIDE = 32
BW = 128
TAPS = 4
KINDS = 8
CAND = 64
PB = 16
NBLK = 1024
MESH = pl.DeviceIdType.MESH
SLOTS = 4
OCTAVES = 44
STEPS = 744
LN2 = math.log(2.0)
ORDER = (1, 2, 3, 4, 5, 6, 7)
VMEM = pltpu.VMEM
F32 = jnp.float32
BF16 = jnp.bfloat16
NT = (((1,), (1,)), ((), ()))


def line_table():
    fx = np.arange(LINE) - LINE // 2
    sx = np.arange(SIDE) - SIDE // 2
    ang = 2.0 * np.pi / LINE * ((fx[:, None] * sx[None, :]) % LINE)
    cos, sin = np.cos(ang), np.sin(ang)
    one = np.zeros((2, 2, BW, 2, SIDE))
    one[:, 0, :, 0] = cos.reshape(2, BW, SIDE)
    one[:, 1, :, 0] = -sin.reshape(2, BW, SIDE)
    one[:, 0, :, 1] = sin.reshape(2, BW, SIDE)
    one[:, 1, :, 1] = cos.reshape(2, BW, SIDE)
    both = np.zeros((2, 2, 2, BW, 2, 2, SIDE))
    both[0, :, :, :, 0] = one
    both[1, :, :, :, 1] = one
    return both.reshape(8 * BW, 4 * SIDE)


def across_table():
    fy = np.arange(PLINES) - PLINES // 2
    sy = np.arange(SIDE) - SIDE // 2
    ang = 2.0 * np.pi / LINE * ((fy[None, :] * sy[:, None]) % LINE)
    full = np.zeros((SIDE, SIDE, PLINES, 2, SIDE))
    for s in range(SIDE):
        full[:, s, :, 0, s] = np.cos(ang)
        full[:, s, :, 1, s] = -np.sin(ang)
    return full.reshape(SIDE * SIDE, PLINES * 2 * SIDE)


def split(v):
    hi = v.astype(BF16)
    return hi, (v - hi.astype(F32)).astype(BF16)


def encode(v):
    size = jnp.abs(v)
    top = jnp.max(jnp.max(size, axis=0), axis=0, keepdims=True)
    base = jnp.log(jnp.maximum(top, 1e-37)) - OCTAVES * LN2
    size = (jnp.log(jnp.maximum(size, 1e-37)) - base) * (STEPS / LN2)
    size = jnp.maximum(size, 0.0) + 0.5
    return jnp.where(v < 0, -size, size).astype(jnp.int32).astype(jnp.int16), base


def decode(code, base):
    step = code.astype(jnp.int32).astype(F32)
    size = jnp.exp(jnp.abs(step) * (LN2 / STEPS) + base)
    return jnp.where(step > 0, size, jnp.where(step < 0, -size, 0.0))


def refine_kernel(
    piece, img_h, ctf_h, cls_h, blk_h, kind_h, bank_h, fx_h, fy_h,
    data, weight, post_out,
    img, ctf, cls, blk, kind, bank, fx, fy, own_sem,
    full, inter, table, parts, rows, rid_v, rids, rid_s, left, right,
    proj, cross, hist, gather_s, gather_r, forward_s, forward_r,
    sums, near, mine, coded, coming, bases, their_bases, s3, r3,
    near_s, near_r, plane_s, plane_r, base_s, base_r, zs, zr, here,
):
    p = lax.axis_index("particle")
    s = lax.axis_index("slab")
    z, x_lo, core = p // 4, lax.rem(p // 2, 2), lax.rem(p, 2)
    x_hi, y = s // 4, lax.rem(s, 4)
    x = x_hi * 2 + x_lo

    sibling = (p + 1 - 2 * core, s)

    def x_peer(d):
        to = lax.rem(x + d, 4)
        return to, (p + (lax.rem(to, 2) - x_lo) * 2, s + (to // 2 - x_hi) * 4)

    def plane_peer(dx, dy):
        to_x, to_y = lax.rem(x + dx, 4), lax.rem(y + dy, 4)
        return to_x, to_y, (p + (lax.rem(to_x, 2) - x_lo) * 2, to_x // 2 * 4 + to_y)

    def z_peer(d):
        to = lax.rem(z + d, 8)
        return to, (p + (to - z) * 4, s)

    def map_peer(n, sign):
        flip = lax.rem(n, 2)
        to = lax.rem(y + 4 + sign * (n // 2), 4)
        return (p + flip * (2 - 4 * x_lo), (x_hi + flip * (1 - 2 * x_hi)) * 4 + to)

    def send(src, dst, ssem, rsem, peer):
        copy = pltpu.make_async_remote_copy(
            src_ref=src, dst_ref=dst, send_sem=ssem, recv_sem=rsem, device_id=peer, device_id_type=MESH
        )
        copy.start()
        return copy

    peers = [map_peer(n, 1) for n in (5, 3, 7, 4)] + [x_peer(d)[1] for d in (2, 1, 3)]
    peers += [map_peer(n, 1) for n in (1, 2, 6)] + [z_peer(d)[1] for d in (1, 7)] + [sibling]
    barrier = pltpu.get_barrier_semaphore()
    for peer in peers:
        pl.semaphore_signal(barrier, inc=1, device_id=peer, device_id_type=MESH)
    pairs = [
        (blk_h, blk), (kind_h, kind), (img_h, img), (ctf_h, ctf), (cls_h, cls), (bank_h, bank),
        (piece, full.at[s]), (fx_h, fx), (fy_h, fy),
    ]
    loads = [pltpu.make_async_copy(a, b, own_sem.at[n]) for n, (a, b) in enumerate(pairs)]
    for load in loads:
        load.start()
    pl.semaphore_wait(barrier, len(peers))
    half = pl.ds(pl.multiple_of(core * 64, 64), 64)
    sends = []
    for n in ORDER:
        sends.append(send(piece.at[half], full.at[s, half], gather_s.at[n], gather_r.at[n], map_peer(n, 1)))

    def tell(n):
        for side, d in enumerate((1, 7)):
            pl.semaphore_signal(here.at[n, side], inc=1, device_id=z_peer(d)[1], device_id_type=MESH)

    def hear(n):
        for side in range(2):
            pl.semaphore_wait(here.at[n, side], 1)

    tell(0)

    loads[0].wait()
    loads[1].wait()
    number = kind[...] * NBLK + blk[...]
    for h in range(2):
        pair = jnp.concatenate([number[:, 2 * h, :], number[:, 2 * h + 1, :]], axis=1)
        rid_v[:, h, :] = pair * 2

    def fetch(u, two):
        return pltpu.make_async_copy(rid_v.at[pl.ds(two * 2, 2)], rids[u], rid_s.at[u])

    for u in range(SLOTS):
        fetch(u, u).start()

    for load in loads[2:6]:
        load.wait()
    lanes = lax.broadcasted_iota(jnp.int32, (16, 64), 1)
    which = lax.broadcasted_iota(jnp.int32, (16, 64), 0)
    pick = jnp.where(which == 0, cls[0], cls[1])
    onehot = (lanes == pick).astype(F32).astype(BF16)
    gain = jnp.dot(onehot, ctf[...], preferred_element_type=F32)
    pixel = img[...].astype(F32)
    for i in range(2):
        g = gain[i : i + 1]
        for c, row in enumerate((g * pixel[i, 0:1], g * pixel[i, 1:2], g * g)):
            for b in range(PB):
                parts[pl.ds(c * 32 + i * PB + b, 1), :] = row[:, b * BW : (b + 1) * BW]
    both = jnp.concatenate(split(parts[...]), axis=0)
    for k in range(KINDS):
        turned = lax.dot_general(both, bank[k], NT, preferred_element_type=F32)
        turned = turned[:96] + turned[96:]
        for c in range(3):
            rows[c, pl.ds(k, 32, stride=KINDS), :] = turned[c * 32 : (c + 1) * 32]

    row_id = lax.broadcasted_iota(jnp.int32, (64, 128), 0)
    col_id = lax.broadcasted_iota(jnp.int32, (128, 128), 0)

    @pl.loop(0, 32)
    def _(ip):
        for h in range(2):
            v = rid_v[ip, pl.ds(h, 1), :] >> 1
            high = ((v >> 5) & 1) * 4 + ((v >> 4) & 1) * 2 + ((v >> 6) & 1)
            low = ((v >> 2) & 3) * 32 + ((v >> 7) & 7) * 4 + (v & 3)
            at = pl.ds(h * 128, 128)
            left[ip, :, at] = jnp.where(row_id == high * KINDS + (v >> 10), 1.0, 0.0).astype(BF16)
            right[ip, :, at] = jnp.where(col_id == low, 1.0, 0.0).astype(BF16)

    def map_piece(source):
        inter[pl.ds(0, BW, stride=2), :] = full[source, :, :BW].astype(F32)
        inter[pl.ds(1, BW, stride=2), :] = full[source, :, BW:].astype(F32)
        lhs = inter[...].astype(BF16)
        for k in range(0, KINDS, 2):
            mapped = jnp.dot(lhs, jnp.concatenate([bank[k], bank[k + 1]], axis=1), preferred_element_type=F32)
            for h in range(2):
                at = pl.ds(pl.multiple_of((k + h) * 2 * NBLK + source * 256, 256), 256)
                table[at, :] = mapped[:, h * BW : (h + 1) * BW].astype(BF16).astype(F32)

    loads[6].wait()
    map_piece(s)

    def forward(n, rows):
        at = full.at[map_peer(n, -1)[1], rows]
        return pltpu.make_async_remote_copy(
            src_ref=at, dst_ref=at, send_sem=forward_s.at[n], recv_sem=forward_r.at[n],
            device_id=sibling, device_id_type=MESH,
        )

    other_half = pl.ds(pl.multiple_of((1 - core) * 64, 64), 64)
    def pass_on(n):
        peer = map_peer(n, -1)
        pltpu.make_async_remote_copy(
            src_ref=piece.at[half], dst_ref=full.at[peer[1], half], send_sem=gather_s.at[n],
            recv_sem=gather_r.at[n], device_id=peer, device_id_type=MESH,
        ).wait_recv()
        forward(n, half).start()

    def use(n):
        forward(n, other_half).wait_recv()
        map_piece(map_peer(n, -1)[1])

    pass_on(1)

    @pl.loop(1, 7)
    def _(n):
        pass_on(n + 1)
        use(n)

    use(7)
    for n in range(1, 8):
        forward(n, half).wait_send()

    hear(0)
    tell(1)
    loads[7].wait()
    loads[8].wait()

    @pl.loop(0, 16 // SLOTS)
    def _(step):
        for u in range(SLOTS):
            two = step * SLOTS + u
            i = two // 8
            fetch(u, two).wait()
            for v in range(2):
                start = (u * 2 + v) * 2 * CAND
                for j in range(CAND):
                    taken = [table[pl.ds(rids[u][v, h, q * CAND + j], 2), :] for h in range(2) for q in range(2)]
                    proj[pl.ds(start + 2 * j, 2), :] = (taken[0] + taken[1]) + (taken[2] + taken[3])
                ca = parts[pl.ds(two * 2 + v, 1), :]
                cb = parts[pl.ds(32 + two * 2 + v, 1), :]
                re = proj[pl.ds(start, CAND, stride=2), :]
                im = proj[pl.ds(start + 1, CAND, stride=2), :]
                group = lax.rem(two, 8) // 2
                at = pl.ds(pl.multiple_of(group * 2 * CAND + i * CAND, CAND), CAND)
                lane = ((u % 2) * 2 + v) * 256
                cross[at, pl.ds(lane, 128)] = (ca * re + cb * im).astype(BF16)
                cross[at, pl.ds(lane + 128, 128)] = (cb * re - ca * im).astype(BF16)
            fetch(u, lax.rem(two + SLOTS, 16)).start()

    along = jnp.dot(cross[...], fx[...], preferred_element_type=F32)
    along = jnp.concatenate([along[g * 2 * CAND : (g + 1) * 2 * CAND] for g in range(4)], axis=1)
    both = jnp.concatenate(split(along), axis=0)
    squares = jnp.zeros((8, 2 * CAND), F32)
    for n in range(8):
        scores = lax.dot_general(fy[n * 128 : (n + 1) * 128, :], both, NT, preferred_element_type=F32)
        scores = scores[:, : 2 * CAND] + scores[:, 2 * CAND :]
        squares = squares + jnp.sum((scores * scores).reshape(16, 8, 2 * CAND), axis=0)
    energy = jnp.sum(squares, axis=0, keepdims=True) * (1.0 / (SIDE * SIDE))
    lane_id = lax.broadcasted_iota(jnp.int32, (1, 2 * CAND), 1)
    first = lane_id < CAND
    sum0 = jnp.sum(jnp.where(first, energy, 0.0), axis=1, keepdims=True)
    sum1 = jnp.sum(jnp.where(first, 0.0, energy), axis=1, keepdims=True)
    post = CAND * energy / (jnp.where(first, sum0, sum1) + 1e-6)
    turned = jnp.concatenate([post[:, CAND:], post[:, :CAND]], axis=1)
    post_out[0:1, :] = post[:, :CAND]
    post_out[1:2, :] = turned[:, :CAND]
    weights = (jnp.where(first, post, turned), jnp.where(first, turned, post))

    for u in range(SLOTS):
        fetch(u, u).wait()
    hear(1)
    tell(2)

    def histogram(i, b, w_hi, w_lo):
        ip = i * PB + b
        hit = left[ip]
        hits = jnp.concatenate([hit * w_hi, hit * w_lo], axis=0)
        both = lax.dot_general(hits, right[ip], NT, preferred_element_type=F32)
        both = both[:64] + both[64:]
        at = pl.ds(pl.multiple_of(ip * KINDS, KINDS), KINDS)
        for h in range(8):
            hist[at, pl.ds(h * 128, 128)] = both[h * 8 : (h + 1) * 8]

    for i in range(2):
        pair = split(jnp.concatenate([weights[i], weights[i]], axis=1))

        @pl.loop(0, PB, unroll=8)
        def _(b):
            histogram(i, b, *pair)

    d_hi, d_lo = split(jnp.concatenate([rows[c] for c in range(3)], axis=1))
    d_both = jnp.concatenate([d_hi, d_lo], axis=1)

    def map_sums(of_core, to):
        start = pl.multiple_of((of_core * 4 + to) * 128, 128)
        h_hi, h_lo = split(hist[:, pl.ds(start, 128)].T)
        got = jnp.dot(h_hi, d_both, preferred_element_type=F32)
        got = got[:, :384] + got[:, 384:] + jnp.dot(h_lo, d_hi, preferred_element_type=F32)
        return got.reshape(4, 32, 384)

    order = (2, 1, 3, 0)
    to_near = []
    for n, d in enumerate(order):
        to = lax.rem(x + d, 4)
        sums[to] = map_sums(1 - core, to)
        to_near.append(send(sums.at[to], near.at[to], near_s.at[n], near_r.at[n], sibling))
    then, with_it = [], []
    for n, dx in enumerate(order):
        to = lax.rem(x + dx, 4)
        total = map_sums(core, to)
        to_near[n].wait_recv()
        total = total + near[to]
        if dx == 0:
            mine[...] = total
        coded[to], bases[to] = encode(total)
        for dy in (2, 1, 3, 0):
            if dx or dy:
                to_x, to_y, peer = plane_peer(dx, dy)
                at = their_bases.at[dx, dy]
                with_it.append(send(bases.at[to_x], at, base_s.at[dx, dy], base_r.at[dx, dy], peer))
                at = coming.at[dx, dy]
                then.append(send(coded.at[to_x, to_y], at, plane_s.at[dx, dy], plane_r.at[dx, dy], peer))
    total = mine[y]
    at = 0
    for dx in order:
        for dy in (2, 1, 3, 0):
            if dx or dy:
                with_it[at].wait_recv()
                then[at].wait_recv()
                total = total + decode(coming[dx, dy], their_bases[dx, dy])
                at += 1
    for n in range(8):
        s3[n] = total[n * 4 : (n + 1) * 4]
    hear(2)
    third = []
    for d in (4, 3, 5, 2, 6, 1, 7):
        to, peer = z_peer(d)
        third.append(send(s3.at[to], r3.at[d], zs.at[d], zr.at[d], peer))
    for copy in third:
        copy.wait_recv()
    total = s3[z]
    for d in range(1, 8):
        total = total + r3[d]
    data[...] = total[:, :256]
    weight[...] = total[:, 256:]
    for copy in sends + to_near + then + with_it + third:
        copy.wait_send()


def finish_kernel(data, weight, post, data_out, weight_out, post_out, sem):
    copies = [
        pltpu.make_async_copy(data, data_out, sem.at[0]),
        pltpu.make_async_copy(weight, weight_out, sem.at[1]),
        pltpu.make_async_copy(post, post_out, sem.at[2]),
    ]
    for copy in copies:
        copy.start()
    for copy in copies:
        copy.wait()


def local(ref_map, images, ctf_table, ctf_class, block_index, interp_kind, interp_bank):
    blk = jnp.transpose(block_index, (0, 2, 3, 1)).reshape(32, TAPS, CAND)
    kind = jnp.transpose(interp_kind, (0, 2, 3, 1)).reshape(32, TAPS, CAND)
    dma = pltpu.SemaphoreType.DMA
    i32 = jnp.int32
    shapes = [
        jax.ShapeDtypeStruct((4, 256), F32),
        jax.ShapeDtypeStruct((4, 128), F32),
        jax.ShapeDtypeStruct((2, CAND), F32),
    ]
    results = pl.pallas_call(
        refine_kernel,
        out_shape=shapes,
        in_specs=[pl.BlockSpec(memory_space=pltpu.HBM)] * 9,
        out_specs=[pl.BlockSpec(memory_space=VMEM)] * 3,
        scratch_shapes=[
            VMEM((2, 2, 2048), BF16),
            VMEM((64, 2048), BF16),
            pltpu.SMEM((2,), i32),
            VMEM((32, TAPS, CAND), i32),
            VMEM((32, TAPS, CAND), i32),
            VMEM((KINDS, BW, BW), BF16),
            VMEM((1024, 128), BF16),
            VMEM((1024, 512), BF16),
            dma((10,)),
            VMEM((8, BW, 2 * BW), BF16),
            VMEM((2 * BW, BW), F32),
            VMEM((2 * KINDS * NBLK, BW), F32),
            VMEM((96, BW), F32),
            VMEM((3, 256, BW), F32),
            VMEM((32, 2, 128), i32),
            [pltpu.SMEM((2, 2, 128), i32)] * SLOTS,
            dma((SLOTS,)),
            VMEM((32, 64, 256), BF16),
            VMEM((32, 128, 256), BF16),
            VMEM((SLOTS * 4 * CAND, BW), F32),
            VMEM((8 * CAND, 1024), BF16),
            VMEM((256, NBLK), F32),
            dma((8,)), dma((8,)), dma((8,)), dma((8,)),
            VMEM((4, 4, 32, 384), F32),
            VMEM((4, 4, 32, 384), F32),
            VMEM((4, 32, 384), F32),
            VMEM((4, 4, 32, 384), jnp.int16),
            VMEM((4, 4, 32, 384), jnp.int16),
            VMEM((4, 1, 384), F32),
            VMEM((4, 4, 1, 384), F32),
            VMEM((8, 4, 384), F32),
            VMEM((8, 4, 384), F32),
            dma((4,)), dma((4,)), dma((4, 4)), dma((4, 4)), dma((4, 4)), dma((4, 4)),
            dma((8,)), dma((8,)),
            pltpu.SemaphoreType.REGULAR((3, 2)),
        ],
        compiler_params=pltpu.CompilerParams(
            collective_id=0, has_side_effects=True, vmem_limit_bytes=56 * 1024 * 1024
        ),
        name="refine",
    )(
        ref_map, images, ctf_table, ctf_class, blk, kind, interp_bank,
        jnp.asarray(line_table(), BF16), jnp.asarray(across_table(), BF16),
    )
    return pl.pallas_call(
        finish_kernel,
        out_shape=shapes,
        in_specs=[pl.BlockSpec(memory_space=pltpu.HBM)] * 3,
        out_specs=[pl.BlockSpec(memory_space=pltpu.HBM)] * 3,
        scratch_shapes=[dma((3,))],
        compiler_params=pltpu.CompilerParams(vmem_limit_bytes=56 * 1024 * 1024),
        name="finish",
    )(*results)


def solution(mesh):
    in_specs = (
        P("slab", None),
        P(("particle", "slab"), None, None),
        P(),
        P(("particle", "slab")),
        P(("particle", "slab"), None, None, None),
        P(("particle", "slab"), None, None, None),
        P(),
    )
    out_specs = (
        P(("particle", "slab"), None),
        P(("particle", "slab"), None),
        P(("particle", "slab"), None),
    )
    return jax.shard_map(local, mesh=mesh, in_specs=in_specs, out_specs=out_specs, check_vma=False)
```

```python
import math

import jax
import jax.numpy as jnp
import numpy as np
from jax import lax
from jax.experimental import pallas as pl
from jax.experimental.pallas import tpu as pltpu
from jax.sharding import PartitionSpec as P

LINE = 256
PLINES = 8
SIDE = 32
BW = 128
TAPS = 4
KINDS = 8
CAND = 64
PB = 16
NBLK = 1024
MESH = pl.DeviceIdType.MESH
SLOTS = 4
OCTAVES = 44
STEPS = 744
LN2 = math.log(2.0)
ORDER = (1, 2, 3, 4, 5, 6, 7)
VMEM = pltpu.VMEM
F32 = jnp.float32
BF16 = jnp.bfloat16
NT = (((1,), (1,)), ((), ()))


def line_table():
    fx = np.arange(LINE) - LINE // 2
    sx = np.arange(SIDE) - SIDE // 2
    ang = 2.0 * np.pi / LINE * ((fx[:, None] * sx[None, :]) % LINE)
    cos, sin = np.cos(ang), np.sin(ang)
    one = np.zeros((2, 2, BW, 2, SIDE))
    one[:, 0, :, 0] = cos.reshape(2, BW, SIDE)
    one[:, 1, :, 0] = -sin.reshape(2, BW, SIDE)
    one[:, 0, :, 1] = sin.reshape(2, BW, SIDE)
    one[:, 1, :, 1] = cos.reshape(2, BW, SIDE)
    both = np.zeros((2, 2, 2, BW, 2, 2, SIDE))
    both[0, :, :, :, 0] = one
    both[1, :, :, :, 1] = one
    return both.reshape(8 * BW, 4 * SIDE)


def across_table():
    fy = np.arange(PLINES) - PLINES // 2
    sy = np.arange(SIDE) - SIDE // 2
    ang = 2.0 * np.pi / LINE * ((fy[None, :] * sy[:, None]) % LINE)
    full = np.zeros((SIDE, SIDE, PLINES, 2, SIDE))
    for s in range(SIDE):
        full[:, s, :, 0, s] = np.cos(ang)
        full[:, s, :, 1, s] = -np.sin(ang)
    return full.reshape(SIDE * SIDE, PLINES * 2 * SIDE)


def split(v):
    hi = v.astype(BF16)
    return hi, (v - hi.astype(F32)).astype(BF16)


def encode(v):
    size = jnp.abs(v)
    top = jnp.max(jnp.max(size, axis=0), axis=0, keepdims=True)
    base = jnp.log(jnp.maximum(top, 1e-37)) - OCTAVES * LN2
    size = (jnp.log(jnp.maximum(size, 1e-37)) - base) * (STEPS / LN2)
    size = jnp.maximum(size, 0.0) + 0.5
    return jnp.where(v < 0, -size, size).astype(jnp.int32).astype(jnp.int16), base


def decode(code, base):
    step = code.astype(jnp.int32).astype(F32)
    size = jnp.exp(jnp.abs(step) * (LN2 / STEPS) + base)
    return jnp.where(step > 0, size, jnp.where(step < 0, -size, 0.0))


def refine_kernel(
    piece, img_h, ctf_h, cls_h, blk_h, kind_h, bank_h, fx_h, fy_h,
    data, weight, post_out,
    img, ctf, cls, blk, kind, bank, fx, fy, own_sem,
    full, inter, table, parts, rows, rid_v, rids, rid_s, left, right,
    proj, cross, hist, gather_s, gather_r, forward_s, forward_r,
    sums, near, mine, coded, coming, bases, their_bases, s3, r3,
    near_s, near_r, plane_s, plane_r, base_s, base_r, zs, zr, here,
):
    p = lax.axis_index("particle")
    s = lax.axis_index("slab")
    z, x_lo, core = p // 4, lax.rem(p // 2, 2), lax.rem(p, 2)
    x_hi, y = s // 4, lax.rem(s, 4)
    x = x_hi * 2 + x_lo

    sibling = (p + 1 - 2 * core, s)

    def x_peer(d):
        to = lax.rem(x + d, 4)
        return to, (p + (lax.rem(to, 2) - x_lo) * 2, s + (to // 2 - x_hi) * 4)

    def plane_peer(dx, dy):
        to_x, to_y = lax.rem(x + dx, 4), lax.rem(y + dy, 4)
        return to_x, to_y, (p + (lax.rem(to_x, 2) - x_lo) * 2, to_x // 2 * 4 + to_y)

    def z_peer(d):
        to = lax.rem(z + d, 8)
        return to, (p + (to - z) * 4, s)

    def map_peer(n, sign):
        flip = lax.rem(n, 2)
        to = lax.rem(y + 4 + sign * (n // 2), 4)
        return (p + flip * (2 - 4 * x_lo), (x_hi + flip * (1 - 2 * x_hi)) * 4 + to)

    def send(src, dst, ssem, rsem, peer):
        copy = pltpu.make_async_remote_copy(
            src_ref=src, dst_ref=dst, send_sem=ssem, recv_sem=rsem, device_id=peer, device_id_type=MESH
        )
        copy.start()
        return copy

    peers = [map_peer(n, 1) for n in (5, 3, 7, 4)] + [x_peer(d)[1] for d in (2, 1, 3)]
    peers += [map_peer(n, 1) for n in (1, 2, 6)] + [z_peer(d)[1] for d in (1, 7)] + [sibling]
    barrier = pltpu.get_barrier_semaphore()
    for peer in peers:
        pl.semaphore_signal(barrier, inc=1, device_id=peer, device_id_type=MESH)
    pairs = [
        (blk_h, blk), (kind_h, kind), (img_h, img), (ctf_h, ctf), (cls_h, cls), (bank_h, bank),
        (piece, full.at[s]), (fx_h, fx), (fy_h, fy),
    ]
    loads = [pltpu.make_async_copy(a, b, own_sem.at[n]) for n, (a, b) in enumerate(pairs)]
    for load in loads:
        load.start()
    pl.semaphore_wait(barrier, len(peers))
    half = pl.ds(pl.multiple_of(core * 64, 64), 64)
    sends = []
    for n in ORDER:
        sends.append(send(piece.at[half], full.at[s, half], gather_s.at[n], gather_r.at[n], map_peer(n, 1)))

    def tell(n):
        for side, d in enumerate((1, 7)):
            pl.semaphore_signal(here.at[n, side], inc=1, device_id=z_peer(d)[1], device_id_type=MESH)

    def hear(n):
        for side in range(2):
            pl.semaphore_wait(here.at[n, side], 1)

    tell(0)

    loads[0].wait()
    loads[1].wait()
    number = kind[...] * NBLK + blk[...]
    for h in range(2):
        pair = jnp.concatenate([number[:, 2 * h, :], number[:, 2 * h + 1, :]], axis=1)
        rid_v[:, h, :] = pair * 2

    def fetch(u, two):
        return pltpu.make_async_copy(rid_v.at[pl.ds(two * 2, 2)], rids[u], rid_s.at[u])

    for u in range(SLOTS):
        fetch(u, u).start()

    for load in loads[2:6]:
        load.wait()
    lanes = lax.broadcasted_iota(jnp.int32, (16, 64), 1)
    which = lax.broadcasted_iota(jnp.int32, (16, 64), 0)
    pick = jnp.where(which == 0, cls[0], cls[1])
    onehot = (lanes == pick).astype(F32).astype(BF16)
    gain = jnp.dot(onehot, ctf[...], preferred_element_type=F32)
    pixel = img[...].astype(F32)
    for i in range(2):
        g = gain[i : i + 1]
        for c, row in enumerate((g * pixel[i, 0:1], g * pixel[i, 1:2], g * g)):
            for b in range(PB):
                parts[pl.ds(c * 32 + i * PB + b, 1), :] = row[:, b * BW : (b + 1) * BW]
    both = jnp.concatenate(split(parts[...]), axis=0)
    for k in range(KINDS):
        turned = lax.dot_general(both, bank[k], NT, preferred_element_type=F32)
        turned = turned[:96] + turned[96:]
        for c in range(3):
            rows[c, pl.ds(k, 32, stride=KINDS), :] = turned[c * 32 : (c + 1) * 32]

    row_id = lax.broadcasted_iota(jnp.int32, (64, 128), 0)
    col_id = lax.broadcasted_iota(jnp.int32, (128, 128), 0)

    @pl.loop(0, 32)
    def _(ip):
        for h in range(2):
            v = rid_v[ip, pl.ds(h, 1), :] >> 1
            high = ((v >> 5) & 1) * 4 + ((v >> 4) & 1) * 2 + ((v >> 6) & 1)
            low = ((v >> 2) & 3) * 32 + ((v >> 7) & 7) * 4 + (v & 3)
            at = pl.ds(h * 128, 128)
            left[ip, :, at] = jnp.where(row_id == high * KINDS + (v >> 10), 1.0, 0.0).astype(BF16)
            right[ip, :, at] = jnp.where(col_id == low, 1.0, 0.0).astype(BF16)

    def map_piece(source):
        inter[pl.ds(0, BW, stride=2), :] = full[source, :, :BW].astype(F32)
        inter[pl.ds(1, BW, stride=2), :] = full[source, :, BW:].astype(F32)
        lhs = inter[...].astype(BF16)
        for k in range(0, KINDS, 2):
            mapped = jnp.dot(lhs, jnp.concatenate([bank[k], bank[k + 1]], axis=1), preferred_element_type=F32)
            for h in range(2):
                at = pl.ds(pl.multiple_of((k + h) * 2 * NBLK + source * 256, 256), 256)
                table[at, :] = mapped[:, h * BW : (h + 1) * BW].astype(BF16).astype(F32)

    loads[6].wait()
    map_piece(s)

    def forward(n, rows):
        at = full.at[map_peer(n, -1)[1], rows]
        return pltpu.make_async_remote_copy(
            src_ref=at, dst_ref=at, send_sem=forward_s.at[n], recv_sem=forward_r.at[n],
            device_id=sibling, device_id_type=MESH,
        )

    other_half = pl.ds(pl.multiple_of((1 - core) * 64, 64), 64)
    def pass_on(n):
        peer = map_peer(n, -1)
        pltpu.make_async_remote_copy(
            src_ref=piece.at[half], dst_ref=full.at[peer[1], half], send_sem=gather_s.at[n],
            recv_sem=gather_r.at[n], device_id=peer, device_id_type=MESH,
        ).wait_recv()
        forward(n, half).start()

    def use(n):
        forward(n, other_half).wait_recv()
        map_piece(map_peer(n, -1)[1])

    pass_on(1)

    @pl.loop(1, 7)
    def _(n):
        pass_on(n + 1)
        use(n)

    use(7)
    hear(0)
    tell(1)
    loads[7].wait()
    loads[8].wait()

    @pl.loop(0, 16 // SLOTS)
    def _(step):
        for u in range(SLOTS):
            two = step * SLOTS + u
            i = two // 8
            fetch(u, two).wait()
            for v in range(2):
                start = (u * 2 + v) * 2 * CAND
                for j in range(CAND):
                    taken = [table[pl.ds(rids[u][v, h, q * CAND + j], 2), :] for h in range(2) for q in range(2)]
                    proj[pl.ds(start + 2 * j, 2), :] = (taken[0] + taken[1]) + (taken[2] + taken[3])
                ca = parts[pl.ds(two * 2 + v, 1), :]
                cb = parts[pl.ds(32 + two * 2 + v, 1), :]
                re = proj[pl.ds(start, CAND, stride=2), :]
                im = proj[pl.ds(start + 1, CAND, stride=2), :]
                group = lax.rem(two, 8) // 2
                at = pl.ds(pl.multiple_of(group * 2 * CAND + i * CAND, CAND), CAND)
                lane = ((u % 2) * 2 + v) * 256
                cross[at, pl.ds(lane, 128)] = (ca * re + cb * im).astype(BF16)
                cross[at, pl.ds(lane + 128, 128)] = (cb * re - ca * im).astype(BF16)
            fetch(u, lax.rem(two + SLOTS, 16)).start()

    along = jnp.dot(cross[...], fx[...], preferred_element_type=F32)
    along = jnp.concatenate([along[g * 2 * CAND : (g + 1) * 2 * CAND] for g in range(4)], axis=1)
    both = jnp.concatenate(split(along), axis=0)
    squares = jnp.zeros((8, 2 * CAND), F32)
    for n in range(8):
        scores = lax.dot_general(fy[n * 128 : (n + 1) * 128, :], both, NT, preferred_element_type=F32)
        scores = scores[:, : 2 * CAND] + scores[:, 2 * CAND :]
        squares = squares + jnp.sum((scores * scores).reshape(16, 8, 2 * CAND), axis=0)
    energy = jnp.sum(squares, axis=0, keepdims=True) * (1.0 / (SIDE * SIDE))
    lane_id = lax.broadcasted_iota(jnp.int32, (1, 2 * CAND), 1)
    first = lane_id < CAND
    sum0 = jnp.sum(jnp.where(first, energy, 0.0), axis=1, keepdims=True)
    sum1 = jnp.sum(jnp.where(first, 0.0, energy), axis=1, keepdims=True)
    post = CAND * energy / (jnp.where(first, sum0, sum1) + 1e-6)
    turned = jnp.concatenate([post[:, CAND:], post[:, :CAND]], axis=1)
    post_out[0:1, :] = post[:, :CAND]
    post_out[1:2, :] = turned[:, :CAND]
    weights = (jnp.where(first, post, turned), jnp.where(first, turned, post))

    for u in range(SLOTS):
        fetch(u, u).wait()
    hear(1)
    tell(2)

    def histogram(i, b, w_hi, w_lo):
        ip = i * PB + b
        hit = left[ip]
        hits = jnp.concatenate([hit * w_hi, hit * w_lo], axis=0)
        both = lax.dot_general(hits, right[ip], NT, preferred_element_type=F32)
        both = both[:64] + both[64:]
        at = pl.ds(pl.multiple_of(ip * KINDS, KINDS), KINDS)
        for h in range(8):
            hist[at, pl.ds(h * 128, 128)] = both[h * 8 : (h + 1) * 8]

    for i in range(2):
        pair = split(jnp.concatenate([weights[i], weights[i]], axis=1))

        @pl.loop(0, PB, unroll=8)
        def _(b):
            histogram(i, b, *pair)

    d_hi, d_lo = split(jnp.concatenate([rows[c] for c in range(3)], axis=1))
    d_both = jnp.concatenate([d_hi, d_lo], axis=1)

    def map_sums(of_core, to):
        start = pl.multiple_of((of_core * 4 + to) * 128, 128)
        h_hi, h_lo = split(hist[:, pl.ds(start, 128)].T)
        got = jnp.dot(h_hi, d_both, preferred_element_type=F32)
        got = got[:, :384] + got[:, 384:] + jnp.dot(h_lo, d_hi, preferred_element_type=F32)
        return got.reshape(4, 32, 384)

    order = (2, 1, 3, 0)
    to_near = []
    for n, d in enumerate(order):
        to = lax.rem(x + d, 4)
        sums[to] = map_sums(1 - core, to)
        to_near.append(send(sums.at[to], near.at[to], near_s.at[n], near_r.at[n], sibling))
    then, with_it = [], []
    for n, dx in enumerate(order):
        to = lax.rem(x + dx, 4)
        total = map_sums(core, to)
        to_near[n].wait_recv()
        total = total + near[to]
        if dx == 0:
            mine[...] = total
        coded[to], bases[to] = encode(total)
        for dy in (2, 1, 3, 0):
            if dx or dy:
                to_x, to_y, peer = plane_peer(dx, dy)
                at = their_bases.at[dx, dy]
                with_it.append(send(bases.at[to_x], at, base_s.at[dx, dy], base_r.at[dx, dy], peer))
                at = coming.at[dx, dy]
                then.append(send(coded.at[to_x, to_y], at, plane_s.at[dx, dy], plane_r.at[dx, dy], peer))
    total = mine[y]
    at = 0
    for dx in order:
        for dy in (2, 1, 3, 0):
            if dx or dy:
                with_it[at].wait_recv()
                then[at].wait_recv()
                total = total + decode(coming[dx, dy], their_bases[dx, dy])
                at += 1
    for n in range(8):
        s3[n] = total[n * 4 : (n + 1) * 4]
    hear(2)
    third = []
    for d in (4, 3, 5, 2, 6, 1, 7):
        to, peer = z_peer(d)
        third.append(send(s3.at[to], r3.at[d], zs.at[d], zr.at[d], peer))
    for copy in third:
        copy.wait_recv()
    total = s3[z]
    for d in range(1, 8):
        total = total + r3[d]
    data[...] = total[:, :256]
    weight[...] = total[:, 256:]
    for n in range(1, 8):
        forward(n, half).wait_send()
    for copy in sends + to_near + then + with_it + third:
        copy.wait_send()


def finish_kernel(data, weight, post, data_out, weight_out, post_out, sem):
    copies = [
        pltpu.make_async_copy(data, data_out, sem.at[0]),
        pltpu.make_async_copy(weight, weight_out, sem.at[1]),
        pltpu.make_async_copy(post, post_out, sem.at[2]),
    ]
    for copy in copies:
        copy.start()
    for copy in copies:
        copy.wait()


def local(ref_map, images, ctf_table, ctf_class, block_index, interp_kind, interp_bank):
    blk = jnp.transpose(block_index, (0, 2, 3, 1)).reshape(32, TAPS, CAND)
    kind = jnp.transpose(interp_kind, (0, 2, 3, 1)).reshape(32, TAPS, CAND)
    dma = pltpu.SemaphoreType.DMA
    i32 = jnp.int32
    shapes = [
        jax.ShapeDtypeStruct((4, 256), F32),
        jax.ShapeDtypeStruct((4, 128), F32),
        jax.ShapeDtypeStruct((2, CAND), F32),
    ]
    results = pl.pallas_call(
        refine_kernel,
        out_shape=shapes,
        in_specs=[pl.BlockSpec(memory_space=pltpu.HBM)] * 9,
        out_specs=[pl.BlockSpec(memory_space=VMEM)] * 3,
        scratch_shapes=[
            VMEM((2, 2, 2048), BF16),
            VMEM((64, 2048), BF16),
            pltpu.SMEM((2,), i32),
            VMEM((32, TAPS, CAND), i32),
            VMEM((32, TAPS, CAND), i32),
            VMEM((KINDS, BW, BW), BF16),
            VMEM((1024, 128), BF16),
            VMEM((1024, 512), BF16),
            dma((10,)),
            VMEM((8, BW, 2 * BW), BF16),
            VMEM((2 * BW, BW), F32),
            VMEM((2 * KINDS * NBLK, BW), F32),
            VMEM((96, BW), F32),
            VMEM((3, 256, BW), F32),
            VMEM((32, 2, 128), i32),
            [pltpu.SMEM((2, 2, 128), i32)] * SLOTS,
            dma((SLOTS,)),
            VMEM((32, 64, 256), BF16),
            VMEM((32, 128, 256), BF16),
            VMEM((SLOTS * 4 * CAND, BW), F32),
            VMEM((8 * CAND, 1024), BF16),
            VMEM((256, NBLK), F32),
            dma((8,)), dma((8,)), dma((8,)), dma((8,)),
            VMEM((4, 4, 32, 384), F32),
            VMEM((4, 4, 32, 384), F32),
            VMEM((4, 32, 384), F32),
            VMEM((4, 4, 32, 384), jnp.int16),
            VMEM((4, 4, 32, 384), jnp.int16),
            VMEM((4, 1, 384), F32),
            VMEM((4, 4, 1, 384), F32),
            VMEM((8, 4, 384), F32),
            VMEM((8, 4, 384), F32),
            dma((4,)), dma((4,)), dma((4, 4)), dma((4, 4)), dma((4, 4)), dma((4, 4)),
            dma((8,)), dma((8,)),
            pltpu.SemaphoreType.REGULAR((3, 2)),
        ],
        compiler_params=pltpu.CompilerParams(
            collective_id=0, has_side_effects=True, vmem_limit_bytes=56 * 1024 * 1024
        ),
        name="refine",
    )(
        ref_map, images, ctf_table, ctf_class, blk, kind, interp_bank,
        jnp.asarray(line_table(), BF16), jnp.asarray(across_table(), BF16),
    )
    return pl.pallas_call(
        finish_kernel,
        out_shape=shapes,
        in_specs=[pl.BlockSpec(memory_space=pltpu.HBM)] * 3,
        out_specs=[pl.BlockSpec(memory_space=pltpu.HBM)] * 3,
        scratch_shapes=[dma((3,))],
        compiler_params=pltpu.CompilerParams(vmem_limit_bytes=56 * 1024 * 1024),
        name="finish",
    )(*results)


def solution(mesh):
    in_specs = (
        P("slab", None),
        P(("particle", "slab"), None, None),
        P(),
        P(("particle", "slab")),
        P(("particle", "slab"), None, None, None),
        P(("particle", "slab"), None, None, None),
        P(),
    )
    out_specs = (
        P(("particle", "slab"), None),
        P(("particle", "slab"), None),
        P(("particle", "slab"), None),
    )
    return jax.shard_map(local, mesh=mesh, in_specs=in_specs, out_specs=out_specs, check_vma=False)
```

```python
import math

import jax
import jax.numpy as jnp
import numpy as np
from jax import lax
from jax.experimental import pallas as pl
from jax.experimental.pallas import tpu as pltpu
from jax.sharding import PartitionSpec as P

LINE = 256
PLINES = 8
SIDE = 32
BW = 128
TAPS = 4
KINDS = 8
CAND = 64
PB = 16
NBLK = 1024
MESH = pl.DeviceIdType.MESH
SLOTS = 4
OCTAVES = 44
STEPS = 744
LN2 = math.log(2.0)
ORDER = (1, 2, 3, 4, 5, 6, 7)
VMEM = pltpu.VMEM
F32 = jnp.float32
BF16 = jnp.bfloat16
NT = (((1,), (1,)), ((), ()))


def line_table():
    fx = np.arange(LINE) - LINE // 2
    sx = np.arange(SIDE) - SIDE // 2
    ang = 2.0 * np.pi / LINE * ((fx[:, None] * sx[None, :]) % LINE)
    cos, sin = np.cos(ang), np.sin(ang)
    one = np.zeros((2, 2, BW, 2, SIDE))
    one[:, 0, :, 0] = cos.reshape(2, BW, SIDE)
    one[:, 1, :, 0] = -sin.reshape(2, BW, SIDE)
    one[:, 0, :, 1] = sin.reshape(2, BW, SIDE)
    one[:, 1, :, 1] = cos.reshape(2, BW, SIDE)
    both = np.zeros((2, 2, 2, BW, 2, 2, SIDE))
    both[0, :, :, :, 0] = one
    both[1, :, :, :, 1] = one
    return both.reshape(8 * BW, 4 * SIDE)


def across_table():
    fy = np.arange(PLINES) - PLINES // 2
    sy = np.arange(SIDE) - SIDE // 2
    ang = 2.0 * np.pi / LINE * ((fy[None, :] * sy[:, None]) % LINE)
    full = np.zeros((SIDE, SIDE, PLINES, 2, SIDE))
    for s in range(SIDE):
        full[:, s, :, 0, s] = np.cos(ang)
        full[:, s, :, 1, s] = -np.sin(ang)
    return full.reshape(SIDE * SIDE, PLINES * 2 * SIDE)


def split(v):
    hi = v.astype(BF16)
    return hi, (v - hi.astype(F32)).astype(BF16)


def encode(v):
    size = jnp.abs(v)
    top = jnp.max(jnp.max(size, axis=0), axis=0, keepdims=True)
    base = jnp.log(jnp.maximum(top, 1e-37)) - OCTAVES * LN2
    size = (jnp.log(jnp.maximum(size, 1e-37)) - base) * (STEPS / LN2)
    size = jnp.maximum(size, 0.0) + 0.5
    return jnp.where(v < 0, -size, size).astype(jnp.int32).astype(jnp.int16), base


def decode(code, base):
    step = code.astype(jnp.int32).astype(F32)
    size = jnp.exp(jnp.abs(step) * (LN2 / STEPS) + base)
    return jnp.where(step > 0, size, jnp.where(step < 0, -size, 0.0))


def refine_kernel(
    piece, img_h, ctf_h, cls_h, blk_h, kind_h, bank_h, fx_h, fy_h,
    data, weight, post_out,
    img, ctf, cls, blk, kind, bank, fx, fy, own_sem,
    full, inter, table, parts, rows, rid_v, rids, rid_s, left, right,
    proj, cross, hist, gather_s, gather_r, forward_s, forward_r,
    sums, near, mine, coded, coming, bases, their_bases, s3, r3,
    near_s, near_r, plane_s, plane_r, base_s, base_r, zs, zr, here,
):
    p = lax.axis_index("particle")
    s = lax.axis_index("slab")
    z, x_lo, core = p // 4, lax.rem(p // 2, 2), lax.rem(p, 2)
    x_hi, y = s // 4, lax.rem(s, 4)
    x = x_hi * 2 + x_lo

    sibling = (p + 1 - 2 * core, s)

    def x_peer(d):
        to = lax.rem(x + d, 4)
        return to, (p + (lax.rem(to, 2) - x_lo) * 2, s + (to // 2 - x_hi) * 4)

    def plane_peer(dx, dy):
        to_x, to_y = lax.rem(x + dx, 4), lax.rem(y + dy, 4)
        return to_x, to_y, (p + (lax.rem(to_x, 2) - x_lo) * 2, to_x // 2 * 4 + to_y)

    def z_peer(d):
        to = lax.rem(z + d, 8)
        return to, (p + (to - z) * 4, s)

    def map_peer(n, sign):
        flip = lax.rem(n, 2)
        to = lax.rem(y + 4 + sign * (n // 2), 4)
        return (p + flip * (2 - 4 * x_lo), (x_hi + flip * (1 - 2 * x_hi)) * 4 + to)

    def send(src, dst, ssem, rsem, peer):
        copy = pltpu.make_async_remote_copy(
            src_ref=src, dst_ref=dst, send_sem=ssem, recv_sem=rsem, device_id=peer, device_id_type=MESH
        )
        copy.start()
        return copy

    peers = [map_peer(n, 1) for n in (5, 3, 7, 4)] + [x_peer(d)[1] for d in (2, 1, 3)]
    peers += [map_peer(n, 1) for n in (1, 2, 6)] + [z_peer(d)[1] for d in (1, 7)] + [sibling]
    barrier = pltpu.get_barrier_semaphore()
    for peer in peers:
        pl.semaphore_signal(barrier, inc=1, device_id=peer, device_id_type=MESH)
    pairs = [
        (blk_h, blk), (kind_h, kind), (img_h, img), (ctf_h, ctf), (cls_h, cls), (bank_h, bank),
        (piece, full.at[s]), (fx_h, fx), (fy_h, fy),
    ]
    loads = [pltpu.make_async_copy(a, b, own_sem.at[n]) for n, (a, b) in enumerate(pairs)]
    for load in loads:
        load.start()
    pl.semaphore_wait(barrier, len(peers))
    half = pl.ds(pl.multiple_of(core * 64, 64), 64)
    sends = []
    for n in ORDER:
        sends.append(send(piece.at[half], full.at[s, half], gather_s.at[n], gather_r.at[n], map_peer(n, 1)))

    def tell(n):
        for side, d in enumerate((1, 7)):
            pl.semaphore_signal(here.at[n, side], inc=1, device_id=z_peer(d)[1], device_id_type=MESH)

    def hear(n):
        for side in range(2):
            pl.semaphore_wait(here.at[n, side], 1)

    tell(0)

    loads[0].wait()
    loads[1].wait()
    number = kind[...] * NBLK + blk[...]
    for h in range(2):
        pair = jnp.concatenate([number[:, 2 * h, :], number[:, 2 * h + 1, :]], axis=1)
        rid_v[:, h, :] = pair * 2

    def fetch(u, two):
        return pltpu.make_async_copy(rid_v.at[pl.ds(two * 2, 2)], rids[u], rid_s.at[u])

    for u in range(SLOTS):
        fetch(u, u).start()

    for load in loads[2:6]:
        load.wait()
    lanes = lax.broadcasted_iota(jnp.int32, (16, 64), 1)
    which = lax.broadcasted_iota(jnp.int32, (16, 64), 0)
    pick = jnp.where(which == 0, cls[0], cls[1])
    onehot = (lanes == pick).astype(F32).astype(BF16)
    gain = jnp.dot(onehot, ctf[...], preferred_element_type=F32)
    pixel = img[...].astype(F32)
    for i in range(2):
        g = gain[i : i + 1]
        for c, row in enumerate((g * pixel[i, 0:1], g * pixel[i, 1:2], g * g)):
            for b in range(PB):
                parts[pl.ds(c * 32 + i * PB + b, 1), :] = row[:, b * BW : (b + 1) * BW]
    both = jnp.concatenate(split(parts[...]), axis=0)
    for k in range(KINDS):
        turned = lax.dot_general(both, bank[k], NT, preferred_element_type=F32)
        turned = turned[:96] + turned[96:]
        for c in range(3):
            rows[c, pl.ds(k, 32, stride=KINDS), :] = turned[c * 32 : (c + 1) * 32]

    row_id = lax.broadcasted_iota(jnp.int32, (64, 128), 0)
    col_id = lax.broadcasted_iota(jnp.int32, (128, 128), 0)

    @pl.loop(0, 32)
    def _(ip):
        for h in range(2):
            v = rid_v[ip, pl.ds(h, 1), :] >> 1
            high = ((v >> 5) & 1) * 4 + ((v >> 4) & 1) * 2 + ((v >> 6) & 1)
            low = ((v >> 2) & 3) * 32 + ((v >> 7) & 7) * 4 + (v & 3)
            at = pl.ds(h * 128, 128)
            left[ip, :, at] = jnp.where(row_id == high * KINDS + (v >> 10), 1.0, 0.0).astype(BF16)
            right[ip, :, at] = jnp.where(col_id == low, 1.0, 0.0).astype(BF16)

    def map_piece(source):
        inter[pl.ds(0, BW, stride=2), :] = full[source, :, :BW].astype(F32)
        inter[pl.ds(1, BW, stride=2), :] = full[source, :, BW:].astype(F32)
        lhs = inter[...].astype(BF16)
        for k in range(0, KINDS, 2):
            mapped = jnp.dot(lhs, jnp.concatenate([bank[k], bank[k + 1]], axis=1), preferred_element_type=F32)
            for h in range(2):
                at = pl.ds(pl.multiple_of((k + h) * 2 * NBLK + source * 256, 256), 256)
                table[at, :] = mapped[:, h * BW : (h + 1) * BW].astype(BF16).astype(F32)

    loads[6].wait()
    map_piece(s)

    def forward(n, rows):
        at = full.at[map_peer(n, -1)[1], rows]
        return pltpu.make_async_remote_copy(
            src_ref=at, dst_ref=at, send_sem=forward_s.at[n], recv_sem=forward_r.at[n],
            device_id=sibling, device_id_type=MESH,
        )

    other_half = pl.ds(pl.multiple_of((1 - core) * 64, 64), 64)
    def pass_on(n):
        peer = map_peer(n, -1)
        pltpu.make_async_remote_copy(
            src_ref=piece.at[half], dst_ref=full.at[peer[1], half], send_sem=gather_s.at[n],
            recv_sem=gather_r.at[n], device_id=peer, device_id_type=MESH,
        ).wait_recv()
        forward(n, half).start()

    def use(n):
        forward(n, other_half).wait_recv()
        map_piece(map_peer(n, -1)[1])

    pass_on(1)

    @pl.loop(1, 7)
    def _(n):
        pass_on(n + 1)
        use(n)

    use(7)
    for n in range(1, 8):
        forward(n, half).wait_send()

    hear(0)
    tell(1)
    loads[7].wait()
    loads[8].wait()

    @pl.loop(0, 16 // SLOTS)
    def _(step):
        for u in range(SLOTS):
            two = step * SLOTS + u
            i = two // 8
            fetch(u, two).wait()
            for v in range(2):
                start = (u * 2 + v) * 2 * CAND
                for j in range(CAND):
                    taken = [table[pl.ds(rids[u][v, h, q * CAND + j], 2), :] for h in range(2) for q in range(2)]
                    proj[pl.ds(start + 2 * j, 2), :] = (taken[0] + taken[1]) + (taken[2] + taken[3])
                ca = parts[pl.ds(two * 2 + v, 1), :]
                cb = parts[pl.ds(32 + two * 2 + v, 1), :]
                re = proj[pl.ds(start, CAND, stride=2), :]
                im = proj[pl.ds(start + 1, CAND, stride=2), :]
                group = lax.rem(two, 8) // 2
                at = pl.ds(pl.multiple_of(group * 2 * CAND + i * CAND, CAND), CAND)
                lane = ((u % 2) * 2 + v) * 256
                cross[at, pl.ds(lane, 128)] = (ca * re + cb * im).astype(BF16)
                cross[at, pl.ds(lane + 128, 128)] = (cb * re - ca * im).astype(BF16)
            fetch(u, lax.rem(two + SLOTS, 16)).start()

    along = jnp.dot(cross[...], fx[...], preferred_element_type=F32)
    along = jnp.concatenate([along[g * 2 * CAND : (g + 1) * 2 * CAND] for g in range(4)], axis=1)
    both = jnp.concatenate(split(along), axis=0)
    squares = jnp.zeros((8, 2 * CAND), F32)
    for n in range(8):
        scores = lax.dot_general(fy[n * 128 : (n + 1) * 128, :], both, NT, preferred_element_type=F32)
        scores = scores[:, : 2 * CAND] + scores[:, 2 * CAND :]
        squares = squares + jnp.sum((scores * scores).reshape(16, 8, 2 * CAND), axis=0)
    energy = jnp.sum(squares, axis=0, keepdims=True) * (1.0 / (SIDE * SIDE))
    lane_id = lax.broadcasted_iota(jnp.int32, (1, 2 * CAND), 1)
    first = lane_id < CAND
    sum0 = jnp.sum(jnp.where(first, energy, 0.0), axis=1, keepdims=True)
    sum1 = jnp.sum(jnp.where(first, 0.0, energy), axis=1, keepdims=True)
    post = CAND * energy / (jnp.where(first, sum0, sum1) + 1e-6)
    turned = jnp.concatenate([post[:, CAND:], post[:, :CAND]], axis=1)
    post_out[0:1, :] = post[:, :CAND]
    post_out[1:2, :] = turned[:, :CAND]
    weights = (jnp.where(first, post, turned), jnp.where(first, turned, post))

    for u in range(SLOTS):
        fetch(u, u).wait()
    hear(1)
    tell(2)

    def histogram(i, b, w_hi, w_lo):
        ip = i * PB + b
        hit = left[ip]
        hits = jnp.concatenate([hit * w_hi, hit * w_lo], axis=0)
        both = lax.dot_general(hits, right[ip], NT, preferred_element_type=F32)
        both = both[:64] + both[64:]
        at = pl.ds(pl.multiple_of(ip * KINDS, KINDS), KINDS)
        for h in range(8):
            hist[at, pl.ds(h * 128, 128)] = both[h * 8 : (h + 1) * 8]

    for i in range(2):
        pair = split(jnp.concatenate([weights[i], weights[i]], axis=1))

        @pl.loop(0, PB, unroll=PB)
        def _(b):
            histogram(i, b, *pair)

    d_hi, d_lo = split(jnp.concatenate([rows[c] for c in range(3)], axis=1))
    d_both = jnp.concatenate([d_hi, d_lo], axis=1)

    def map_sums(of_core, to):
        start = pl.multiple_of((of_core * 4 + to) * 128, 128)
        h_hi, h_lo = split(hist[:, pl.ds(start, 128)].T)
        got = jnp.dot(h_hi, d_both, preferred_element_type=F32)
        got = got[:, :384] + got[:, 384:] + jnp.dot(h_lo, d_hi, preferred_element_type=F32)
        return got.reshape(4, 32, 384)

    order = (2, 1, 3, 0)
    to_near = []
    for n, d in enumerate(order):
        to = lax.rem(x + d, 4)
        sums[to] = map_sums(1 - core, to)
        to_near.append(send(sums.at[to], near.at[to], near_s.at[n], near_r.at[n], sibling))
    then, with_it = [], []
    for n, dx in enumerate(order):
        to = lax.rem(x + dx, 4)
        total = map_sums(core, to)
        to_near[n].wait_recv()
        total = total + near[to]
        if dx == 0:
            mine[...] = total
        coded[to], bases[to] = encode(total)
        for dy in (2, 1, 3, 0):
            if dx or dy:
                to_x, to_y, peer = plane_peer(dx, dy)
                at = their_bases.at[dx, dy]
                with_it.append(send(bases.at[to_x], at, base_s.at[dx, dy], base_r.at[dx, dy], peer))
                at = coming.at[dx, dy]
                then.append(send(coded.at[to_x, to_y], at, plane_s.at[dx, dy], plane_r.at[dx, dy], peer))
    total = mine[y]
    at = 0
    for dx in order:
        for dy in (2, 1, 3, 0):
            if dx or dy:
                with_it[at].wait_recv()
                then[at].wait_recv()
                total = total + decode(coming[dx, dy], their_bases[dx, dy])
                at += 1
    for n in range(8):
        s3[n] = total[n * 4 : (n + 1) * 4]
    hear(2)
    third = []
    for d in (4, 3, 5, 2, 6, 1, 7):
        to, peer = z_peer(d)
        third.append(send(s3.at[to], r3.at[d], zs.at[d], zr.at[d], peer))
    for copy in third:
        copy.wait_recv()
    total = s3[z]
    for d in range(1, 8):
        total = total + r3[d]
    data[...] = total[:, :256]
    weight[...] = total[:, 256:]
    for copy in sends + to_near + then + with_it + third:
        copy.wait_send()


def finish_kernel(data, weight, post, data_out, weight_out, post_out, sem):
    copies = [
        pltpu.make_async_copy(data, data_out, sem.at[0]),
        pltpu.make_async_copy(weight, weight_out, sem.at[1]),
        pltpu.make_async_copy(post, post_out, sem.at[2]),
    ]
    for copy in copies:
        copy.start()
    for copy in copies:
        copy.wait()


def local(ref_map, images, ctf_table, ctf_class, block_index, interp_kind, interp_bank):
    blk = jnp.transpose(block_index, (0, 2, 3, 1)).reshape(32, TAPS, CAND)
    kind = jnp.transpose(interp_kind, (0, 2, 3, 1)).reshape(32, TAPS, CAND)
    dma = pltpu.SemaphoreType.DMA
    i32 = jnp.int32
    shapes = [
        jax.ShapeDtypeStruct((4, 256), F32),
        jax.ShapeDtypeStruct((4, 128), F32),
        jax.ShapeDtypeStruct((2, CAND), F32),
    ]
    results = pl.pallas_call(
        refine_kernel,
        out_shape=shapes,
        in_specs=[pl.BlockSpec(memory_space=pltpu.HBM)] * 9,
        out_specs=[pl.BlockSpec(memory_space=VMEM)] * 3,
        scratch_shapes=[
            VMEM((2, 2, 2048), BF16),
            VMEM((64, 2048), BF16),
            pltpu.SMEM((2,), i32),
            VMEM((32, TAPS, CAND), i32),
            VMEM((32, TAPS, CAND), i32),
            VMEM((KINDS, BW, BW), BF16),
            VMEM((1024, 128), BF16),
            VMEM((1024, 512), BF16),
            dma((10,)),
            VMEM((8, BW, 2 * BW), BF16),
            VMEM((2 * BW, BW), F32),
            VMEM((2 * KINDS * NBLK, BW), F32),
            VMEM((96, BW), F32),
            VMEM((3, 256, BW), F32),
            VMEM((32, 2, 128), i32),
            [pltpu.SMEM((2, 2, 128), i32)] * SLOTS,
            dma((SLOTS,)),
            VMEM((32, 64, 256), BF16),
            VMEM((32, 128, 256), BF16),
            VMEM((SLOTS * 4 * CAND, BW), F32),
            VMEM((8 * CAND, 1024), BF16),
            VMEM((256, NBLK), F32),
            dma((8,)), dma((8,)), dma((8,)), dma((8,)),
            VMEM((4, 4, 32, 384), F32),
            VMEM((4, 4, 32, 384), F32),
            VMEM((4, 32, 384), F32),
            VMEM((4, 4, 32, 384), jnp.int16),
            VMEM((4, 4, 32, 384), jnp.int16),
            VMEM((4, 1, 384), F32),
            VMEM((4, 4, 1, 384), F32),
            VMEM((8, 4, 384), F32),
            VMEM((8, 4, 384), F32),
            dma((4,)), dma((4,)), dma((4, 4)), dma((4, 4)), dma((4, 4)), dma((4, 4)),
            dma((8,)), dma((8,)),
            pltpu.SemaphoreType.REGULAR((3, 2)),
        ],
        compiler_params=pltpu.CompilerParams(
            collective_id=0, has_side_effects=True, vmem_limit_bytes=56 * 1024 * 1024
        ),
        name="refine",
    )(
        ref_map, images, ctf_table, ctf_class, blk, kind, interp_bank,
        jnp.asarray(line_table(), BF16), jnp.asarray(across_table(), BF16),
    )
    return pl.pallas_call(
        finish_kernel,
        out_shape=shapes,
        in_specs=[pl.BlockSpec(memory_space=pltpu.HBM)] * 3,
        out_specs=[pl.BlockSpec(memory_space=pltpu.HBM)] * 3,
        scratch_shapes=[dma((3,))],
        compiler_params=pltpu.CompilerParams(vmem_limit_bytes=56 * 1024 * 1024),
        name="finish",
    )(*results)


def solution(mesh):
    in_specs = (
        P("slab", None),
        P(("particle", "slab"), None, None),
        P(),
        P(("particle", "slab")),
        P(("particle", "slab"), None, None, None),
        P(("particle", "slab"), None, None, None),
        P(),
    )
    out_specs = (
        P(("particle", "slab"), None),
        P(("particle", "slab"), None),
        P(("particle", "slab"), None),
    )
    return jax.shard_map(local, mesh=mesh, in_specs=in_specs, out_specs=out_specs, check_vma=False)
```
